32 devices in a mesh: dp: 4 (over y, x), seq: 4 (over z), section: 2 (over core).
Axes of the slice: x: 2, y: 2, z: 4, core: 2. Of those that a mesh axis runs over, the one named last changes fastest.
Arguments:
- tokens: bfloat16 [8, 1024, 512], P('dp', 'seq'), may hold values from -6 to 6
- cotangent: bfloat16 [8, 1024, 512], P('dp', 'seq'), may hold values from -6 to 6
- w_qkv: bfloat16 [2, 512, 1536], P('section'), may hold values from -0.5 to 0.5
- w_out: bfloat16 [2, 512, 512], P('section'), may hold values from -1 to 1
- first_norm_gain: float32 [2, 512], P('section'), may hold values from 0.25 to 1.75
- ln1_bias: float32 [2, 512], P('section'), may hold values from -0.6 to 0.6
- w_up: bfloat16 [2, 512, 2048], P('section'), may hold values from -0.25 to 0.25
- b_up: float32 [2, 2048], P('section'), may hold values from -1.8 to 1.8
- w_down: bfloat16 [2, 2048, 512], P('section'), may hold values from -0.125 to 0.125
- b_down: float32 [2, 512], P('section'), may hold values from -0.6 to 0.6
- ln2_gain: float32 [2, 512], P('section'), may hold values from 0.25 to 1.75
- ln2_bias: float32 [2, 512], P('section'), may hold values from -0.6 to 0.6
Outputs:
- layer_outputs: bfloat16 [2, 8, 1024, 512], P('section', 'dp', 'seq')
- input_grads: bfloat16 [2, 8, 1024, 512], P('section', 'dp', 'seq')
- grad_w_qkv: float32 [2, 512, 1536], P('section')
- grad_w_out: float32 [2, 512, 512], P('section')
- grad_ln1_gain: float32 [2, 512], P('section')
- grad_ln1_bias: float32 [2, 512], P('section')
- grad_w_up: float32 [2, 512, 2048], P('section')
- grad_b_up: float32 [2, 2048], P('section')
- grad_w_down: float32 [2, 2048, 512], P('section')
- grad_b_down: float32 [2, 512], P('section')
- grad_ln2_gain: float32 [2, 512], P('section')
- grad_ln2_bias: float32 [2, 512], P('section')
The draws below stay inside these ranges and needn't reach their ends.
All inputs are finite; a program needn't handle non-finite values.
Results may differ from the reference program's by a relative error of at most 0.014.
Values may be sent and summed in bfloat16 or wider, within the bound.
No kernel may reach another device: no remote copies, remote signals or barrier semaphores. Data moves between devices by JAX's collectives and lax.ppermute only.
A program may use at most 192 MiB of HBM per device.

```python
import math
import jax
import jax.numpy as jnp
from jax import lax

D = 512
HEADS = 8
HEAD_DIM = 64
FF = 2048
LAYERS = 2
LEN = 1024
SEQS = 8


def block_levels(own_key, dims, split, least, top_value):
    factor_of = 1.0
    for position, blocks in split:
        heights = jax.random.uniform(jax.random.fold_in(jax.random.fold_in(own_key, 6), position), (blocks,), jnp.float32, least / len(split), top_value / len(split))
        factor_of = factor_of * jnp.repeat(jnp.exp(heights), dims[position] // blocks).reshape((-1,) + (1,) * (len(dims) - 1 - position))
    return factor_of


def bell_draw(own_key, dims, deviation, limit, shards=(), held_as=jnp.bfloat16):
    array = jax.random.normal(own_key, dims, jnp.float32) * deviation
    if len(shards) > 0:
        array = block_levels(own_key, dims, shards, -0.22, 0.18) * array
    return jnp.clip(array, min=-limit, max=limit).astype(held_as)


def setup_inputs(seed: int = 0) -> dict:
    keys = jax.random.split(jax.random.key(seed), 13)
    tokens = bell_draw(keys[0], (SEQS, LEN, D), 1.0, 6.0, ((0, 4), (1, 4)))
    cotangent = bell_draw(keys[1], (SEQS, LEN, D), 1.0, 6.0, ((0, 4), (1, 4)))
    w_qkv = bell_draw(keys[2], (LAYERS, D, 3 * D), (D // 4) ** -0.5, 0.5, ((0, 2),))
    w_out = bell_draw(keys[3], (LAYERS, D, D), (D // 16) ** -0.5, 1.0, ((0, 2),))
    first_norm_gain = jnp.clip(1.0 + 0.15 * jax.random.normal(keys[4], (LAYERS, D), jnp.float32), 0.25, 1.75)
    ln1_bias = bell_draw(keys[5], (LAYERS, D), 0.1, 0.6, ((0, 2),), jnp.float32)
    w_up = bell_draw(keys[6], (LAYERS, D, FF), D ** -0.5, 0.25, ((0, 2),))
    b_up = bell_draw(keys[7], (LAYERS, FF), 0.3, 1.8, ((0, 2),), jnp.float32)
    w_down = bell_draw(keys[8], (LAYERS, FF, D), FF ** -0.5, 0.125, ((0, 2),))
    b_down = bell_draw(keys[9], (LAYERS, D), 0.1, 0.6, ((0, 2),), jnp.float32)
    ln2_gain = jnp.clip(1.0 + 0.15 * jax.random.normal(keys[10], (LAYERS, D), jnp.float32), 0.25, 1.75)
    ln2_bias = bell_draw(keys[11], (LAYERS, D), 0.1, 0.6, ((0, 2),), jnp.float32)
    return {"tokens": tokens, "cotangent": cotangent, "w_qkv": w_qkv, "w_out": w_out, "first_norm_gain": first_norm_gain, "ln1_bias": ln1_bias, "w_up": w_up, "b_up": b_up, "w_down": w_down, "b_down": b_down, "ln2_gain": ln2_gain, "ln2_bias": ln2_bias}


@jax.custom_vjp
def low(v):
    return lax.optimization_barrier(v.astype(jnp.bfloat16)).astype(jnp.float32)

@jax.custom_vjp
def low_back(v):
    return v

def low_keep(v):
    return (low(v), None)

def low_pass(kept, grad):
    return (grad,)

def back_keep(v):
    return (v, None)

def back_low(kept, grad):
    return (low(grad),)
low.defvjp(low_keep, low_pass)
low_back.defvjp(back_keep, back_low)
norm_eps = 1e-05

def matmul(operand_a, operand_b):
    return jnp.dot(operand_a, operand_b, precision=lax.Precision.HIGHEST, preferred_element_type=jnp.float32)

def norm_rows(values, gain_vec, bias_vec):
    row_mean = lax.optimization_barrier(jnp.mean(values, axis=-1, keepdims=True))
    centered = values - row_mean
    variance = lax.optimization_barrier(jnp.mean(centered * centered, axis=-1, keepdims=True))
    return centered * lax.rsqrt(variance + norm_eps) * gain_vec + bias_vec

def features(cos_weight, sin_weight, raw_values):
    positive = jax.nn.softplus(raw_values)
    return jnp.concatenate([positive * cos_weight[:, None, None], positive * sin_weight[:, None, None]], axis=-1)

def attend(query_feat, key_features_mapped, value_rows):
    length = query_feat.shape[0]
    block_len = 512 if length % 512 == 0 else length
    key_places = jnp.arange(length, dtype=jnp.int32)

    def one_block(block_index):
        offset = block_index * block_len
        query_matrix_rows = lax.dynamic_slice_in_dim(query_feat, offset, block_len, 0)
        score_matrix = jnp.einsum('jvr,zvr->vjz', query_matrix_rows, key_features_mapped, precision=lax.Precision.HIGHEST)
        token_places = offset + jnp.arange(block_len, dtype=jnp.int32)
        score_matrix = jnp.where((token_places[:, None] >= key_places[None, :])[None], score_matrix, 0.0)
        numerator = jnp.einsum('hqk,khe->qhe', score_matrix, value_rows, precision=lax.Precision.HIGHEST)
        denominator = lax.optimization_barrier(jnp.sum(score_matrix, axis=-1))
        return numerator / jnp.transpose(denominator)[:, :, None]
    blocks_out = lax.map(jax.checkpoint(one_block), jnp.arange(length // block_len, dtype=jnp.int32))
    return blocks_out.reshape(length, HEADS, HEAD_DIM)

def layer(layer_in, weights, cos_weight, sin_weight):
    w_qkv, w_out, first_norm_gain, ln1_bias, w_up, b_up, w_down, b_down, ln2_gain, ln2_bias = weights
    layer_in = low_back(layer_in)
    length = layer_in.shape[0]
    qkv_raw = low_back(matmul(layer_in, w_qkv)).reshape(length, 3, HEADS, HEAD_DIM)
    query_feat = low(features(cos_weight, sin_weight, qkv_raw[:, 0]))
    key_features_mapped = low(features(cos_weight, sin_weight, qkv_raw[:, 1]))
    value_rows = low(qkv_raw[:, 2])
    mixed_heads = low(attend(query_feat, key_features_mapped, value_rows).reshape(length, HEADS * HEAD_DIM))
    branch = low_back(matmul(mixed_heads, w_out))
    normed = norm_rows(layer_in + branch, first_norm_gain, ln1_bias)
    up_proj = low_back(matmul(low(normed), w_up) + b_up)
    hidden = low(jax.nn.gelu(up_proj, approximate=False))
    ffn_out = low_back(matmul(hidden, w_down) + b_down)
    return norm_rows(normed + ffn_out, ln2_gain, ln2_bias)

def reference(tokens, cotangent, w_qkv, w_out, first_norm_gain, ln1_bias, w_up, b_up, w_down, b_down, ln2_gain, ln2_bias):
    params = tuple((p.astype(jnp.float32) for p in (w_qkv, w_out, first_norm_gain, ln1_bias, w_up, b_up, w_down, b_down, ln2_gain, ln2_bias)))
    angles = jnp.arange(LEN, dtype=jnp.int32).astype(jnp.float32) * (math.pi / (2.0 * LEN))
    cos_weight = jnp.cos(angles)
    sin_weight = jnp.sin(angles)

    def forward(sequence_input, extra, *weights):
        first_set = tuple((w[0] for w in weights))
        second_group = tuple((w[1] for w in weights))
        middle = low(layer(sequence_input, first_set, cos_weight, sin_weight)) + extra
        return (middle, layer(middle, second_group, cos_weight, sin_weight))

    def seq_step(totals, inputs):
        seq_tokens, seq_cot = inputs
        sequence_input = seq_tokens.astype(jnp.float32)
        (middle, final_out), pullback = jax.vjp(forward, sequence_input, jnp.zeros_like(sequence_input), *params)
        gradients = pullback((jnp.zeros_like(middle), seq_cot.astype(jnp.float32)))
        totals = tuple((t_acc + g_new for t_acc, g_new in zip(totals, gradients[2:])))
        return (totals, (middle.astype(jnp.bfloat16), final_out.astype(jnp.bfloat16), gradients[0].astype(jnp.bfloat16), gradients[1].astype(jnp.bfloat16)))
    zero_sums = tuple((jnp.zeros_like(p) for p in params))
    totals, (middles, finals, d_first, d_second) = lax.scan(seq_step, zero_sums, (tokens, cotangent))
    return (jnp.stack([middles, finals]), jnp.stack([d_first, d_second]), totals[0], totals[1], totals[2], totals[3], totals[4], totals[5], totals[6], totals[7], totals[8], totals[9])
```

```python
import functools
import math

import jax
import jax.numpy as jnp
from jax import lax
from jax.experimental import pallas as pl
from jax.experimental.pallas import tpu as pltpu
from jax.sharding import PartitionSpec as P

D = 512
HEADS = 8
HEAD_DIM = 64
FF = 2048
PAIRS = HEADS // 2
EPS = 1e-05
BF = jnp.bfloat16
F32 = jnp.float32
MIB = 1024 * 1024


def dot(a, b):
    return lax.dot_general(a, b, (((1,), (0,)), ((), ())), preferred_element_type=F32)


def dot_nt(a, b):
    return lax.dot_general(a, b, (((1,), (1,)), ((), ())), preferred_element_type=F32)


def dot_tn(a, b):
    return lax.dot_general(a, b, (((0,), (0,)), ((), ())), preferred_element_type=F32)


def low_half(rows, lanes):
    place = lax.broadcasted_iota(jnp.int32, (rows, lanes), 1)
    return lax.rem(place, 128) < HEAD_DIM


def block_diag(pair):
    rows, lanes = pair.shape
    low = low_half(rows, lanes)
    zero = jnp.zeros_like(pair)
    return jnp.concatenate([jnp.where(low, pair, zero), jnp.where(low, zero, pair)], axis=0)


def pair_cols(ref, g, width=128):
    return ref[:, g * width : (g + 1) * width]


def value_block(v_pair):
    ones = jnp.ones_like(v_pair)
    return jnp.concatenate([block_diag(v_pair), block_diag(ones)], axis=1)


def pack_message(blocks, keys):
    places = lax.broadcasted_iota(jnp.int32, (16, 256), 0)
    tail = jnp.zeros((16, 256), F32)
    for g in range(PAIRS):
        tail = jnp.where(places == g, jnp.broadcast_to(keys[g], (16, 256)), tail)
    return jnp.concatenate(list(blocks) + [tail], axis=0).astype(BF)


def sum_messages(refs):
    total = refs[0][...].astype(F32)
    for ref in refs[1:]:
        total = total + ref[...].astype(F32)
    return total


def row_chunks(rows, step=32):
    return range(0, rows, step)


def row_mean(values):
    return jnp.sum(values, axis=-1, keepdims=True) * (1.0 / values.shape[-1])


def project(x, w_ref, cosb, sinb, outs, tmp):
    spq, spk, vv, sigq, sigk, qf, kf, msg = outs
    rows = x.shape[0]
    for part, (sp_ref, sig_ref, f_ref) in enumerate(((spq, sigq, qf), (spk, sigk, kf))):
        tmp[...] = dot(x, w_ref[:, part * D : (part + 1) * D])
        for r in row_chunks(rows):
            s = slice(r, r + 32)
            raw = tmp[s, :]
            tail = jnp.exp(-jnp.abs(raw))
            soft = jnp.maximum(raw, 0.0) + jnp.log1p(tail)
            sig = jnp.where(raw >= 0.0, 1.0, tail) / (1.0 + tail)
            sp_ref[s, :] = soft.astype(BF)
            sig_ref[s, :] = sig
            cos_rows = cosb[s, :]
            sin_rows = sinb[s, :]
            for g in range(PAIRS):
                pair = soft[:, 128 * g : 128 * (g + 1)]
                f_ref[s, 256 * g : 256 * g + 128] = (pair * cos_rows).astype(BF)
                f_ref[s, 256 * g + 128 : 256 * (g + 1)] = (pair * sin_rows).astype(BF)
    vv[...] = dot(x, w_ref[:, 2 * D : 3 * D]).astype(BF)
    low = low_half(64, 256)
    blocks, keys = [], []
    for g in range(PAIRS):
        kf_g = pair_cols(kf, g, 256)
        full = dot_tn(pair_cols(vv, g), kf_g)
        blocks.append(jnp.where(low, full[:64], full[64:]))
        keys.append(jnp.sum(kf_g.astype(F32), axis=0, keepdims=True))
    msg[...] = pack_message(blocks, keys)


def state_block(total, g):
    low = low_half(64, 256)
    block = total[64 * g : 64 * (g + 1), :]
    keys = jnp.broadcast_to(total[256 + g : 257 + g, :], (64, 256))
    zero = jnp.zeros((64, 256), F32)
    return jnp.concatenate(
        [
            jnp.where(low, block, zero),
            jnp.where(low, zero, block),
            jnp.where(low, keys, zero),
            jnp.where(low, zero, keys),
        ],
        axis=0,
    ).astype(BF)


def norm_forward(tmp, gain, bias, hat_ref, scale_ref, out_fn):
    rows = tmp.shape[0]
    for r in row_chunks(rows):
        s = slice(r, r + 32)
        values = tmp[s, :]
        centered = values - row_mean(values)
        scale = lax.rsqrt(row_mean(centered * centered) + EPS)
        hat = centered * scale
        hat_ref[s, :] = hat
        scale_ref[s, :] = jnp.broadcast_to(scale, (32, 128))
        out_fn(s, hat * gain + bias)


def attend_and_ffn(x_f32, spq, spk, vv, qf, recvs, mask, params, w_out, w_up, w_down, waits, outs, tmp, tmp_up):
    att, rden, mixed, hat1, scale1, normed, hidden, gprime, hat2, scale2, prefix, result = outs
    rows = spq.shape[0]
    total = sum_messages(recvs)
    prefix[...] = total
    mask2 = jnp.concatenate([mask[...], mask[...]], axis=1)
    for g in range(PAIRS):
        scores = dot_nt(pair_cols(spq, g), block_diag(pair_cols(spk, g))) * mask2
        both = dot(scores.astype(BF), value_block(pair_cols(vv, g)))
        both = both + dot_nt(pair_cols(qf, g, 256), state_block(total, g))
        inverse = 1.0 / both[:, 128:]
        attended = both[:, :128] * inverse
        cols = slice(128 * g, 128 * (g + 1))
        att[:, cols] = attended
        rden[:, cols] = inverse
        mixed[:, cols] = attended.astype(BF)
    gain1, bias1, b_down, gain2, bias2 = (params[i : i + 1, :] for i in range(5))
    waits[0]()
    tmp[...] = x_f32() + dot(mixed[...], w_out[...])

    def put_normed(s, value):
        normed[s, :] = value.astype(BF)
        tmp[s, :] = value

    norm_forward(tmp, gain1, bias1, hat1, scale1, put_normed)
    waits[1]()
    for c in range(FF // D):
        cols = slice(c * D, (c + 1) * D)
        tmp_up[...] = dot(normed[...], w_up[:, cols])
        b_up = params[5 + c : 6 + c, :]
        for r in row_chunks(rows):
            s = slice(r, r + 32)
            up = tmp_up[s, :] + b_up
            cdf = 0.5 + 0.5 * lax.erf(up * (1.0 / math.sqrt(2.0)))
            density = jnp.exp(-0.5 * up * up) * (1.0 / math.sqrt(2.0 * math.pi))
            hidden[s, cols] = (up * cdf).astype(BF)
            gprime[s, cols] = (cdf + up * density).astype(BF)
    waits[2]()
    tmp[...] = tmp[...] + b_down + dot(hidden[...], w_down[...])

    def put_result(s, value):
        result[s, :] = value.astype(BF)

    norm_forward(tmp, gain2, bias2, hat2, scale2, put_result)


def column_sum(values):
    return jnp.sum(values, axis=0, keepdims=True)


def norm_backward(grad_fn, gain, hat_ref, scale_ref, rows, put):
    d_gain = jnp.zeros((1, D), F32)
    d_bias = jnp.zeros((1, D), F32)
    for r in row_chunks(rows):
        s = slice(r, r + 32)
        grad = grad_fn(s)
        hat = hat_ref[s, :]
        scaled = grad * gain
        first = row_mean(scaled)
        second = row_mean(scaled * hat)
        scale = scale_ref[s, :][:, :1]
        put(s, (scaled - first - hat * second) * scale)
        d_gain = d_gain + column_sum(grad * hat)
        d_bias = d_bias + column_sum(grad)
    return d_gain, d_bias


def ffn_backward(grad_fn, att, rden, qf, hat1, scale1, gprime, hat2, scale2, params, w_out, w_up, w_down, waits, outs, tmp, tmp_up):
    d_ffn, d_up, d_branch, d_pre_one, r_low, t_high, t_low, smalls, msg = outs
    rows = att.shape[0]
    gain1, gain2 = params[0:1, :], params[3:4, :]
    sums = {"b_down": jnp.zeros((1, D), F32)}

    def put_two(s, value):
        rounded = value.astype(BF)
        tmp[s, :] = value
        d_ffn[s, :] = rounded
        sums["b_down"] = sums["b_down"] + column_sum(rounded.astype(F32))

    d_gain2, d_bias2 = norm_backward(grad_fn, gain2, hat2, scale2, rows, put_two)
    waits[0]()
    b_up = []
    for c in range(FF // D):
        cols = slice(c * D, (c + 1) * D)
        tmp_up[...] = dot_nt(d_ffn[...], w_down[cols, :])
        total = jnp.zeros((1, D), F32)
        for r in row_chunks(rows):
            s = slice(r, r + 32)
            value = (tmp_up[s, :] * gprime[s, cols].astype(F32)).astype(BF)
            d_up[s, cols] = value
            total = total + column_sum(value.astype(F32))
        b_up.append(total)
    waits[1]()
    tmp[...] = tmp[...] + dot_nt(d_up[...], w_up[...])

    def put_one(s, value):
        d_pre_one[s, :] = value
        d_branch[s, :] = value.astype(BF)

    d_gain1, d_bias1 = norm_backward(lambda s: tmp[s, :], gain1, hat1, scale1, rows, put_one)
    waits[2]()
    tmp[...] = dot_nt(d_branch[...], w_out[...])
    for r in row_chunks(rows):
        s = slice(r, r + 32)
        rounded = (tmp[s, :] * rden[s, :]).astype(BF)
        product = -(rounded.astype(F32) * att[s, :])
        high = product.astype(BF)
        r_low[s, :] = rounded
        t_high[s, :] = high
        t_low[s, :] = (product - high.astype(F32)).astype(BF)
    low = low_half(64, 256)
    blocks, keys = [], []
    for g in range(PAIRS):
        sides = jnp.concatenate([pair_cols(r_low, g), pair_cols(t_high, g)], axis=1)
        full = dot_tn(sides, pair_cols(qf, g, 256))
        blocks.append(jnp.where(low, full[:64], full[64:128]))
        keys.append(column_sum(jnp.where(low, full[128:192], full[192:])))
    msg[...] = pack_message(blocks, keys)
    smalls[...] = jnp.concatenate(
        [d_gain1, d_bias1, sums["b_down"], d_gain2, d_bias2] + b_up + [jnp.zeros((7, D), F32)], axis=0
    )


def ffn_weight_grads(sec, normed, hidden, d_ffn, d_up, out):
    for slot in range(2):
        half = sec if slot == 0 else 1 - sec
        for j in range(2):
            place = pl.multiple_of(half * (FF // 2) + j * D, D)
            out[slot, j * D : (j + 1) * D, :] = dot_tn(normed[...], d_up[:, pl.ds(place, D)]).astype(BF)
            out[slot, (2 + j) * D : (3 + j) * D, :] = dot_tn(
                hidden[:, pl.ds(place, D)], d_ffn[...]
            ).astype(BF)


def attention_backward(
    sec, x, spq, spk, vv, sigq, sigk, qf, kf, r_low, t_high, t_low, prefix, recvs, mask, mask_t, cosb, sinb,
    d_pre_one, mixed, d_branch, w_qkv, wait, outs, d_qkv,
):
    d_in, grads = outs
    total = sum_messages(recvs)
    mask2 = jnp.concatenate([mask[...], mask[...]], axis=1)
    mask_t2 = jnp.concatenate([mask_t[...], mask_t[...]], axis=1)
    low = low_half(64, 256)
    for g in range(PAIRS):
        spq_g, spk_g, vv_g = pair_cols(spq, g), pair_cols(spk, g), pair_cols(vv, g)
        r_g, th_g, tl_g = pair_cols(r_low, g), pair_cols(t_high, g), pair_cols(t_low, g)
        values = value_block(vv_g)
        spk_diag, spq_diag = block_diag(spk_g), block_diag(spq_g)
        r_diag = block_diag(r_g)
        sides = jnp.concatenate([r_g, th_g], axis=1)
        d_scores = dot_nt(sides, values) + dot_nt(tl_g, values[:, 128:])
        d_soft_q = dot((d_scores * mask2).astype(BF), spk_diag)
        state = state_block(prefix[...], g)
        d_feat = dot(sides, state) + dot(tl_g, state[128:, :])
        d_soft_q = d_soft_q + cosb[...] * d_feat[:, :128] + sinb[...] * d_feat[:, 128:]
        scores_t = (dot_nt(spk_g, spq_diag) * mask_t2).astype(BF)
        block = total[64 * g : 64 * (g + 1), :]
        zero = jnp.zeros_like(block)
        later = jnp.concatenate([jnp.where(low, block, zero), jnp.where(low, zero, block)], axis=0).astype(BF)
        d_value = dot(scores_t, r_diag) + dot_nt(pair_cols(kf, g, 256), later)
        d_scores_t = dot_nt(
            jnp.concatenate([vv_g, jnp.ones_like(vv_g)], axis=1),
            jnp.concatenate([r_diag, block_diag(th_g)], axis=1),
        )
        d_soft_k = dot((d_scores_t * mask_t2).astype(BF), spq_diag)
        d_feat_k = dot(vv_g, later) + total[256 + g : 257 + g, :]
        d_soft_k = d_soft_k + cosb[...] * d_feat_k[:, :128] + sinb[...] * d_feat_k[:, 128:]
        d_qkv[:, 128 * g : 128 * (g + 1)] = (pair_cols(sigq, g) * d_soft_q).astype(BF)
        d_qkv[:, D + 128 * g : D + 128 * (g + 1)] = (pair_cols(sigk, g) * d_soft_k).astype(BF)
        d_qkv[:, 2 * D + 128 * g : 2 * D + 128 * (g + 1)] = d_value.astype(BF)
    wait()
    d_in[...] = (d_pre_one[...] + dot_nt(d_qkv[...], w_qkv[...])).astype(BF)
    half_rows = D // 2
    for slot in range(2):
        half = sec if slot == 0 else 1 - sec
        place = pl.multiple_of(half * half_rows, half_rows)
        x_half = x(place, half_rows)
        for j in range(3):
            grads[slot, j * half_rows : (j + 1) * half_rows, :] = dot_tn(
                x_half, d_qkv[:, j * D : (j + 1) * D]
            ).astype(BF)
        grads[slot, 3 * half_rows :, :] = dot_tn(mixed[:, pl.ds(place, half_rows)], d_branch[...]).astype(BF)


def load_weights(sec, layer, pairs, sems):
    waits = []
    for i, (own, other, held) in enumerate(pairs):

        @pl.when(sec == layer)
        def _(own=own, held=held, i=i):
            pltpu.make_async_copy(own, held, sems.at[i]).start()

        @pl.when(sec != layer)
        def _(other=other, held=held, i=i):
            pltpu.make_async_copy(other, held, sems.at[i]).start()

        def wait(own=own, held=held, i=i):
            pltpu.make_async_copy(own, held, sems.at[i]).wait()

        waits.append(wait)
    return waits


def shape(rows, cols, kind):
    return jax.ShapeDtypeStruct((rows, cols), kind)


VMEM_SPEC = pl.BlockSpec(memory_space=pltpu.VMEM)
ANY_SPEC = pl.BlockSpec(memory_space=pl.ANY)


def call(kernel, args, specs, outs, scratch, name):
    return pl.pallas_call(
        kernel,
        out_shape=tuple(outs),
        in_specs=specs,
        out_specs=tuple(VMEM_SPEC for _ in outs),
        scratch_shapes=scratch,
        compiler_params=pltpu.CompilerParams(vmem_limit_bytes=48 * MIB),
        name=name,
    )(*args)


def run_project(layer, x, w_own, w_other, cosb, sinb, rows, pick):
    outs = [shape(rows, D, BF)] * 3 + [shape(rows, D, F32)] * 2 + [shape(rows, 2 * D, BF)] * 2 + [shape(272, 256, BF)]

    def kernel(x_ref, own, other, cos_ref, sin_ref, *rest):
        sec = lax.axis_index("section")
        out_refs, (held, tmp, sems) = rest[:8], rest[8:]
        (wait,) = load_weights(sec, layer, [(own, other, held)], sems)
        wait()
        x_rows = x_ref[sec] if pick else x_ref[...]
        project(x_rows, held, cos_ref, sin_ref, out_refs, tmp)

    return call(
        kernel,
        (x, w_own, w_other, cosb, sinb),
        [VMEM_SPEC, ANY_SPEC, ANY_SPEC, VMEM_SPEC, VMEM_SPEC],
        outs,
        [pltpu.VMEM((D, 3 * D), BF), pltpu.VMEM((rows, D), F32), pltpu.SemaphoreType.DMA((1,))],
        f"project_{layer}",
    )


def run_forward(layer, x, kept, recvs, mask, params, weights, rows, pick):
    spq, spk, vv, qf = kept
    outs = (
        [shape(rows, D, F32)] * 2
        + [shape(rows, D, BF), shape(rows, D, F32), shape(rows, 128, F32), shape(rows, D, BF)]
        + [shape(rows, FF, BF)] * 2
        + [shape(rows, D, F32), shape(rows, 128, F32), shape(272, 256, F32), shape(rows, D, BF)]
    )
    count = len(recvs)

    def kernel(*refs):
        sec = lax.axis_index("section")
        x_ref, spq_ref, spk_ref, vv_ref, qf_ref, mask_ref, own_p, other_p = refs[:8]
        recv_refs = refs[8 : 8 + count]
        w_refs = refs[8 + count : 14 + count]
        out_refs = refs[14 + count : 26 + count]
        held_out, held_up, held_down, params_ref, tmp, tmp_up, sems = refs[26 + count :]
        waits = load_weights(
            sec,
            layer,
            [(w_refs[0], w_refs[1], held_out), (w_refs[2], w_refs[3], held_up), (w_refs[4], w_refs[5], held_down)],
            sems,
        )
        params_ref[...] = jnp.where(sec == layer, own_p[...], other_p[...])
        attend_and_ffn(
            lambda: (x_ref[sec] if pick else x_ref[...]).astype(F32),
            spq_ref, spk_ref, vv_ref, qf_ref, recv_refs, mask_ref, params_ref,
            held_out, held_up, held_down, waits, out_refs, tmp, tmp_up,
        )

    return call(
        kernel,
        (x, spq, spk, vv, qf, mask, *params, *recvs, *weights),
        [VMEM_SPEC] * (8 + count) + [ANY_SPEC] * 6,
        outs,
        [
            pltpu.VMEM((D, D), BF),
            pltpu.VMEM((D, FF), BF),
            pltpu.VMEM((FF, D), BF),
            pltpu.VMEM((16, D), F32),
            pltpu.VMEM((rows, D), F32),
            pltpu.VMEM((rows, D), F32),
            pltpu.SemaphoreType.DMA((3,)),
        ],
        f"forward_{layer}",
    )


def run_ffn_backward(layer, grad, kept, params, weights, rows, pick):
    outs = (
        [shape(rows, D, BF), shape(rows, FF, BF), shape(rows, D, BF), shape(rows, D, F32)]
        + [shape(rows, D, BF)] * 3
        + [shape(16, D, F32), shape(272, 256, BF)]
    )

    def kernel(*refs):
        sec = lax.axis_index("section")
        g_ref, att, rden, qf, hat1, scale1, gprime, hat2, scale2, own_p, other_p = refs[:11]
        w_refs = refs[11:17]
        out_refs = refs[17:26]
        held_out, held_up, held_down, params_ref, tmp, tmp_up, sems = refs[26:]
        waits = load_weights(
            sec,
            layer,
            [(w_refs[4], w_refs[5], held_down), (w_refs[2], w_refs[3], held_up), (w_refs[0], w_refs[1], held_out)],
            sems,
        )
        params_ref[...] = jnp.where(sec == layer, own_p[...], other_p[...])

        def grad_fn(s):
            return (g_ref[sec, s, :] if pick else g_ref[s, :]).astype(F32)

        ffn_backward(
            grad_fn, att, rden, qf, hat1, scale1, gprime, hat2, scale2, params_ref,
            held_out, held_up, held_down, waits, out_refs, tmp, tmp_up,
        )

    return call(
        kernel,
        (grad, *kept, *params, *weights),
        [VMEM_SPEC] * 11 + [ANY_SPEC] * 6,
        outs,
        [
            pltpu.VMEM((D, D), BF),
            pltpu.VMEM((D, FF), BF),
            pltpu.VMEM((FF, D), BF),
            pltpu.VMEM((16, D), F32),
            pltpu.VMEM((rows, D), F32),
            pltpu.VMEM((rows, D), F32),
            pltpu.SemaphoreType.DMA((3,)),
        ],
        f"ffn_backward_{layer}",
    )


def run_ffn_grads(layer, normed, hidden, d_ffn, d_up):
    def kernel(normed_ref, hidden_ref, d_ffn_ref, d_up_ref, out):
        ffn_weight_grads(lax.axis_index("section"), normed_ref, hidden_ref, d_ffn_ref, d_up_ref, out)

    return call(
        kernel,
        (normed, hidden, d_ffn, d_up),
        [VMEM_SPEC] * 4,
        [jax.ShapeDtypeStruct((2, 4 * D, D), BF)],
        [],
        f"ffn_grads_{layer}",
    )[0]


def run_attention_backward(layer, x, kept, recvs, fixed, w_own, w_other, rows, pick):
    count = len(recvs)
    kept_count = len(kept)

    def kernel(*refs):
        sec = lax.axis_index("section")
        x_ref = refs[0]
        spq, spk, vv, sigq, sigk, qf, kf, r_low, t_high, t_low, prefix, d_pre_one, mixed, d_branch = refs[
            1 : 1 + kept_count
        ]
        rest = refs[1 + kept_count :]
        recv_refs = rest[:count]
        mask, mask_t, cosb, sinb, own, other = rest[count : count + 6]
        d_in, grads, held, d_qkv, sems = rest[count + 6 :]
        (wait,) = load_weights(sec, layer, [(own, other, held)], sems)

        def x_cols(place, width):
            cols = pl.ds(place, width)
            return x_ref[sec, :, cols] if pick else x_ref[:, cols]

        attention_backward(
            sec, x_cols, spq, spk, vv, sigq, sigk, qf, kf, r_low, t_high, t_low, prefix, recv_refs, mask, mask_t,
            cosb, sinb, d_pre_one, mixed, d_branch, held, wait, (d_in, grads), d_qkv,
        )

    return call(
        kernel,
        (x, *kept, *recvs, *fixed, w_own, w_other),
        [VMEM_SPEC] * (5 + kept_count + count) + [ANY_SPEC] * 2,
        [shape(rows, D, BF), jax.ShapeDtypeStruct((2, 2 * D, D), BF)],
        [pltpu.VMEM((D, 3 * D), BF), pltpu.VMEM((rows, 3 * D), BF), pltpu.SemaphoreType.DMA((1,))],
        f"attention_backward_{layer}",
    )


def swap_cores(block):
    return lax.ppermute(block, "section", [(0, 1), (1, 0)])


def from_others(message, backward):
    count = lax.axis_size("seq")
    received = []
    for distance in range(1, count):
        if backward:
            route = [(i + distance, i) for i in range(count - distance)]
        else:
            route = [(i, i + distance) for i in range(count - distance)]
        received.append(lax.ppermute(message, "seq", route))
    return received


def reduce_halves(halves):
    other = swap_cores(halves[1])
    total = (halves[0].astype(F32) + other.astype(F32)).astype(BF)
    return lax.psum(total, ("dp", "seq"))


def body(tokens, cotangent, w_qkv, w_out, first_norm_gain, ln1_bias, w_up, b_up, w_down, b_down, ln2_gain, ln2_bias):
    sec = lax.axis_index("section")
    rows = tokens.shape[1]
    whole = rows * lax.axis_size("seq")
    step = math.pi / (2.0 * whole)
    own_w = tuple(w[0] for w in (w_qkv, w_out, w_up, w_down))
    other_w = tuple(swap_cores(w) for w in own_w)
    own_p = jnp.concatenate(
        [first_norm_gain, ln1_bias, b_down, ln2_gain, ln2_bias, b_up.reshape(4, D), jnp.zeros((7, D), F32)], axis=0
    )
    params = (own_p, swap_cores(own_p))
    places = jnp.arange(rows, dtype=jnp.int32)
    angles = (lax.axis_index("seq") * rows + places).astype(F32) * step
    cosb = jnp.broadcast_to(jnp.cos(angles)[:, None], (rows, 128))
    sinb = jnp.broadcast_to(jnp.sin(angles)[:, None], (rows, 128))
    apart = places[:, None] - places[None, :]
    near = jnp.cos(apart.astype(F32) * step)
    mask = jnp.where(apart >= 0, near, 0.0)
    mask_t = jnp.where(apart <= 0, near, 0.0)
    fixed = (mask, mask_t, cosb, sinb)
    qkv_w = (own_w[0], other_w[0])
    rest_w = (own_w[1], other_w[1], own_w[2], other_w[2], own_w[3], other_w[3])

    saved = []
    x = tokens
    for layer in range(2):
        pick = layer == 0
        spq, spk, vv, sigq, sigk, qf, kf, msg = run_project(layer, x, *qkv_w, cosb, sinb, rows, pick)
        recvs = from_others(msg, False)
        forward = run_forward(layer, x, (spq, spk, vv, qf), recvs, mask, params, rest_w, rows, pick)
        saved.append((x, (spq, spk, vv, sigq, sigk, qf, kf), forward))
        x = forward[-1]
    mids = (saved[0][2][-1], saved[1][2][-1])

    grad = cotangent
    d_inputs = [None, None]
    ffn_sums, attention_sums, smalls = [None, None], [None, None], [None, None]
    for layer in (1, 0):
        x, (spq, spk, vv, sigq, sigk, qf, kf), forward = saved[layer]
        att, rden, mixed, hat1, scale1, normed, hidden, gprime, hat2, scale2, prefix, _ = forward
        d_ffn, d_up, d_branch, d_pre_one, r_low, t_high, t_low, smalls[layer], msg = run_ffn_backward(
            layer, grad, (att, rden, qf, hat1, scale1, gprime, hat2, scale2), params, rest_w, rows, layer == 1
        )
        recvs = from_others(msg, True)
        ffn_halves = run_ffn_grads(layer, normed, hidden, d_ffn, d_up)
        kept = (spq, spk, vv, sigq, sigk, qf, kf, r_low, t_high, t_low, prefix, d_pre_one, mixed, d_branch)
        grad, attention_halves = run_attention_backward(
            layer, x, kept, recvs, fixed, *qkv_w, rows, layer == 0
        )
        d_inputs[layer] = grad
        both = jnp.concatenate([ffn_halves, attention_halves], axis=1)
        summed = reduce_halves(both)
        ffn_sums[layer], attention_sums[layer] = summed[: 4 * D], summed[4 * D :]

    first = sec == 0

    def exchange_rows(pair):
        other = swap_cores(jnp.where(first, pair[1], pair[0]))
        return jnp.stack([jnp.where(first, pair[0], other), jnp.where(first, other, pair[1])])[None]

    layer_outputs = exchange_rows(mids)
    input_grads = exchange_rows(d_inputs)

    def both_halves(sums):
        other = swap_cores(jnp.where(first, sums[1], sums[0]))
        return jnp.where(first, sums[0], other).astype(F32), jnp.where(first, other, sums[1]).astype(F32)

    ffn_a, ffn_b = both_halves(ffn_sums)
    att_a, att_b = both_halves(attention_sums)
    grad_up = jnp.concatenate([h[j * D : (j + 1) * D] for h in (ffn_a, ffn_b) for j in range(2)], axis=1)
    grad_down = jnp.concatenate([h[2 * D :] for h in (ffn_a, ffn_b)], axis=0)
    half = D // 2
    grad_qkv = jnp.concatenate(
        [jnp.concatenate([h[j * half : (j + 1) * half] for j in range(3)], axis=1) for h in (att_a, att_b)], axis=0
    )
    grad_out = jnp.concatenate([h[3 * half :] for h in (att_a, att_b)], axis=0)
    small = jnp.where(first, smalls[0], smalls[1]) + swap_cores(jnp.where(first, smalls[1], smalls[0]))
    for axis in ("dp", "seq"):
        bit = 1
        while bit < lax.axis_size(axis):
            small = small + lax.ppermute(small, axis, [(i, i ^ bit) for i in range(lax.axis_size(axis))])
            bit *= 2
    d_gain1, d_bias1, d_b_down, d_gain2, d_bias2 = (small[i : i + 1] for i in range(5))
    d_b_up = small[5:9].reshape(1, FF)
    return (
        layer_outputs,
        input_grads,
        grad_qkv[None],
        grad_out[None],
        d_gain1,
        d_bias1,
        grad_up[None],
        d_b_up,
        grad_down[None],
        d_b_down,
        d_gain2,
        d_bias2,
    )


def solution(mesh):
    rows = P("dp", "seq", None)
    matrix = P("section", None, None)
    vector = P("section", None)
    out_rows = P("section", "dp", "seq", None)
    return jax.shard_map(
        body,
        mesh=mesh,
        in_specs=(rows, rows, matrix, matrix, vector, vector, matrix, vector, matrix, vector, vector, vector),
        out_specs=(
            out_rows, out_rows, matrix, matrix, vector, vector, matrix, vector, matrix, vector, vector, vector,
        ),
        check_vma=False,
    )
```

```python
import functools
import math

import jax
import jax.numpy as jnp
from jax import lax
from jax.experimental import pallas as pl
from jax.experimental.pallas import tpu as pltpu
from jax.sharding import PartitionSpec as P

D = 512
HEADS = 8
HEAD_DIM = 64
FF = 2048
PAIRS = HEADS // 2
EPS = 1e-05
BF = jnp.bfloat16
F32 = jnp.float32
MIB = 1024 * 1024


def dot(a, b):
    return lax.dot_general(a, b, (((1,), (0,)), ((), ())), preferred_element_type=F32)


def dot_nt(a, b):
    return lax.dot_general(a, b, (((1,), (1,)), ((), ())), preferred_element_type=F32)


def dot_tn(a, b):
    return lax.dot_general(a, b, (((0,), (0,)), ((), ())), preferred_element_type=F32)


def low_half(rows, lanes):
    place = lax.broadcasted_iota(jnp.int32, (rows, lanes), 1)
    return lax.rem(place, 128) < HEAD_DIM


def block_diag(pair):
    rows, lanes = pair.shape
    low = low_half(rows, lanes)
    zero = jnp.zeros_like(pair)
    return jnp.concatenate([jnp.where(low, pair, zero), jnp.where(low, zero, pair)], axis=0)


def pair_cols(ref, g, width=128):
    return ref[:, g * width : (g + 1) * width]


def value_block(v_pair):
    ones = jnp.ones_like(v_pair)
    return jnp.concatenate([block_diag(v_pair), block_diag(ones)], axis=1)


def pack_message(blocks, keys):
    places = lax.broadcasted_iota(jnp.int32, (16, 256), 0)
    tail = jnp.zeros((16, 256), F32)
    for g in range(PAIRS):
        tail = jnp.where(places == g, jnp.broadcast_to(keys[g], (16, 256)), tail)
    return jnp.concatenate(list(blocks) + [tail], axis=0).astype(BF)


def place():
    length = lax.axis_size("seq") // 2
    z = lax.axis_index("seq")
    lower = z < length
    return lax.axis_index("section"), lower, jnp.where(lower, z, z - length), length


def sum_messages(refs, backward):
    core, _, j, length = place()
    total = jnp.zeros(refs[0].shape, F32)
    for i, ref in enumerate(refs):
        distance = i + 1
        if distance < length:
            wanted = j < distance if backward else j >= distance
        else:
            wanted = core == (0 if backward else 1)
        total = total + jnp.where(wanted, ref[...].astype(F32), 0.0)
    return total


def row_chunks(rows, step=32):
    return range(0, rows, step)


def row_mean(values):
    return jnp.sum(values, axis=-1, keepdims=True) * (1.0 / values.shape[-1])


def project(x, w_ref, waits, cosb, sinb, outs, tmp):
    spq, spk, vv, sigq, sigk, qf, kf, msg = outs
    rows = x.shape[0]

    def softplus_part(part, sp_ref, sig_ref, f_ref):
        waits[part]()
        tmp[...] = dot(x, w_ref[:, part * D : (part + 1) * D])
        for r in row_chunks(rows):
            s = slice(r, r + 32)
            raw = tmp[s, :]
            tail = jnp.exp(-jnp.abs(raw))
            soft = jnp.maximum(raw, 0.0) + jnp.log1p(tail)
            sig = jnp.where(raw >= 0.0, 1.0, tail) / (1.0 + tail)
            sp_ref[s, :] = soft.astype(BF)
            sig_ref[s, :] = sig
            cos_rows = cosb[s, :]
            sin_rows = sinb[s, :]
            for g in range(PAIRS):
                pair = soft[:, 128 * g : 128 * (g + 1)]
                f_ref[s, 256 * g : 256 * g + 128] = (pair * cos_rows).astype(BF)
                f_ref[s, 256 * g + 128 : 256 * (g + 1)] = (pair * sin_rows).astype(BF)

    softplus_part(1, spk, sigk, kf)
    waits[2]()
    vv[...] = dot(x, w_ref[:, 2 * D : 3 * D]).astype(BF)
    softplus_part(0, spq, sigq, qf)
    low = low_half(64, 256)
    blocks, keys = [], []
    for g in range(PAIRS):
        kf_g = pair_cols(kf, g, 256)
        full = dot_tn(pair_cols(vv, g), kf_g)
        blocks.append(jnp.where(low, full[:64], full[64:]))
        keys.append(jnp.sum(kf_g.astype(F32), axis=0, keepdims=True))
    msg[...] = pack_message(blocks, keys)


def state_block(total, g):
    low = low_half(64, 256)
    block = total[64 * g : 64 * (g + 1), :]
    keys = jnp.broadcast_to(total[256 + g : 257 + g, :], (64, 256))
    zero = jnp.zeros((64, 256), F32)
    return jnp.concatenate(
        [
            jnp.where(low, block, zero),
            jnp.where(low, zero, block),
            jnp.where(low, keys, zero),
            jnp.where(low, zero, keys),
        ],
        axis=0,
    ).astype(BF)


def norm_forward(tmp, gain, bias, hat_ref, scale_ref, out_fn):
    rows = tmp.shape[0]
    for r in row_chunks(rows):
        s = slice(r, r + 32)
        values = tmp[s, :]
        centered = values - row_mean(values)
        scale = lax.rsqrt(row_mean(centered * centered) + EPS)
        hat = centered * scale
        hat_ref[s, :] = hat
        scale_ref[s, :] = jnp.broadcast_to(scale, (32, 128))
        out_fn(s, hat * gain + bias)


def near_attention(spq, spk, vv, mask, near):
    mask2 = jnp.concatenate([mask[...], mask[...]], axis=1)
    for g in range(PAIRS):
        scores = dot_nt(pair_cols(spq, g), block_diag(pair_cols(spk, g))) * mask2
        near[:, 256 * g : 256 * (g + 1)] = dot(scores.astype(BF), value_block(pair_cols(vv, g)))


def attend_and_ffn(x, near, qf, recvs, params, w_out, w_up, w_down, waits, outs, tmp, tmp_up):
    att, rden, mixed, hat1, scale1, normed, hidden, gprime, hat2, scale2, prefix, result = outs
    rows = x.shape[0]
    total = sum_messages(recvs, False)
    prefix[...] = total
    for g in range(PAIRS):
        both = pair_cols(near, g, 256) + dot_nt(pair_cols(qf, g, 256), state_block(total, g))
        inverse = 1.0 / both[:, 128:]
        attended = both[:, :128] * inverse
        cols = slice(128 * g, 128 * (g + 1))
        att[:, cols] = attended
        rden[:, cols] = inverse
        mixed[:, cols] = attended.astype(BF)
    gain1, bias1, b_down, gain2, bias2 = (params[i : i + 1, :] for i in range(5))
    waits[0]()
    tmp[...] = x[...].astype(F32) + dot(mixed[...], w_out[...])

    def put_normed(s, value):
        normed[s, :] = value.astype(BF)
        tmp[s, :] = value

    norm_forward(tmp, gain1, bias1, hat1, scale1, put_normed)
    waits[1]()
    for c in range(FF // D):
        cols = slice(c * D, (c + 1) * D)
        tmp_up[...] = dot(normed[...], w_up[:, cols])
        b_up = params[5 + c : 6 + c, :]
        for r in row_chunks(rows):
            s = slice(r, r + 32)
            up = tmp_up[s, :] + b_up
            cdf = 0.5 + 0.5 * lax.erf(up * (1.0 / math.sqrt(2.0)))
            density = jnp.exp(-0.5 * up * up) * (1.0 / math.sqrt(2.0 * math.pi))
            hidden[s, cols] = (up * cdf).astype(BF)
            gprime[s, cols] = (cdf + up * density).astype(BF)
    waits[2]()
    tmp[...] = tmp[...] + b_down + dot(hidden[...], w_down[...])

    def put_result(s, value):
        result[s, :] = value.astype(BF)

    norm_forward(tmp, gain2, bias2, hat2, scale2, put_result)


def column_sum(values):
    return jnp.sum(values, axis=0, keepdims=True)


def norm_backward(grad_fn, gain, hat_ref, scale_ref, rows, put):
    d_gain = jnp.zeros((1, D), F32)
    d_bias = jnp.zeros((1, D), F32)
    for r in row_chunks(rows):
        s = slice(r, r + 32)
        grad = grad_fn(s)
        hat = hat_ref[s, :]
        scaled = grad * gain
        first = row_mean(scaled)
        second = row_mean(scaled * hat)
        scale = scale_ref[s, :][:, :1]
        put(s, (scaled - first - hat * second) * scale)
        d_gain = d_gain + column_sum(grad * hat)
        d_bias = d_bias + column_sum(grad)
    return d_gain, d_bias


def ffn_backward(grad, att, rden, qf, hat1, scale1, gprime, hat2, scale2, params, w_out, w_up, w_down, waits, outs, tmp, tmp_up):
    d_ffn, d_up, d_branch, d_pre_one, r_low, t_high, t_low, smalls, msg = outs
    rows = att.shape[0]
    gain1, gain2 = params[0:1, :], params[3:4, :]
    sums = {"b_down": jnp.zeros((1, D), F32)}

    def put_two(s, value):
        rounded = value.astype(BF)
        tmp[s, :] = value
        d_ffn[s, :] = rounded
        sums["b_down"] = sums["b_down"] + column_sum(rounded.astype(F32))

    d_gain2, d_bias2 = norm_backward(lambda s: grad[s, :].astype(F32), gain2, hat2, scale2, rows, put_two)
    waits[0]()
    b_up = []
    for c in range(FF // D):
        cols = slice(c * D, (c + 1) * D)
        tmp_up[...] = dot_nt(d_ffn[...], w_down[cols, :])
        total = jnp.zeros((1, D), F32)
        for r in row_chunks(rows):
            s = slice(r, r + 32)
            value = (tmp_up[s, :] * gprime[s, cols].astype(F32)).astype(BF)
            d_up[s, cols] = value
            total = total + column_sum(value.astype(F32))
        b_up.append(total)
    waits[1]()
    tmp[...] = tmp[...] + dot_nt(d_up[...], w_up[...])

    def put_one(s, value):
        d_pre_one[s, :] = value
        d_branch[s, :] = value.astype(BF)

    d_gain1, d_bias1 = norm_backward(lambda s: tmp[s, :], gain1, hat1, scale1, rows, put_one)
    waits[2]()
    tmp[...] = dot_nt(d_branch[...], w_out[...])
    for r in row_chunks(rows):
        s = slice(r, r + 32)
        rounded = (tmp[s, :] * rden[s, :]).astype(BF)
        product = -(rounded.astype(F32) * att[s, :])
        high = product.astype(BF)
        r_low[s, :] = rounded
        t_high[s, :] = high
        t_low[s, :] = (product - high.astype(F32)).astype(BF)
    low = low_half(64, 256)
    blocks, keys = [], []
    for g in range(PAIRS):
        sides = jnp.concatenate([pair_cols(r_low, g), pair_cols(t_high, g)], axis=1)
        full = dot_tn(sides, pair_cols(qf, g, 256))
        blocks.append(jnp.where(low, full[:64], full[64:128]))
        keys.append(column_sum(jnp.where(low, full[128:192], full[192:])))
    msg[...] = pack_message(blocks, keys)
    smalls[...] = jnp.concatenate(
        [d_gain1, d_bias1, sums["b_down"], d_gain2, d_bias2] + b_up + [jnp.zeros((7, D), F32)], axis=0
    )


def near_backward(spq, spk, vv, r_low, t_high, t_low, mask, mask_t, outs):
    near_q, near_k, near_v = outs
    mask2 = jnp.concatenate([mask[...], mask[...]], axis=1)
    mask_t2 = jnp.concatenate([mask_t[...], mask_t[...]], axis=1)
    for g in range(PAIRS):
        spq_g, spk_g, vv_g = pair_cols(spq, g), pair_cols(spk, g), pair_cols(vv, g)
        r_g, th_g, tl_g = pair_cols(r_low, g), pair_cols(t_high, g), pair_cols(t_low, g)
        values = value_block(vv_g)
        spk_diag, spq_diag, r_diag = block_diag(spk_g), block_diag(spq_g), block_diag(r_g)
        cols = slice(128 * g, 128 * (g + 1))
        d_scores = dot_nt(jnp.concatenate([r_g, th_g], axis=1), values) + dot_nt(tl_g, values[:, 128:])
        near_q[:, cols] = dot((d_scores * mask2).astype(BF), spk_diag)
        scores_t = (dot_nt(spk_g, spq_diag) * mask_t2).astype(BF)
        near_v[:, cols] = dot(scores_t, r_diag)
        d_scores_t = dot_nt(
            jnp.concatenate([vv_g, jnp.ones_like(vv_g)], axis=1),
            jnp.concatenate([r_diag, block_diag(th_g)], axis=1),
        )
        near_k[:, cols] = dot((d_scores_t * mask_t2).astype(BF), spq_diag)


def attention_backward(
    x, vv, sigq, sigk, kf, r_low, t_high, t_low, prefix, near, recvs, cosb, sinb,
    d_pre_one, mixed, d_branch, smalls, w_qkv, wait, outs, d_qkv,
):
    d_in, kept, sent = outs
    near_q, near_k, near_v = near
    total = sum_messages(recvs, True)
    low = low_half(64, 256)
    for g in range(PAIRS):
        cols = slice(128 * g, 128 * (g + 1))
        vv_g = pair_cols(vv, g)
        sides = jnp.concatenate([pair_cols(r_low, g), pair_cols(t_high, g)], axis=1)
        state = state_block(prefix[...], g)
        d_feat = dot(sides, state) + dot(pair_cols(t_low, g), state[128:, :])
        d_soft_q = near_q[:, cols] + cosb[...] * d_feat[:, :128] + sinb[...] * d_feat[:, 128:]
        block = total[64 * g : 64 * (g + 1), :]
        zero = jnp.zeros_like(block)
        later = jnp.concatenate([jnp.where(low, block, zero), jnp.where(low, zero, block)], axis=0).astype(BF)
        d_value = near_v[:, cols] + dot_nt(pair_cols(kf, g, 256), later)
        d_feat_k = dot(vv_g, later) + total[256 + g : 257 + g, :]
        d_soft_k = near_k[:, cols] + cosb[...] * d_feat_k[:, :128] + sinb[...] * d_feat_k[:, 128:]
        d_qkv[:, 128 * g : 128 * (g + 1)] = (pair_cols(sigq, g) * d_soft_q).astype(BF)
        d_qkv[:, D + 128 * g : D + 128 * (g + 1)] = (pair_cols(sigk, g) * d_soft_k).astype(BF)
        d_qkv[:, 2 * D + 128 * g : 2 * D + 128 * (g + 1)] = d_value.astype(BF)
    wait()
    d_in[...] = (d_pre_one[...] + dot_nt(d_qkv[...], w_qkv[...])).astype(BF)
    core = lax.axis_index("section")
    _, ids = part_ids(1)
    half_rows = D // 2
    for out, half in ((kept, core), (sent, 1 - core)):
        start = pl.multiple_of(half * half_rows, half_rows)
        x_half = x[:, pl.ds(start, half_rows)]
        for j in range(3):
            store_chunks(out, j * half_rows, dot_tn(x_half, d_qkv[:, j * D : (j + 1) * D]).astype(BF), ids[0], 4 * half_rows)
        value = dot_tn(mixed[:, pl.ds(start, half_rows)], d_branch[...]).astype(BF)
        store_chunks(out, 3 * half_rows, value, ids[0], 4 * half_rows)
        put_smalls(out, 4 * half_rows, smalls[...])


def ffn_weight_grads(normed, hidden, d_ffn, d_up, kept, sent):
    core = lax.axis_index("section")
    _, ids = part_ids(0)
    for out, half in ((kept, core), (sent, 1 - core)):
        order = jnp.where(half == 0, ids[0], ids[1])
        for j in range(2):
            start = pl.multiple_of(half * (FF // 2) + j * D, D)
            store_chunks(out, j * D, dot_tn(normed[...], d_up[:, pl.ds(start, D)]).astype(BF), order, 4 * D)
            value = dot_tn(hidden[:, pl.ds(start, D)], d_ffn[...]).astype(BF)
            store_chunks(out, (2 + j) * D, value, order, 4 * D)


def partner_bits():
    bits = [(axis, i) for axis in ("dp", "seq") for i in range(lax.axis_size(axis).bit_length() - 1)]
    last = bits.pop()
    return bits, last


def turned(bits, places):
    return bits[places:] + bits[:places]


def orders_of(part):
    bits, _ = partner_bits()
    third = max(1, len(bits) // 3)
    if part == 0:
        return [bits, turned(bits, third)]
    return [turned(bits, 2 * third)] * 2


def part_ids(part):
    ids = []
    for order in orders_of(part):
        number = jnp.int32(0)
        for axis, i in order:
            number = 2 * number + lax.rem(lax.div(lax.axis_index(axis), 1 << i), 2)
        ids.append(number)
    return len(orders_of(part)[0]), ids


def chunk_rows(total):
    bits, _ = partner_bits()
    return total >> len(bits)


def store_chunks(out, first_row, value, number, total):
    size = chunk_rows(total)
    for i in range(value.shape[0] // size):
        chunk = first_row // size + i
        spot = pl.multiple_of(jnp.bitwise_xor(jnp.int32(chunk), number) * size, size)
        out[pl.ds(spot, size), :] = value[i * size : (i + 1) * size, :]


SMALL = 32


def put_smalls(out, start, value):
    high = value.astype(BF)
    out[start : start + 16, :] = high
    out[start + 16 : start + SMALL, :] = (value - high.astype(F32)).astype(BF)


def get_smalls(ref, start):
    return ref[start : start + 16, :].astype(F32) + ref[start + 16 : start + SMALL, :].astype(F32)


def load_weights(core, layer, pairs, sems):
    waits = []
    for own, other, held, parts in pairs:
        width = held.shape[1] // parts
        for p in range(parts):
            i = len(waits)
            cols = slice(p * width, (p + 1) * width)

            @pl.when(core == layer)
            def _(own=own, held=held, i=i, cols=cols):
                pltpu.make_async_copy(own.at[:, cols], held.at[:, cols], sems.at[i]).start()

            @pl.when(core != layer)
            def _(other=other, held=held, i=i, cols=cols):
                pltpu.make_async_copy(other.at[:, cols], held.at[:, cols], sems.at[i]).start()

            def wait(own=own, held=held, i=i, cols=cols):
                pltpu.make_async_copy(own.at[:, cols], held.at[:, cols], sems.at[i]).wait()

            waits.append(wait)
    return waits


def shape(rows, cols, kind):
    return jax.ShapeDtypeStruct((rows, cols), kind)


VMEM_SPEC = pl.BlockSpec(memory_space=pltpu.VMEM)
HBM_SPEC = pl.BlockSpec(memory_space=pltpu.HBM)


def call(kernel, args, specs, outs, scratch, name, micros, limit=16):
    return pl.pallas_call(
        kernel,
        out_shape=tuple(outs),
        in_specs=specs,
        out_specs=tuple(VMEM_SPEC for _ in outs),
        scratch_shapes=scratch,
        compiler_params=pltpu.CompilerParams(vmem_limit_bytes=limit * MIB),
        cost_estimate=pl.CostEstimate(flops=int(micros * 1.1e9), bytes_accessed=1 << 20, transcendentals=0),
        name=name,
    )(*args)


def run_project(layer, x, w_own, w_other, cosb, sinb):
    rows = x.shape[0]
    outs = [shape(rows, D, BF)] * 3 + [shape(rows, D, F32)] * 2 + [shape(rows, 2 * D, BF)] * 2 + [shape(272, 256, BF)]

    def kernel(x_ref, own, other, cos_ref, sin_ref, *rest):
        out_refs, (held, tmp, sems) = rest[:8], rest[8:]
        waits = load_weights(lax.axis_index("section"), layer, [(own, other, held, 3)], sems)
        project(x_ref[...], held, waits, cos_ref, sin_ref, out_refs, tmp)

    return call(
        kernel,
        (x, w_own, w_other, cosb, sinb),
        [VMEM_SPEC, HBM_SPEC, HBM_SPEC, VMEM_SPEC, VMEM_SPEC],
        outs,
        [pltpu.VMEM((D, 3 * D), BF), pltpu.VMEM((rows, D), F32), pltpu.SemaphoreType.DMA((3,))],
        f"project_{layer}",
        3,
    )


def run_near(layer, spq, spk, vv, mask):
    return call(
        near_attention,
        (spq, spk, vv, mask),
        [VMEM_SPEC] * 4,
        [shape(spq.shape[0], 2 * D, F32)],
        [],
        f"near_{layer}",
        3,
    )[0]


def ffn_scratch(rows):
    return [
        pltpu.VMEM((D, D), BF),
        pltpu.VMEM((D, FF), BF),
        pltpu.VMEM((FF, D), BF),
        pltpu.VMEM((16, D), F32),
        pltpu.VMEM((rows, D), F32),
        pltpu.VMEM((rows, D), F32),
        pltpu.SemaphoreType.DMA((3,)),
    ]


def run_forward(layer, x, near, qf, recvs, params, weights):
    rows = x.shape[0]
    outs = (
        [shape(rows, D, F32)] * 2
        + [shape(rows, D, BF), shape(rows, D, F32), shape(rows, 128, F32), shape(rows, D, BF)]
        + [shape(rows, FF, BF)] * 2
        + [shape(rows, D, F32), shape(rows, 128, F32), shape(272, 256, F32), shape(rows, D, BF)]
    )
    count = len(recvs)

    def kernel(*refs):
        core = lax.axis_index("section")
        x_ref, near_ref, qf_ref, own_p, other_p = refs[:5]
        recv_refs = refs[5 : 5 + count]
        w = refs[5 + count : 11 + count]
        out_refs = refs[11 + count : 23 + count]
        held_out, held_up, held_down, params_ref, tmp, tmp_up, sems = refs[23 + count :]
        waits = load_weights(
            core, layer, [(w[0], w[1], held_out, 1), (w[2], w[3], held_up, 1), (w[4], w[5], held_down, 1)], sems
        )
        params_ref[...] = jnp.where(core == layer, own_p[...], other_p[...])
        attend_and_ffn(
            x_ref, near_ref, qf_ref, recv_refs, params_ref, held_out, held_up, held_down, waits, out_refs, tmp, tmp_up
        )

    return call(
        kernel,
        (x, near, qf, *params, *recvs, *weights),
        [VMEM_SPEC] * (5 + count) + [HBM_SPEC] * 6,
        outs,
        ffn_scratch(rows),
        f"forward_{layer}",
        5,
        20,
    )


def run_ffn_backward(layer, grad, kept, params, weights):
    rows = grad.shape[0]
    outs = (
        [shape(rows, D, BF), shape(rows, FF, BF), shape(rows, D, BF), shape(rows, D, F32)]
        + [shape(rows, D, BF)] * 3
        + [shape(16, D, F32), shape(272, 256, BF)]
    )

    def kernel(*refs):
        core = lax.axis_index("section")
        grad_ref, att, rden, qf, hat1, scale1, gprime, hat2, scale2, own_p, other_p = refs[:11]
        w = refs[11:17]
        out_refs = refs[17:26]
        held_out, held_up, held_down, params_ref, tmp, tmp_up, sems = refs[26:]
        waits = load_weights(
            core, layer, [(w[4], w[5], held_down, 1), (w[2], w[3], held_up, 1), (w[0], w[1], held_out, 1)], sems
        )
        params_ref[...] = jnp.where(core == layer, own_p[...], other_p[...])
        ffn_backward(
            grad_ref, att, rden, qf, hat1, scale1, gprime, hat2, scale2, params_ref,
            held_out, held_up, held_down, waits, out_refs, tmp, tmp_up,
        )

    return call(
        kernel,
        (grad, *kept, *params, *weights),
        [VMEM_SPEC] * 11 + [HBM_SPEC] * 6,
        outs,
        ffn_scratch(rows),
        f"ffn_backward_{layer}",
        5,
        20,
    )


def run_ffn_grads(layer, normed, hidden, d_ffn, d_up):
    return call(
        ffn_weight_grads,
        (normed, hidden, d_ffn, d_up),
        [VMEM_SPEC] * 4,
        [shape(4 * D, D, BF)] * 2,
        [],
        f"ffn_grads_{layer}",
        4,
    )


def run_near_backward(layer, spq, spk, vv, r_low, t_high, t_low, mask, mask_t):
    def kernel(*refs):
        near_backward(*refs[:8], refs[8:])

    return call(
        kernel,
        (spq, spk, vv, r_low, t_high, t_low, mask, mask_t),
        [VMEM_SPEC] * 8,
        [shape(spq.shape[0], D, F32)] * 3,
        [],
        f"near_backward_{layer}",
        4,
    )


def run_attention_backward(layer, x, kept, near, recvs, fixed, rest, w_own, w_other):
    rows = x.shape[0]
    count = len(recvs)

    def kernel(*refs):
        x_ref, vv, sigq, sigk, kf, r_low, t_high, t_low, prefix = refs[:9]
        near_refs = refs[9:12]
        recv_refs = refs[12 : 12 + count]
        cosb, sinb, d_pre_one, mixed, d_branch, smalls, own, other = refs[12 + count : 20 + count]
        d_in, grads_kept, grads_sent, held, d_qkv, sems = refs[20 + count :]
        (wait,) = load_weights(lax.axis_index("section"), layer, [(own, other, held, 1)], sems)
        attention_backward(
            x_ref, vv, sigq, sigk, kf, r_low, t_high, t_low, prefix, near_refs, recv_refs, cosb, sinb,
            d_pre_one, mixed, d_branch, smalls, held, wait, (d_in, grads_kept, grads_sent), d_qkv,
        )

    return call(
        kernel,
        (x, *kept, *near, *recvs, *fixed, *rest, w_own, w_other),
        [VMEM_SPEC] * (18 + count) + [HBM_SPEC] * 2,
        [shape(rows, D, BF)] + [shape(2 * D + SMALL, D, BF)] * 2,
        [pltpu.VMEM((D, 3 * D), BF), pltpu.VMEM((rows, 3 * D), BF), pltpu.SemaphoreType.DMA((1,))],
        f"attention_backward_{layer}",
        5,
        20,
    )


def combine(kept, received, tail, last, name):
    rows = kept.shape[0] - (SMALL if tail else 0)
    next_rows = rows if last else rows // 2
    count = 1 if last else 2

    def kernel(kept_ref, received_ref, *outs):
        for i, out in enumerate(outs):
            s = slice(i * next_rows, (i + 1) * next_rows)
            out[:next_rows, :] = (kept_ref[s, :].astype(F32) + received_ref[s, :].astype(F32)).astype(BF)
            if tail:
                put_smalls(out, next_rows, get_smalls(kept_ref, rows) + get_smalls(received_ref, rows))

    out_rows = next_rows + (SMALL if tail else 0)
    return call(
        kernel,
        (kept, received),
        [VMEM_SPEC] * 2,
        [shape(out_rows, kept.shape[1], BF)] * count,
        [],
        name,
        1,
    )


def join(a, b, name):
    def kernel(a_ref, b_ref, out):
        out[: a.shape[0], :] = a_ref[...]
        out[a.shape[0] :, :] = b_ref[...]

    return call(kernel, (a, b), [VMEM_SPEC] * 2, [shape(a.shape[0] + b.shape[0], D, BF)], [], name, 1)[0]


def split_sums(joined, received, ffn_rows, other_rows, name):
    def kernel(joined_ref, received_ref, ffn, other, smalls):
        for out, start, rows in ((ffn, 0, ffn_rows), (other, ffn_rows, other_rows)):
            s = slice(start, start + rows)
            out[...] = (joined_ref[s, :].astype(F32) + received_ref[s, :].astype(F32)).astype(BF)
        start = ffn_rows + other_rows
        smalls[...] = get_smalls(joined_ref, start) + get_smalls(received_ref, start)

    return call(
        kernel,
        (joined, received),
        [VMEM_SPEC] * 2,
        [shape(ffn_rows, D, BF), shape(other_rows, D, BF), shape(16, D, F32)],
        [],
        name,
        1,
    )


def unpack(part, sources, name):
    total = sources[0].shape[0]
    size = chunk_rows(total)
    rows = D if part == 0 else D // 2

    def copy_piece(source, number, first_row, out, cols):
        for i in range(rows // size):
            spot = pl.multiple_of(jnp.bitwise_xor(first_row // size + i, number) * size, size)
            out[i * size : (i + 1) * size, cols] = source[pl.ds(spot, size), :].astype(F32)

    def kernel(own0, other0, own1, other1, *outs):
        step = pl.program_id(0)
        core = lax.axis_index("section")
        _, ids = part_ids(part)

        def piece(half, first_row, out, cols=slice(0, D)):
            for layer, source_half, source in ((0, 0, own0), (0, 1, other0), (1, 1, own1), (1, 0, other1)):

                @pl.when((core == layer) & (half == source_half))
                def _(source=source, source_half=source_half):
                    copy_piece(source, ids[source_half], first_row, out, cols)

        if part == 0:

            @pl.when(step < 4)
            def _():
                piece(lax.div(step, 2), lax.rem(step, 2) * D, outs[0])

            @pl.when(step >= 4)
            def _():
                piece(lax.div(step - 4, 2), (2 + lax.rem(step, 2)) * D, outs[1])

        else:
            for j in range(3):
                piece(step, jnp.int32(j * rows), outs[0], slice(j * D, (j + 1) * D))
            piece(step, jnp.int32(3 * rows), outs[1])

    if part == 0:
        out_shape = (shape(D, FF, F32), shape(FF, D, F32))
        out_specs = (
            pl.BlockSpec((D, D), lambda i: (0, jnp.minimum(i, 3))),
            pl.BlockSpec((D, D), lambda i: (jnp.maximum(i - 4, 0), 0)),
        )
        grid = (8,)
    else:
        out_shape = (shape(D, 3 * D, F32), shape(D, D, F32))
        out_specs = (pl.BlockSpec((rows, 3 * D), lambda i: (i, 0)), pl.BlockSpec((rows, D), lambda i: (i, 0)))
        grid = (2,)
    return pl.pallas_call(
        kernel,
        out_shape=out_shape,
        grid=grid,
        in_specs=[VMEM_SPEC] * 4,
        out_specs=out_specs,
        compiler_params=pltpu.CompilerParams(vmem_limit_bytes=24 * MIB),
        cost_estimate=pl.CostEstimate(flops=int(4 * 1.1e9), bytes_accessed=1 << 20, transcendentals=0),
        name=name,
    )(*sources)


def swap_cores(block):
    return lax.ppermute(block, "section", [(0, 1), (1, 0)])


def from_others(message):
    length = lax.axis_size("seq") // 2
    mine = []
    for distance in range(1, length):
        route = [(base + j, base + (j + distance) % length) for base in (0, length) for j in range(length)]
        mine.append(lax.ppermute(message, "seq", route))
    return mine + [swap_cores(message)] + [swap_cores(m) for m in mine]


def halves_route(cores):
    length = lax.axis_size("seq") // 2
    route = []
    for j in range(length):
        route.append((2 * (j + length) + cores[0][0], 2 * j + cores[0][1]))
        route.append((2 * j + cores[1][0], 2 * (j + length) + cores[1][1]))
    return route


def take_rows(whole):
    core, lower, _, _ = place()
    sent = jnp.where(lower, whole[1], whole[0])
    received = lax.ppermute(sent, ("seq", "section"), halves_route(((1, 1), (0, 0))))
    local = jnp.where(lower, whole[0], whole[1])
    return jnp.where((core == 0) == lower, local, received)


def give_rows(first, second):
    core, lower, _, _ = place()
    rows = first.shape[0]
    both = jnp.concatenate([first, second], axis=0)
    far = lax.ppermute(both, ("seq", "section"), halves_route(((0, 0), (1, 0))))
    far_second = lax.ppermute(far[rows:], "section", [(0, 1)])
    hop = swap_cores(jnp.where(lower, second, first))
    local = jnp.where(core == 0, jnp.where(lower, first, hop), jnp.where(lower, hop, second))
    remote = jnp.where(core == 0, far[:rows], far_second)
    return jnp.stack([jnp.where(lower, local, remote), jnp.where(lower, remote, local)])[None]


def exchange(block, part, step):
    routes = []
    dp, seq = lax.axis_size("dp"), lax.axis_size("seq")
    for core, order in enumerate(orders_of(part)):
        axis, i = order[step]
        for a in range(dp):
            for b in range(seq):
                to = (a ^ (1 << i), b) if axis == "dp" else (a, b ^ (1 << i))
                routes.append(((a * seq + b) * 2 + core, (to[0] * seq + to[1]) * 2 + core))
    return lax.ppermute(block, ("dp", "seq", "section"), routes)


def exchange_last(block):
    _, (axis, i) = partner_bits()
    return lax.ppermute(block, axis, [(j, j ^ (1 << i)) for j in range(lax.axis_size(axis))])


def sum_gradients(layer, ffn, other):
    steps = len(partner_bits()[0])
    parts = []
    for part, (kept, sent) in enumerate((ffn, other)):
        kept, sent = combine(kept, swap_cores(sent), part == 1, False, f"add_{layer}_{part}")
        parts.append((kept, sent))
    for step in range(steps):
        last = step == steps - 1
        results = []
        for part, (kept, sent) in enumerate(parts):
            received = exchange(sent, part, step)
            results.append(combine(kept, received, part == 1, last, f"add_{layer}_{part}_{step}"))
        parts = results
    joined = join(parts[0][0], parts[1][0], f"join_{layer}")
    ffn_rows, other_rows = parts[0][0].shape[0], parts[1][0].shape[0] - SMALL
    ffn_sum, other_sum, smalls = split_sums(joined, exchange_last(joined), ffn_rows, other_rows, f"split_{layer}")
    sums = [ffn_sum, other_sum]
    for step in reversed(range(steps)):
        sums = [join(s, exchange(s, part, step), f"join_{layer}_{part}_{step}") for part, s in enumerate(sums)]
    return sums, smalls


def body(tokens, cotangent, w_qkv, w_out, first_norm_gain, ln1_bias, w_up, b_up, w_down, b_down, ln2_gain, ln2_bias):
    core, _, j, length = place()
    rows = tokens.shape[1]
    whole = rows * lax.axis_size("seq")
    step = math.pi / (2.0 * whole)
    x = take_rows(tokens)
    own_qkv = w_qkv[0]
    other_qkv = swap_cores(own_qkv)
    own_p = jnp.concatenate(
        [first_norm_gain, ln1_bias, b_down, ln2_gain, ln2_bias, b_up.reshape(4, D), jnp.zeros((7, D), F32)], axis=0
    )
    later_w = lax.optimization_barrier((w_out[0], w_up[0], w_down[0], own_p, cotangent, other_qkv))
    own_w, own_p, cotangent, other_qkv = later_w[:3], later_w[3], later_w[4], later_w[5]
    other_w = tuple(swap_cores(w) for w in own_w)
    params = (own_p, swap_cores(own_p))
    qkv_w = (own_qkv, other_qkv)
    rest_w = (own_w[0], other_w[0], own_w[1], other_w[1], own_w[2], other_w[2])
    cot = take_rows(cotangent)

    places = jnp.arange(rows, dtype=jnp.int32)
    angles = ((j + core * length) * rows + places).astype(F32) * step
    cosb = jnp.broadcast_to(jnp.cos(angles)[:, None], (rows, 128))
    sinb = jnp.broadcast_to(jnp.sin(angles)[:, None], (rows, 128))
    apart = places[:, None] - places[None, :]
    near = jnp.cos(apart.astype(F32) * step)
    mask = jnp.where(apart >= 0, near, 0.0)
    mask_t = jnp.where(apart <= 0, near, 0.0)

    saved = []
    for layer in range(2):
        projected = run_project(layer, x, *qkv_w, cosb, sinb)
        spq, spk, vv, sigq, sigk, qf, kf, msg = projected
        recvs = from_others(msg)
        near_sums = run_near(layer, spq, spk, vv, mask)
        forward = run_forward(layer, x, near_sums, qf, recvs, params, rest_w)
        saved.append((x, projected, forward))
        x = forward[-1]
    layer_outputs = give_rows(saved[0][2][-1], saved[1][2][-1])

    grad = cot
    d_inputs, sums, smalls = [None, None], [None, None], [None, None]
    for layer in (1, 0):
        x, (spq, spk, vv, sigq, sigk, qf, kf, _), forward = saved[layer]
        att, rden, mixed, hat1, scale1, normed, hidden, gprime, hat2, scale2, prefix, _ = forward
        d_ffn, d_up, d_branch, d_pre_one, r_low, t_high, t_low, small, msg = run_ffn_backward(
            layer, grad, (att, rden, qf, hat1, scale1, gprime, hat2, scale2), params, rest_w
        )
        recvs = from_others(msg)
        ffn = run_ffn_grads(layer, normed, hidden, d_ffn, d_up)
        near_grads = run_near_backward(layer, spq, spk, vv, r_low, t_high, t_low, mask, mask_t)
        grad, kept, sent = run_attention_backward(
            layer, x, (vv, sigq, sigk, kf, r_low, t_high, t_low, prefix), near_grads, recvs, (cosb, sinb),
            (d_pre_one, mixed, d_branch, small), *qkv_w,
        )
        d_inputs[layer] = grad
        sums[layer], smalls[layer] = sum_gradients(layer, ffn, (kept, sent))
    input_grads = give_rows(d_inputs[0], d_inputs[1])

    arrays = []
    for part in range(2):
        zero, one = sums[0][part], sums[1][part]
        sources = (
            zero, lax.ppermute(zero, "section", [(1, 0)]), one, lax.ppermute(one, "section", [(0, 1)])
        )
        arrays.append(unpack(part, sources, f"unpack_{part}"))
    (grad_up, grad_down), (grad_qkv, grad_out) = arrays
    small = jnp.where(core == 0, smalls[0], smalls[1])
    d_gain1, d_bias1, d_b_down, d_gain2, d_bias2 = (small[i : i + 1] for i in range(5))
    d_b_up = small[5:9].reshape(1, FF)
    return (
        layer_outputs,
        input_grads,
        grad_qkv[None],
        grad_out[None],
        d_gain1,
        d_bias1,
        grad_up[None],
        d_b_up,
        grad_down[None],
        d_b_down,
        d_gain2,
        d_bias2,
    )


def solution(mesh):
    rows = P("dp", "seq", None)
    matrix = P("section", None, None)
    vector = P("section", None)
    out_rows = P("section", "dp", "seq", None)
    return jax.shard_map(
        body,
        mesh=mesh,
        in_specs=(rows, rows, matrix, matrix, vector, vector, matrix, vector, matrix, vector, vector, vector),
        out_specs=(
            out_rows, out_rows, matrix, matrix, vector, vector, matrix, vector, matrix, vector, vector, vector,
        ),
        check_vma=False,
    )
```

```python
import functools
import math

import jax
import jax.numpy as jnp
from jax import lax
from jax.experimental import pallas as pl
from jax.experimental.pallas import tpu as pltpu
from jax.sharding import PartitionSpec as P

D = 512
HEADS = 8
HEAD_DIM = 64
FF = 2048
PAIRS = HEADS // 2
EPS = 1e-05
BF = jnp.bfloat16
F32 = jnp.float32
MIB = 1024 * 1024
FLOPS = 1 << 20


def dot(a, b):
    return lax.dot_general(a, b, (((1,), (0,)), ((), ())), preferred_element_type=F32)


def dot_nt(a, b):
    return lax.dot_general(a, b, (((1,), (1,)), ((), ())), preferred_element_type=F32)


def dot_tn(a, b):
    return lax.dot_general(a, b, (((0,), (0,)), ((), ())), preferred_element_type=F32)


def low_half(rows, lanes):
    place = lax.broadcasted_iota(jnp.int32, (rows, lanes), 1)
    return lax.rem(place, 128) < HEAD_DIM


def block_diag(pair):
    rows, lanes = pair.shape
    low = low_half(rows, lanes)
    zero = jnp.zeros_like(pair)
    return jnp.concatenate([jnp.where(low, pair, zero), jnp.where(low, zero, pair)], axis=0)


def pair_cols(ref, g, width=128):
    return ref[:, g * width : (g + 1) * width]


def value_block(v_pair):
    ones = jnp.ones_like(v_pair)
    return jnp.concatenate([block_diag(v_pair), block_diag(ones)], axis=1)


def pack_message(blocks, keys):
    places = lax.broadcasted_iota(jnp.int32, (16, 256), 0)
    tail = jnp.zeros((16, 256), F32)
    for g in range(PAIRS):
        tail = jnp.where(places == g, jnp.broadcast_to(keys[g], (16, 256)), tail)
    return jnp.concatenate(list(blocks) + [tail], axis=0).astype(BF)


def place():
    length = lax.axis_size("seq") // 2
    z = lax.axis_index("seq")
    lower = z < length
    return lax.axis_index("section"), lower, jnp.where(lower, z, z - length), length


def sum_messages(refs, backward):
    core, _, j, length = place()
    total = jnp.zeros(refs[0].shape, F32)
    for i, ref in enumerate(refs):
        distance = i + 1
        if distance < length:
            wanted = j < distance if backward else j >= distance
        else:
            wanted = core == (0 if backward else 1)
        total = total + jnp.where(wanted, ref[...].astype(F32), 0.0)
    return total


CHUNK = 32


def each_rows(rows, fn, carry=None, unroll=False):
    if unroll:
        for r in range(0, rows, CHUNK):
            carry = fn(slice(r, r + CHUNK), carry)
        return carry

    def one(i, carry):
        return fn(pl.ds(pl.multiple_of(i * CHUNK, CHUNK), CHUNK), carry)

    return lax.fori_loop(0, rows // CHUNK, one, carry)


def row_mean(values):
    return jnp.sum(values, axis=-1, keepdims=True) * (1.0 / values.shape[-1])


def project(x, w_ref, waits, cosb, sinb, outs, tmp):
    spq, spk, vv, sigq, sigk, qf, kf, msg = outs
    rows = x.shape[0]

    def softplus_part(part, sp_ref, sig_ref, f_ref):
        waits[part]()
        tmp[...] = dot(x, w_ref[:, part * D : (part + 1) * D])

        def soften(s, _):
            raw = tmp[s, :]
            tail = jnp.exp(-jnp.abs(raw))
            soft = jnp.maximum(raw, 0.0) + jnp.log1p(tail)
            sig = jnp.where(raw >= 0.0, 1.0, tail) / (1.0 + tail)
            sp_ref[s, :] = soft.astype(BF)
            sig_ref[s, :] = sig
            cos_rows = cosb[s, :]
            sin_rows = sinb[s, :]
            for g in range(PAIRS):
                pair = soft[:, 128 * g : 128 * (g + 1)]
                f_ref[s, 256 * g : 256 * g + 128] = (pair * cos_rows).astype(BF)
                f_ref[s, 256 * g + 128 : 256 * (g + 1)] = (pair * sin_rows).astype(BF)

        each_rows(rows, soften)

    softplus_part(1, spk, sigk, kf)
    waits[2]()
    vv[...] = dot(x, w_ref[:, 2 * D : 3 * D]).astype(BF)
    softplus_part(0, spq, sigq, qf)
    low = low_half(64, 256)
    blocks, keys = [], []
    for g in range(PAIRS):
        kf_g = pair_cols(kf, g, 256)
        full = dot_tn(pair_cols(vv, g), kf_g)
        blocks.append(jnp.where(low, full[:64], full[64:]))
        keys.append(jnp.sum(kf_g.astype(F32), axis=0, keepdims=True))
    msg[...] = pack_message(blocks, keys)


def state_block(total, g):
    low = low_half(64, 256)
    block = total[64 * g : 64 * (g + 1), :]
    keys = jnp.broadcast_to(total[256 + g : 257 + g, :], (64, 256))
    zero = jnp.zeros((64, 256), F32)
    return jnp.concatenate(
        [
            jnp.where(low, block, zero),
            jnp.where(low, zero, block),
            jnp.where(low, keys, zero),
            jnp.where(low, zero, keys),
        ],
        axis=0,
    ).astype(BF)


def norm_forward(tmp, gain, bias, hat_ref, scale_ref, out_fn):

    def norm(s, _):
        values = tmp[s, :]
        centered = values - row_mean(values)
        scale = lax.rsqrt(row_mean(centered * centered) + EPS)
        hat = centered * scale
        hat_ref[s, :] = hat
        scale_ref[s, :] = jnp.broadcast_to(scale, (32, 128))
        out_fn(s, hat * gain + bias)

    each_rows(tmp.shape[0], norm, unroll=True)


def near_attention(spq, spk, vv, mask, near):
    mask2 = jnp.concatenate([mask[...], mask[...]], axis=1)
    for g in range(PAIRS):
        scores = dot_nt(pair_cols(spq, g), block_diag(pair_cols(spk, g))) * mask2
        near[:, 256 * g : 256 * (g + 1)] = dot(scores.astype(BF), value_block(pair_cols(vv, g)))


def attend_and_ffn(x, near, qf, recvs, params, w_out, w_up, w_down, waits, outs, tmp, tmp_up):
    att, rden, mixed, hat1, scale1, normed, hidden, gprime, hat2, scale2, prefix, result = outs
    rows = x.shape[0]
    total = sum_messages(recvs, False)
    prefix[...] = total
    for g in range(PAIRS):
        both = pair_cols(near, g, 256) + dot_nt(pair_cols(qf, g, 256), state_block(total, g))
        inverse = 1.0 / both[:, 128:]
        attended = both[:, :128] * inverse
        cols = slice(128 * g, 128 * (g + 1))
        att[:, cols] = attended
        rden[:, cols] = inverse
        mixed[:, cols] = attended.astype(BF)
    gain1, bias1, b_down, gain2, bias2 = (params[i : i + 1, :] for i in range(5))
    waits[0]()
    tmp[...] = x[...].astype(F32) + dot(mixed[...], w_out[...])

    def put_normed(s, value):
        normed[s, :] = value.astype(BF)
        tmp[s, :] = value

    norm_forward(tmp, gain1, bias1, hat1, scale1, put_normed)
    waits[1]()
    for c in range(FF // D):
        cols = slice(c * D, (c + 1) * D)
        tmp_up[...] = dot(normed[...], w_up[:, cols])
        b_up = params[5 + c : 6 + c, :]

        def activate(s, _, cols=cols, b_up=b_up):
            up = tmp_up[s, :] + b_up
            cdf = 0.5 + 0.5 * lax.erf(up * (1.0 / math.sqrt(2.0)))
            density = jnp.exp(-0.5 * up * up) * (1.0 / math.sqrt(2.0 * math.pi))
            hidden[s, cols] = (up * cdf).astype(BF)
            gprime[s, cols] = (cdf + up * density).astype(BF)

        each_rows(rows, activate, unroll=True)
    waits[2]()
    tmp[...] = tmp[...] + b_down + dot(hidden[...], w_down[...])

    def put_result(s, value):
        result[s, :] = value.astype(BF)

    norm_forward(tmp, gain2, bias2, hat2, scale2, put_result)


def column_sum(values):
    return jnp.sum(values, axis=0, keepdims=True)


def norm_backward(grad_fn, gain, hat_ref, scale_ref, rows, put, extras=0):
    def norm(s, sums):
        grad = grad_fn(s)
        hat = hat_ref[s, :]
        scaled = grad * gain
        first = row_mean(scaled)
        second = row_mean(scaled * hat)
        scale = scale_ref[s, :][:, :1]
        extra = put(s, (scaled - first - hat * second) * scale)
        new = (column_sum(grad * hat), column_sum(grad)) + extra
        return tuple(a + b for a, b in zip(sums, new))

    zero = jnp.zeros((1, D), F32)
    return each_rows(rows, norm, (zero,) * (2 + extras), True)


def ffn_backward(grad, att, rden, qf, hat1, scale1, gprime, hat2, scale2, params, w_out, w_up, w_down, waits, outs, tmp, tmp_up):
    d_ffn, d_up, d_branch, d_pre_one, r_low, t_high, t_low, smalls, msg = outs
    rows = att.shape[0]
    gain1, gain2 = params[0:1, :], params[3:4, :]

    def put_two(s, value):
        rounded = value.astype(BF)
        tmp[s, :] = value
        d_ffn[s, :] = rounded
        return (column_sum(rounded.astype(F32)),)

    d_gain2, d_bias2, d_b_down = norm_backward(
        lambda s: grad[s, :].astype(F32), gain2, hat2, scale2, rows, put_two, 1
    )
    waits[0]()
    b_up = []
    for c in range(FF // D):
        cols = slice(c * D, (c + 1) * D)
        tmp_up[...] = dot_nt(d_ffn[...], w_down[cols, :])

        def scale_up(s, total, cols=cols):
            value = (tmp_up[s, :] * gprime[s, cols].astype(F32)).astype(BF)
            d_up[s, cols] = value
            return total + column_sum(value.astype(F32))

        b_up.append(each_rows(rows, scale_up, jnp.zeros((1, D), F32), True))
    waits[1]()
    tmp[...] = tmp[...] + dot_nt(d_up[...], w_up[...])

    def put_one(s, value):
        d_pre_one[s, :] = value
        d_branch[s, :] = value.astype(BF)
        return ()

    d_gain1, d_bias1 = norm_backward(lambda s: tmp[s, :], gain1, hat1, scale1, rows, put_one)
    waits[2]()
    tmp[...] = dot_nt(d_branch[...], w_out[...])

    def scores(s, _):
        rounded = (tmp[s, :] * rden[s, :]).astype(BF)
        product = -(rounded.astype(F32) * att[s, :])
        high = product.astype(BF)
        r_low[s, :] = rounded
        t_high[s, :] = high
        t_low[s, :] = (product - high.astype(F32)).astype(BF)

    each_rows(rows, scores, unroll=True)
    low = low_half(64, 256)
    blocks, keys = [], []
    for g in range(PAIRS):
        sides = jnp.concatenate([pair_cols(r_low, g), pair_cols(t_high, g)], axis=1)
        full = dot_tn(sides, pair_cols(qf, g, 256))
        blocks.append(jnp.where(low, full[:64], full[64:128]))
        keys.append(column_sum(jnp.where(low, full[128:192], full[192:])))
    msg[...] = pack_message(blocks, keys)
    smalls[...] = jnp.concatenate(
        [d_gain1, d_bias1, d_b_down, d_gain2, d_bias2] + b_up + [jnp.zeros((7, D), F32)], axis=0
    )


def near_backward(spq, spk, vv, r_low, t_high, t_low, mask, mask_t, outs):
    near_q, near_k, near_v = outs
    mask2 = jnp.concatenate([mask[...], mask[...]], axis=1)
    mask_t2 = jnp.concatenate([mask_t[...], mask_t[...]], axis=1)
    for g in range(PAIRS):
        spq_g, spk_g, vv_g = pair_cols(spq, g), pair_cols(spk, g), pair_cols(vv, g)
        r_g, th_g, tl_g = pair_cols(r_low, g), pair_cols(t_high, g), pair_cols(t_low, g)
        values = value_block(vv_g)
        spk_diag, spq_diag, r_diag = block_diag(spk_g), block_diag(spq_g), block_diag(r_g)
        cols = slice(128 * g, 128 * (g + 1))
        d_scores = dot_nt(jnp.concatenate([r_g, th_g], axis=1), values) + dot_nt(tl_g, values[:, 128:])
        near_q[:, cols] = dot((d_scores * mask2).astype(BF), spk_diag)
        scores_t = (dot_nt(spk_g, spq_diag) * mask_t2).astype(BF)
        near_v[:, cols] = dot(scores_t, r_diag)
        d_scores_t = dot_nt(
            jnp.concatenate([vv_g, jnp.ones_like(vv_g)], axis=1),
            jnp.concatenate([r_diag, block_diag(th_g)], axis=1),
        )
        near_k[:, cols] = dot((d_scores_t * mask_t2).astype(BF), spq_diag)


def attention_backward(
    layer, x, vv, sigq, sigk, kf, r_low, t_high, t_low, prefix, near, recvs, cosb, sinb,
    d_pre_one, mixed, d_branch, smalls, w_qkv, wait, outs, d_qkv,
):
    d_in, kept, sent = outs
    near_q, near_k, near_v = near
    total = sum_messages(recvs, True)
    low = low_half(64, 256)
    for g in range(PAIRS):
        cols = slice(128 * g, 128 * (g + 1))
        vv_g = pair_cols(vv, g)
        sides = jnp.concatenate([pair_cols(r_low, g), pair_cols(t_high, g)], axis=1)
        state = state_block(prefix[...], g)
        d_feat = dot(sides, state) + dot(pair_cols(t_low, g), state[128:, :])
        d_soft_q = near_q[:, cols] + cosb[...] * d_feat[:, :128] + sinb[...] * d_feat[:, 128:]
        block = total[64 * g : 64 * (g + 1), :]
        zero = jnp.zeros_like(block)
        later = jnp.concatenate([jnp.where(low, block, zero), jnp.where(low, zero, block)], axis=0).astype(BF)
        d_value = near_v[:, cols] + dot_nt(pair_cols(kf, g, 256), later)
        d_feat_k = dot(vv_g, later) + total[256 + g : 257 + g, :]
        d_soft_k = near_k[:, cols] + cosb[...] * d_feat_k[:, :128] + sinb[...] * d_feat_k[:, 128:]
        d_qkv[:, 128 * g : 128 * (g + 1)] = (pair_cols(sigq, g) * d_soft_q).astype(BF)
        d_qkv[:, D + 128 * g : D + 128 * (g + 1)] = (pair_cols(sigk, g) * d_soft_k).astype(BF)
        d_qkv[:, 2 * D + 128 * g : 2 * D + 128 * (g + 1)] = d_value.astype(BF)
    wait()
    d_in[...] = (d_pre_one[...] + dot_nt(d_qkv[...], w_qkv[...])).astype(BF)
    core = lax.axis_index("section")
    ids = part_ids(1)
    half_rows = D // 2
    for out, half in ((kept, core), (sent, 1 - core)):
        order = jnp.where(half == 0, ids[0], ids[1])
        start = pl.multiple_of(half * half_rows, half_rows)
        x_half = x[:, pl.ds(start, half_rows)]
        for j in range(3):
            store_chunks(out, j * half_rows, dot_tn(x_half, d_qkv[:, j * D : (j + 1) * D]).astype(BF), order, 4 * half_rows)
        value = dot_tn(mixed[:, pl.ds(start, half_rows)], d_branch[...]).astype(BF)
        store_chunks(out, 3 * half_rows, value, order, 4 * half_rows)
        put_smalls(out, 4 * half_rows, smalls[...])


def ffn_weight_grads(layer, normed, hidden, d_ffn, d_up, kept, sent):
    core = lax.axis_index("section")
    ids = part_ids(0)
    for out, half in ((kept, core), (sent, 1 - core)):
        order = jnp.where(half == 0, ids[0], ids[1])
        for j in range(2):
            start = pl.multiple_of(half * (FF // 2) + j * D, D)
            store_chunks(out, j * D, dot_tn(normed[...], d_up[:, pl.ds(start, D)]).astype(BF), order, 4 * D)
            value = dot_tn(hidden[:, pl.ds(start, D)], d_ffn[...]).astype(BF)
            store_chunks(out, (2 + j) * D, value, order, 4 * D)


def partner_bits():
    bits = [(axis, i) for axis in ("dp", "seq") for i in range(lax.axis_size(axis).bit_length() - 1)]
    last = bits.pop()
    return bits, last


def turned(bits, places):
    return bits[places:] + bits[:places]


def orders_of(part):
    bits, _ = partner_bits()
    third = max(1, len(bits) // 3)
    a, b, c = bits[:third], bits[third : 2 * third], bits[2 * third :]
    return [a + b + c, b + a + c] if part == 0 else [b + c + a, a + c + b]


def part_ids(part):
    ids = []
    for order in orders_of(part):
        number = jnp.int32(0)
        for axis, i in order:
            number = 2 * number + lax.rem(lax.div(lax.axis_index(axis), 1 << i), 2)
        ids.append(number)
    return ids


def chunk_rows(total):
    bits, _ = partner_bits()
    return total >> len(bits)


def store_chunks(out, first_row, value, number, total):
    size = chunk_rows(total)
    for i in range(value.shape[0] // size):
        chunk = first_row // size + i
        spot = pl.multiple_of(jnp.bitwise_xor(jnp.int32(chunk), number) * size, size)
        out[pl.ds(spot, size), :] = value[i * size : (i + 1) * size, :]


SMALL = 32


def put_smalls(out, start, value):
    high = value.astype(BF)
    out[start : start + 16, :] = high
    out[start + 16 : start + SMALL, :] = (value - high.astype(F32)).astype(BF)


def get_smalls(ref, start):
    return ref[start : start + 16, :].astype(F32) + ref[start + 16 : start + SMALL, :].astype(F32)


def load_weights(core, layer, pairs, sems):
    waits = []
    for own, other, held, parts in pairs:
        width = held.shape[1] // parts
        for p in range(parts):
            i = len(waits)
            cols = slice(p * width, (p + 1) * width)

            @pl.when(core == layer)
            def _(own=own, held=held, i=i, cols=cols):
                pltpu.make_async_copy(own.at[:, cols], held.at[:, cols], sems.at[i]).start()

            @pl.when(core != layer)
            def _(other=other, held=held, i=i, cols=cols):
                pltpu.make_async_copy(other.at[:, cols], held.at[:, cols], sems.at[i]).start()

            def wait(own=own, held=held, i=i, cols=cols):
                pltpu.make_async_copy(own.at[:, cols], held.at[:, cols], sems.at[i]).wait()

            waits.append(wait)
    return waits


def shape(rows, cols, kind):
    return jax.ShapeDtypeStruct((rows, cols), kind)


VMEM_SPEC = pl.BlockSpec(memory_space=pltpu.VMEM)
HBM_SPEC = pl.BlockSpec(memory_space=pltpu.HBM)
ANY_SPEC = pl.BlockSpec(memory_space=pl.ANY)


def call(kernel, args, specs, outs, scratch, name, micros, limit=16, pinned=False):
    if pinned:
        args = [pltpu.with_memory_space_constraint(a, pltpu.HBM) if s is HBM_SPEC else a for a, s in zip(args, specs)]
    return pl.pallas_call(
        kernel,
        out_shape=tuple(outs),
        in_specs=specs,
        out_specs=tuple(VMEM_SPEC for _ in outs),
        scratch_shapes=scratch,
        compiler_params=pltpu.CompilerParams(vmem_limit_bytes=limit * MIB),
        cost_estimate=pl.CostEstimate(flops=int(micros * FLOPS), bytes_accessed=1 << 10, transcendentals=0),
        name=name,
    )(*args)


def run_project(layer, x, w_own, w_other, cosb, sinb):
    rows = x.shape[0]
    outs = [shape(rows, D, BF)] * 3 + [shape(rows, D, F32)] * 2 + [shape(rows, 2 * D, BF)] * 2 + [shape(272, 256, BF)]

    def kernel(x_ref, own, other, cos_ref, sin_ref, *rest):
        out_refs, (held, tmp, sems) = rest[:8], rest[8:]
        waits = load_weights(lax.axis_index("section"), layer, [(own, other, held, 3)], sems)
        project(x_ref[...], held, waits, cos_ref, sin_ref, out_refs, tmp)

    return call(
        kernel,
        (x, w_own, w_other, cosb, sinb),
        [VMEM_SPEC, HBM_SPEC, HBM_SPEC, VMEM_SPEC, VMEM_SPEC],
        outs,
        [pltpu.VMEM((D, 3 * D), BF), pltpu.VMEM((rows, D), F32), pltpu.SemaphoreType.DMA((3,))],
        f"project_{layer}",
        3,
        pinned=layer == 0,
    )


def run_near(layer, spq, spk, vv, mask):
    return call(
        near_attention,
        (spq, spk, vv, mask),
        [VMEM_SPEC] * 4,
        [shape(spq.shape[0], 2 * D, F32)],
        [],
        f"near_{layer}",
        3,
    )[0]


def ffn_scratch(rows):
    return [
        pltpu.VMEM((D, D), BF),
        pltpu.VMEM((D, FF), BF),
        pltpu.VMEM((FF, D), BF),
        pltpu.VMEM((16, D), F32),
        pltpu.VMEM((rows, D), F32),
        pltpu.VMEM((rows, D), F32),
        pltpu.SemaphoreType.DMA((3,)),
    ]


def run_forward(layer, x, near, qf, recvs, params, weights):
    rows = x.shape[0]
    outs = (
        [shape(rows, D, F32)] * 2
        + [shape(rows, D, BF), shape(rows, D, F32), shape(rows, 128, F32), shape(rows, D, BF)]
        + [shape(rows, FF, BF)] * 2
        + [shape(rows, D, F32), shape(rows, 128, F32), shape(272, 256, F32), shape(rows, D, BF)]
    )
    count = len(recvs)

    def kernel(*refs):
        core = lax.axis_index("section")
        x_ref, near_ref, qf_ref, own_p, other_p = refs[:5]
        recv_refs = refs[5 : 5 + count]
        w = refs[5 + count : 11 + count]
        out_refs = refs[11 + count : 23 + count]
        held_out, held_up, held_down, params_ref, tmp, tmp_up, sems = refs[23 + count :]
        waits = load_weights(
            core, layer, [(w[0], w[1], held_out, 1), (w[2], w[3], held_up, 1), (w[4], w[5], held_down, 1)], sems
        )
        params_ref[...] = jnp.where(core == layer, own_p[...], other_p[...])
        attend_and_ffn(
            x_ref, near_ref, qf_ref, recv_refs, params_ref, held_out, held_up, held_down, waits, out_refs, tmp, tmp_up
        )

    return call(
        kernel,
        (x, near, qf, *params, *recvs, *weights),
        [VMEM_SPEC] * (5 + count) + [HBM_SPEC] * 6,
        outs,
        ffn_scratch(rows),
        f"forward_{layer}",
        5,
        20,
    )


def run_ffn_backward(layer, grad, kept, params, weights):
    rows = grad.shape[0]
    outs = (
        [shape(rows, D, BF), shape(rows, FF, BF), shape(rows, D, BF), shape(rows, D, F32)]
        + [shape(rows, D, BF)] * 3
        + [shape(16, D, F32), shape(272, 256, BF)]
    )

    def kernel(*refs):
        core = lax.axis_index("section")
        grad_ref, att, rden, qf, hat1, scale1, gprime, hat2, scale2, own_p, other_p = refs[:11]
        w = refs[11:17]
        out_refs = refs[17:26]
        held_out, held_up, held_down, params_ref, tmp, tmp_up, sems = refs[26:]
        waits = load_weights(
            core, layer, [(w[4], w[5], held_down, 1), (w[2], w[3], held_up, 1), (w[0], w[1], held_out, 1)], sems
        )
        params_ref[...] = jnp.where(core == layer, own_p[...], other_p[...])
        ffn_backward(
            grad_ref, att, rden, qf, hat1, scale1, gprime, hat2, scale2, params_ref,
            held_out, held_up, held_down, waits, out_refs, tmp, tmp_up,
        )

    return call(
        kernel,
        (grad, *kept, *params, *weights),
        [VMEM_SPEC] * 11 + [HBM_SPEC] * 6,
        outs,
        ffn_scratch(rows),
        f"ffn_backward_{layer}",
        5,
        20,
    )


def run_ffn_grads(layer, normed, hidden, d_ffn, d_up):
    return call(
        functools.partial(ffn_weight_grads, layer),
        (normed, hidden, d_ffn, d_up),
        [VMEM_SPEC] * 4,
        [shape(4 * D, D, BF)] * 2,
        [],
        f"ffn_grads_{layer}",
        4,
    )


def run_near_backward(layer, spq, spk, vv, r_low, t_high, t_low, mask, mask_t):
    def kernel(*refs):
        near_backward(*refs[:8], refs[8:])

    return call(
        kernel,
        (spq, spk, vv, r_low, t_high, t_low, mask, mask_t),
        [VMEM_SPEC] * 8,
        [shape(spq.shape[0], D, F32)] * 3,
        [],
        f"near_backward_{layer}",
        4,
    )


def run_attention_backward(layer, x, kept, near, recvs, fixed, rest, w_own, w_other):
    rows = x.shape[0]
    count = len(recvs)

    def kernel(*refs):
        x_ref, vv, sigq, sigk, kf, r_low, t_high, t_low, prefix = refs[:9]
        near_refs = refs[9:12]
        recv_refs = refs[12 : 12 + count]
        cosb, sinb, d_pre_one, mixed, d_branch, smalls, own, other = refs[12 + count : 20 + count]
        d_in, grads_kept, grads_sent, held, d_qkv, sems = refs[20 + count :]
        (wait,) = load_weights(lax.axis_index("section"), layer, [(own, other, held, 1)], sems)
        attention_backward(
            layer, x_ref, vv, sigq, sigk, kf, r_low, t_high, t_low, prefix, near_refs, recv_refs, cosb, sinb,
            d_pre_one, mixed, d_branch, smalls, held, wait, (d_in, grads_kept, grads_sent), d_qkv,
        )

    return call(
        kernel,
        (x, *kept, *near, *recvs, *fixed, *rest, w_own, w_other),
        [VMEM_SPEC] * (18 + count) + [HBM_SPEC] * 2,
        [shape(rows, D, BF)] + [shape(2 * D + SMALL, D, BF)] * 2,
        [pltpu.VMEM((D, 3 * D), BF), pltpu.VMEM((rows, 3 * D), BF), pltpu.SemaphoreType.DMA((1,))],
        f"attention_backward_{layer}",
        5,
        20,
    )


def combine(kept, received, tail, last, name):
    rows = kept.shape[0] - (SMALL if tail else 0)
    next_rows = rows if last else rows // 2
    count = 1 if last else 2

    def kernel(kept_ref, received_ref, *outs):
        for i, out in enumerate(outs):
            s = slice(i * next_rows, (i + 1) * next_rows)
            out[:next_rows, :] = (kept_ref[s, :].astype(F32) + received_ref[s, :].astype(F32)).astype(BF)
            if tail:
                put_smalls(out, next_rows, get_smalls(kept_ref, rows) + get_smalls(received_ref, rows))

    out_rows = next_rows + (SMALL if tail else 0)
    return call(
        kernel,
        (kept, received),
        [VMEM_SPEC] * 2,
        [shape(out_rows, kept.shape[1], BF)] * count,
        [],
        name,
        1,
    )


def join(a, b, name):
    def kernel(a_ref, b_ref, out):
        out[: a.shape[0], :] = a_ref[...]
        out[a.shape[0] :, :] = b_ref[...]

    return call(kernel, (a, b), [VMEM_SPEC] * 2, [shape(a.shape[0] + b.shape[0], D, BF)], [], name, 1)[0]


def split_sums(joined, received, ffn_rows, other_rows, name):
    def kernel(joined_ref, received_ref, ffn, other, smalls):
        for out, start, rows in ((ffn, 0, ffn_rows), (other, ffn_rows, other_rows)):
            s = slice(start, start + rows)
            out[...] = (joined_ref[s, :].astype(F32) + received_ref[s, :].astype(F32)).astype(BF)
        start = ffn_rows + other_rows
        smalls[...] = get_smalls(joined_ref, start) + get_smalls(received_ref, start)

    return call(
        kernel,
        (joined, received),
        [VMEM_SPEC] * 2,
        [shape(ffn_rows, D, BF), shape(other_rows, D, BF), shape(16, D, F32)],
        [],
        name,
        1,
    )


def by_core(zero, one, name):
    rows = [block.shape[0] for block in zero]

    def kernel(*refs):
        core = lax.axis_index("section")
        for out, wanted in ((refs[4], 0), (refs[5], 1)):
            for layer in range(2):

                @pl.when(core == (layer if wanted == 0 else 1 - layer))
                def _(out=out, layer=layer):
                    out[: rows[0], :] = refs[2 * layer][...]
                    out[rows[0] :, :] = refs[2 * layer + 1][...]

    return call(kernel, (*zero, *one), [VMEM_SPEC] * 4, [shape(sum(rows), D, BF)] * 2, [], name, 1)


def unpack(blocks, second, arrays, name):
    given = [b for b in blocks if b is not None]
    ffn_total, other_total = 4 * D, 2 * D
    sizes = (chunk_rows(ffn_total), chunk_rows(other_total))
    count = ffn_total // sizes[0] // 2
    out_shapes = [shape(D, FF, F32), shape(FF, D, F32), shape(D, 3 * D, F32), shape(D, D, F32)]

    def kernel(*refs):
        refs = list(refs)
        sources = [refs.pop(0) for _ in given]
        if arrays is not None:
            del refs[:4]
        up, down, qkv, out, held_ffn, held_other, sem_ffn, sem_other = refs
        core = lax.axis_index("section")
        slot = 0
        waits = []
        for block_place, block in enumerate(blocks):
            if block is None:
                continue
            source = sources.pop(0)
            half = core if block_place == 0 else 1 - core
            for part, size, held, sems in ((0, sizes[0], held_ffn, sem_ffn), (1, sizes[1], held_other, sem_other)):
                ids = part_ids(part)
                number = jnp.where(half == 0, ids[0], ids[1])
                base = 0 if part == 0 else ffn_total // 2
                for k in range(count):
                    index = slot * count + k
                    held[index] = source[base + k * size : base + (k + 1) * size, :].astype(F32)
                    chunk = jnp.bitwise_xor(k + (count if second else 0), number)
                    row = chunk * size
                    if part == 0:
                        piece, sub = lax.div(row, D), lax.rem(row, D)

                        @pl.when(piece < 2)
                        def _(piece=piece, sub=sub, index=index, half=half, held=held, sems=sems, size=size):
                            cols = pl.ds(pl.multiple_of((2 * half + piece) * D, D), D)
                            to = up.at[pl.ds(pl.multiple_of(sub, size), size), cols]
                            pltpu.make_async_copy(held.at[index], to, sems.at[index]).start()

                        @pl.when(piece >= 2)
                        def _(piece=piece, sub=sub, index=index, half=half, held=held, sems=sems, size=size):
                            start = pl.multiple_of((2 * half + piece - 2) * D + sub, size)
                            to = down.at[pl.ds(start, size), :]
                            pltpu.make_async_copy(held.at[index], to, sems.at[index]).start()

                        waits.append((held.at[index], down.at[pl.ds(0, size), :], sems.at[index]))
                    else:
                        piece, sub = lax.div(row, D // 2), lax.rem(row, D // 2)
                        start = pl.multiple_of(half * (D // 2) + sub, size)

                        @pl.when(piece < 3)
                        def _(piece=piece, start=start, index=index, held=held, sems=sems, size=size):
                            to = qkv.at[pl.ds(start, size), pl.ds(pl.multiple_of(piece * D, D), D)]
                            pltpu.make_async_copy(held.at[index], to, sems.at[index]).start()

                        @pl.when(piece == 3)
                        def _(start=start, index=index, held=held, sems=sems, size=size):
                            to = out.at[pl.ds(start, size), :]
                            pltpu.make_async_copy(held.at[index], to, sems.at[index]).start()

                        waits.append((held.at[index], out.at[pl.ds(0, size), :], sems.at[index]))
            slot += 1
        for wait in waits:
            pltpu.make_async_copy(*wait).wait()

    total = len(given) * count
    return pl.pallas_call(
        kernel,
        out_shape=tuple(out_shapes),
        in_specs=[VMEM_SPEC] * len(given) + ([ANY_SPEC] * 4 if arrays is not None else []),
        out_specs=(ANY_SPEC,) * 4,
        scratch_shapes=[
            pltpu.VMEM((total, sizes[0], D), F32),
            pltpu.VMEM((total, sizes[1], D), F32),
            pltpu.SemaphoreType.DMA((total,)),
            pltpu.SemaphoreType.DMA((total,)),
        ],
        input_output_aliases={} if arrays is None else {len(given) + k: k for k in range(4)},
        compiler_params=pltpu.CompilerParams(vmem_limit_bytes=24 * MIB),
        cost_estimate=pl.CostEstimate(flops=FLOPS, bytes_accessed=1 << 10, transcendentals=0),
        name=name,
    )(*given, *(arrays or ()))


def swap_cores(block):
    return lax.ppermute(block, "section", [(0, 1), (1, 0)])


def from_chips(message):
    length = lax.axis_size("seq") // 2
    received = []
    for distance in range(1, length):
        route = [(base + j, base + (j + distance) % length) for base in (0, length) for j in range(length)]
        received.append(lax.ppermute(message, "seq", route))
    return received


def from_cores(message, received):
    return received + [swap_cores(message)] + [swap_cores(m) for m in received]


def halves_route(cores):
    length = lax.axis_size("seq") // 2
    route = []
    for j in range(length):
        route.append((2 * (j + length) + cores[0][0], 2 * j + cores[0][1]))
        route.append((2 * j + cores[1][0], 2 * (j + length) + cores[1][1]))
    return route


def rows_to_send(whole):
    _, lower, _, _ = place()
    return lax.dynamic_index_in_dim(whole, jnp.where(lower, 1, 0), 0, False)


def swap_halves(block):
    return lax.ppermute(block, ("seq", "section"), halves_route(((1, 1), (0, 0))))


def rows_taken(whole, far):
    core, lower, _, _ = place()
    local = lax.dynamic_index_in_dim(whole, jnp.where(lower, 0, 1), 0, False)
    return jnp.where((core == 0) == lower, local, far)


def place_rows(firsts, seconds):
    count = len(firsts)
    rows, width = firsts[0].shape
    half = count * rows

    def stack(*refs):
        _, lower, _, _ = place()
        out, hop = refs[2 * count :]
        for k in range(2 * count):
            out[k * rows : (k + 1) * rows, :] = refs[k][...]
        for k in range(count):
            hop[k * rows : (k + 1) * rows, :] = jnp.where(lower, refs[count + k][...], refs[k][...])

    both, hop = call(
        stack, (*firsts, *seconds), [VMEM_SPEC] * 2 * count, [shape(2 * half, width, BF), shape(half, width, BF)],
        [], "stack_rows", 1,
    )
    far = lax.ppermute(both, ("seq", "section"), halves_route(((0, 0), (1, 0))))

    def finish(far):
        def kernel(both_ref, hop_ref, far_ref, far_second_ref, *outs):
            core, lower, _, _ = place()
            for k, out in enumerate(outs):
                s = slice(k * rows, (k + 1) * rows)
                own = jnp.where(core == 0, both_ref[s, :], both_ref[half + k * rows : half + (k + 1) * rows, :])
                local = jnp.where((core == 0) == lower, own, hop_ref[s, :])
                remote = jnp.where(core == 0, far_ref[s, :], far_second_ref[s, :])
                out[0, :, :] = jnp.where(lower, local, remote)
                out[1, :, :] = jnp.where(lower, remote, local)

        far_second = lax.ppermute(far[half:], "section", [(0, 1)])
        outs = [jax.ShapeDtypeStruct((2, rows, width), BF)] * count
        placed = call(kernel, (both, swap_cores(hop), far, far_second), [VMEM_SPEC] * 4, outs, [], "place_rows", 1)
        return [out[None] for out in placed]

    return far, finish


def exchange(block, layer, part, step):
    routes = []
    dp, seq = lax.axis_size("dp"), lax.axis_size("seq")
    for core, order in enumerate(orders_of(part)):
        axis, i = order[step]
        for a in range(dp):
            for b in range(seq):
                to = (a ^ (1 << i), b) if axis == "dp" else (a, b ^ (1 << i))
                routes.append(((a * seq + b) * 2 + core, (to[0] * seq + to[1]) * 2 + core))
    return lax.ppermute(block, ("dp", "seq", "section"), routes)


def exchange_last(block):
    _, (axis, i) = partner_bits()
    return lax.ppermute(block, axis, [(j, j ^ (1 << i)) for j in range(lax.axis_size(axis))])


def tie(*trees):
    return lax.optimization_barrier(trees)


class PartSum:
    def __init__(self, layer, part, kept, sent):
        self.name = f"{layer}_{part}"
        self.layer, self.part = layer, part
        self.kept, self.sent = kept, sent
        self.step = -1

    def send(self):
        self.received = swap_cores(self.sent) if self.step < 0 else exchange(self.sent, self.layer, self.part, self.step)

    def add(self):
        last = self.step == len(partner_bits()[0]) - 1
        result = combine(self.kept, self.received, self.part == 1, last, f"add_{self.name}_{self.step + 1}")
        self.kept, self.sent = result[0], result[-1]
        self.step += 1


EVENTS = (
    "F0.w", "C1.s0", "C0.w", "F1.s1", "C1.s1", "place", "C1.s2", "F1.s2", "F0.s0", "C0.s0", "Z1", "C0.s1", "F0.s1", "F1.a2", "C1.a2", "F0.s2",
    "C0.s2", "C1.a1", "F1.a1", "Z0", "C1.a0", "C0.a2", "F0.a2", "F0.a1", "F1.a0", "C0.a1", "C0.a0", "pre", "unpack", "F0.a0",
)


def default_events(steps):
    events = ["F0.w", "C0.w", "C1.s0"]
    for layer in (1, 0):
        for part in ("F", "C"):
            first = 1 if (part, layer) != ("F", 0) and (part, layer) != ("C", 0) else 0
            events += [f"{part}{layer}.s{step}" for step in range(first, steps)]
        events.append(f"Z{layer}")
    events.append("place")
    for step in reversed(range(steps)):
        if step == 0:
            events += ["pre", "unpack"]
        events += [f"{part}{layer}.a{step}" for layer in (1, 0) for part in ("F", "C")]
    return events


class Sums:
    def __init__(self, parts):
        self.parts = parts
        self.steps = len(partner_bits()[0])
        self.token = None
        self.extra, self.joined, self.far, self.smalls = {}, {}, {}, {}
        self.whole, self.received = {}, {}

    def after(self, received):
        if self.token is not None:
            received, self.token = tie(received, self.token)
        return received

    def of(self, layer):
        return self.whole[f"F{layer}"], self.whole[f"C{layer}"]

    def last(self, layer):
        return self.received[f"F{layer}"], self.received[f"C{layer}"]

    def gather(self, name, step):
        if step >= 0:
            self.received[name] = exchange(self.whole[name], int(name[1]), "FC".index(name[0]), step)

    def process(self, event):
        if event[0] == "Z":
            layer = int(event[1])
            pair = self.parts[f"F{layer}"], self.parts[f"C{layer}"]
            rows = pair[0].kept.shape[0], pair[1].kept.shape[0] - SMALL
            far = self.after(self.far[layer])
            ffn, other, self.smalls[layer] = split_sums(self.joined[layer], far, *rows, f"split_{layer}")
            self.token = self.smalls[layer]
            for name, block in ((f"C{layer}", other), (f"F{layer}", ffn)):
                self.whole[name] = block
                self.gather(name, self.steps - 1)
            return
        name, kind = event.split(".")
        layer = int(name[1])
        if kind[0] == "a":
            step = int(kind[1:])
            received = self.after(self.received[name])
            self.received[name] = received
            if step == 0:
                self.token = received
                return
            self.whole[name] = join(self.whole[name], received, f"join_{name}_{step}")
            self.token = self.whole[name]
            self.gather(name, step - 1)
            return
        part = self.parts[name]
        part.received = self.after(part.received)
        part.add()
        self.token = part.kept
        if part.step < self.steps:
            part.send()
        pair = self.parts[f"F{layer}"], self.parts[f"C{layer}"]
        if all(p.step == self.steps for p in pair):
            self.joined[layer] = join(pair[0].kept, pair[1].kept, f"join_{layer}")
            self.far[layer] = exchange_last(self.joined[layer])


def body(tokens, cotangent, w_qkv, w_out, first_norm_gain, ln1_bias, w_up, b_up, w_down, b_down, ln2_gain, ln2_bias):
    core, _, j, length = place()
    rows = tokens.shape[1]
    whole = rows * lax.axis_size("seq")
    step = math.pi / (2.0 * whole)
    sent = rows_to_send(tokens)
    sent, cotangent, w_qkv, vectors = tie(
        sent, cotangent, w_qkv, (first_norm_gain, ln1_bias, b_down, ln2_gain, ln2_bias, b_up)
    )
    far = swap_halves(sent)
    far_cot = swap_halves(rows_to_send(cotangent))
    qkv_w = (w_qkv[0], swap_cores(w_qkv[0]))
    own_p = jnp.concatenate([*vectors[:5], vectors[5].reshape(4, D), jnp.zeros((7, D), F32)], axis=0)
    places = jnp.arange(rows, dtype=jnp.int32)
    angles = ((j + core * length) * rows + places).astype(F32) * step
    cosb = jnp.broadcast_to(jnp.cos(angles)[:, None], (rows, 128))
    sinb = jnp.broadcast_to(jnp.sin(angles)[:, None], (rows, 128))
    apart = places[:, None] - places[None, :]
    near = jnp.cos(apart.astype(F32) * step)
    mask = jnp.where(apart >= 0, near, 0.0)
    mask_t = jnp.where(apart <= 0, near, 0.0)

    x = rows_taken(tokens, far)
    cot = rows_taken(cotangent, far_cot)
    x, cot, own_p, mask, mask_t, cosb, sinb, qkv_w, own_w = tie(
        x, cot, own_p, mask, mask_t, cosb, sinb, qkv_w, (w_out[0], w_up[0], w_down[0])
    )
    params = (own_p, swap_cores(own_p))
    other_w = tuple(swap_cores(w) for w in own_w)
    rest_w = (own_w[0], other_w[0], own_w[1], other_w[1], own_w[2], other_w[2])

    saved = []
    for layer in range(2):
        projected = run_project(layer, x, *qkv_w, cosb, sinb)
        spq, spk, vv, sigq, sigk, qf, kf, msg = projected
        recvs = from_chips(msg)
        near_sums = run_near(layer, spq, spk, vv, mask)
        recvs, near_sums = tie(recvs, near_sums)
        recvs = from_cores(msg, recvs)
        forward = run_forward(layer, x, near_sums, qf, recvs, params, rest_w)
        saved.append((x, projected, forward))
        x = forward[-1]
    outputs = (saved[0][2][-1], saved[1][2][-1])

    def ffn_part(layer, grad):
        x, (spq, spk, vv, sigq, sigk, qf, kf, _), forward = saved[layer]
        att, rden, mixed, hat1, scale1, normed, hidden, gprime, hat2, scale2, prefix, _ = forward
        d_ffn, d_up, d_branch, d_pre_one, r_low, t_high, t_low, small, msg = run_ffn_backward(
            layer, grad, (att, rden, qf, hat1, scale1, gprime, hat2, scale2), params, rest_w
        )
        recvs = from_chips(msg)
        sums = PartSum(layer, 0, *run_ffn_grads(layer, normed, hidden, d_ffn, d_up))
        return (r_low, t_high, t_low), (d_pre_one, mixed, d_branch, small), (msg, recvs), sums

    def near_part(layer, sides):
        _, (spq, spk, vv, _, _, _, _, _), _ = saved[layer]
        return run_near_backward(layer, spq, spk, vv, *sides, mask, mask_t)

    def attention_part(layer, sides, rest, near_grads, recvs):
        x, (_, _, vv, sigq, sigk, _, kf, _), forward = saved[layer]
        grad, kept, sent = run_attention_backward(
            layer, x, (vv, sigq, sigk, kf, *sides, forward[-2]), near_grads, recvs, (cosb, sinb), rest, *qkv_w
        )
        return grad, PartSum(layer, 1, kept, sent)

    sides, rest, (msg, recvs), ffn1 = ffn_part(1, cot)
    ffn1.send()
    near_grads = near_part(1, sides)
    near_grads, recvs, ffn1.received = tie(near_grads, recvs, ffn1.received)
    recvs = from_cores(msg, recvs)
    ffn1.add()
    recvs, ffn1.kept, ffn1.sent = tie(recvs, ffn1.kept, ffn1.sent)
    d_second, other1 = attention_part(1, sides, rest, near_grads, recvs)
    ffn1.send()
    other1.send()
    sides, rest, (msg, recvs), ffn0 = ffn_part(0, d_second)
    near_grads = near_part(0, sides)
    near_grads, recvs, other1.received = tie(near_grads, recvs, other1.received)
    recvs = from_cores(msg, recvs)
    other1.add()
    d_first, other0 = attention_part(0, sides, rest, near_grads, recvs)
    ffn1.received, other1.kept, other1.sent, other0.kept, other0.sent, ffn0.kept, ffn0.sent = tie(
        ffn1.received, other1.kept, other1.sent, other0.kept, other0.sent, ffn0.kept, ffn0.sent
    )
    ffn1.add()
    rows_far, place_finish = place_rows((outputs[0], d_first), (outputs[1], d_second))
    sums = Sums({"F1": ffn1, "C1": other1, "F0": ffn0, "C0": other0})
    sums.extra["rows"] = rows_far
    for name in ("F0", "C1", "F1", "C0"):
        sums.parts[name].send()
    for event in EVENTS if sums.steps == 3 else default_events(sums.steps):
        if event == "pre":
            mine, theirs = by_core(sums.of(0), sums.of(1), "by_core_0")
            hop = swap_cores(theirs)
        elif event == "unpack":
            arrays = unpack((mine, sums.after(hop)), False, None, "unpack_0")
            sums.token = arrays[3]
        elif event == "place":
            layer_outputs, input_grads = place_finish(sums.after(rows_far))
            sums.token = input_grads
        else:
            sums.process(event)
    small0, small1 = sums.smalls[0], sums.smalls[1]
    mine, theirs = by_core(sums.last(0), sums.last(1), "by_core_1")
    arrays = unpack((mine, None), True, arrays, "unpack_1")
    grad_up, grad_down, grad_qkv, grad_out = unpack((None, swap_cores(theirs)), True, arrays, "unpack_2")
    small = jnp.where(core == 0, small0, small1)
    d_gain1, d_bias1, d_b_down, d_gain2, d_bias2 = (small[i : i + 1] for i in range(5))
    d_b_up = small[5:9].reshape(1, FF)
    return (
        layer_outputs,
        input_grads,
        grad_qkv[None],
        grad_out[None],
        d_gain1,
        d_bias1,
        grad_up[None],
        d_b_up,
        grad_down[None],
        d_b_down,
        d_gain2,
        d_bias2,
    )


def solution(mesh):
    rows = P("dp", "seq", None)
    matrix = P("section", None, None)
    vector = P("section", None)
    out_rows = P("section", "dp", "seq", None)
    return jax.shard_map(
        body,
        mesh=mesh,
        in_specs=(rows, rows, matrix, matrix, vector, vector, matrix, vector, matrix, vector, vector, vector),
        out_specs=(
            out_rows, out_rows, matrix, matrix, vector, vector, matrix, vector, matrix, vector, vector, vector,
        ),
        check_vma=False,
    )
```

```python
import functools
import math

import jax
import jax.numpy as jnp
from jax import lax
from jax.experimental import pallas as pl
from jax.experimental.pallas import tpu as pltpu
from jax.sharding import PartitionSpec as P

D = 512
HEADS = 8
HEAD_DIM = 64
FF = 2048
PAIRS = HEADS // 2
EPS = 1e-05
BF = jnp.bfloat16
F32 = jnp.float32
MIB = 1024 * 1024
FLOPS = 1 << 20


def dot(a, b):
    return lax.dot_general(a, b, (((1,), (0,)), ((), ())), preferred_element_type=F32)


def dot_nt(a, b):
    return lax.dot_general(a, b, (((1,), (1,)), ((), ())), preferred_element_type=F32)


def dot_tn(a, b):
    return lax.dot_general(a, b, (((0,), (0,)), ((), ())), preferred_element_type=F32)


def low_half(rows, lanes):
    place = lax.broadcasted_iota(jnp.int32, (rows, lanes), 1)
    return lax.rem(place, 128) < HEAD_DIM


def block_diag(pair):
    rows, lanes = pair.shape
    low = low_half(rows, lanes)
    zero = jnp.zeros_like(pair)
    return jnp.concatenate([jnp.where(low, pair, zero), jnp.where(low, zero, pair)], axis=0)


def pair_cols(ref, g, width=128):
    return ref[:, g * width : (g + 1) * width]


def value_block(v_pair):
    ones = jnp.ones_like(v_pair)
    return jnp.concatenate([block_diag(v_pair), block_diag(ones)], axis=1)


def pack_message(blocks, keys):
    places = lax.broadcasted_iota(jnp.int32, (16, 256), 0)
    tail = jnp.zeros((16, 256), F32)
    for g in range(PAIRS):
        tail = jnp.where(places == g, jnp.broadcast_to(keys[g], (16, 256)), tail)
    return jnp.concatenate(list(blocks) + [tail], axis=0).astype(BF)


def place():
    length = lax.axis_size("seq") // 2
    z = lax.axis_index("seq")
    lower = z < length
    return lax.axis_index("section"), lower, jnp.where(lower, z, z - length), length


def sum_messages(refs, backward):
    core, _, j, length = place()
    total = jnp.zeros(refs[0].shape, F32)
    for i, ref in enumerate(refs):
        distance = i + 1
        if distance < length:
            wanted = j < distance if backward else j >= distance
        else:
            wanted = core == (0 if backward else 1)
        total = total + jnp.where(wanted, ref[...].astype(F32), 0.0)
    return total


CHUNK = 32


def each_rows(rows, fn, carry=None, unroll=False):
    if unroll:
        for r in range(0, rows, CHUNK):
            carry = fn(slice(r, r + CHUNK), carry)
        return carry

    def one(i, carry):
        return fn(pl.ds(pl.multiple_of(i * CHUNK, CHUNK), CHUNK), carry)

    return lax.fori_loop(0, rows // CHUNK, one, carry)


def row_mean(values):
    return jnp.sum(values, axis=-1, keepdims=True) * (1.0 / values.shape[-1])


def project(x, w_ref, waits, cosb, sinb, outs, tmp):
    spq, spk, vv, sigq, sigk, qf, kf, msg = outs
    rows = x.shape[0]

    def softplus_part(part, sp_ref, sig_ref, f_ref):
        waits[part]()
        tmp[...] = dot(x, w_ref[:, part * D : (part + 1) * D])

        def soften(s, _):
            raw = tmp[s, :]
            tail = jnp.exp(-jnp.abs(raw))
            soft = jnp.maximum(raw, 0.0) + jnp.log1p(tail)
            sig = jnp.where(raw >= 0.0, 1.0, tail) / (1.0 + tail)
            sp_ref[s, :] = soft.astype(BF)
            sig_ref[s, :] = sig
            cos_rows = cosb[s, :]
            sin_rows = sinb[s, :]
            for g in range(PAIRS):
                pair = soft[:, 128 * g : 128 * (g + 1)]
                f_ref[s, 256 * g : 256 * g + 128] = (pair * cos_rows).astype(BF)
                f_ref[s, 256 * g + 128 : 256 * (g + 1)] = (pair * sin_rows).astype(BF)

        each_rows(rows, soften)

    softplus_part(1, spk, sigk, kf)
    waits[2]()
    vv[...] = dot(x, w_ref[:, 2 * D : 3 * D]).astype(BF)
    softplus_part(0, spq, sigq, qf)
    low = low_half(64, 256)
    blocks, keys = [], []
    for g in range(PAIRS):
        kf_g = pair_cols(kf, g, 256)
        full = dot_tn(pair_cols(vv, g), kf_g)
        blocks.append(jnp.where(low, full[:64], full[64:]))
        keys.append(jnp.sum(kf_g.astype(F32), axis=0, keepdims=True))
    msg[...] = pack_message(blocks, keys)


def state_block(total, g):
    low = low_half(64, 256)
    block = total[64 * g : 64 * (g + 1), :]
    keys = jnp.broadcast_to(total[256 + g : 257 + g, :], (64, 256))
    zero = jnp.zeros((64, 256), F32)
    return jnp.concatenate(
        [
            jnp.where(low, block, zero),
            jnp.where(low, zero, block),
            jnp.where(low, keys, zero),
            jnp.where(low, zero, keys),
        ],
        axis=0,
    ).astype(BF)


def norm_forward(tmp, gain, bias, hat_ref, scale_ref, out_fn):

    def norm(s, _):
        values = tmp[s, :]
        centered = values - row_mean(values)
        scale = lax.rsqrt(row_mean(centered * centered) + EPS)
        hat = centered * scale
        hat_ref[s, :] = hat
        scale_ref[s, :] = jnp.broadcast_to(scale, (32, 128))
        out_fn(s, hat * gain + bias)

    each_rows(tmp.shape[0], norm, unroll=True)


def near_attention(spq, spk, vv, mask, near):
    mask2 = jnp.concatenate([mask[...], mask[...]], axis=1)
    for g in range(PAIRS):
        scores = dot_nt(pair_cols(spq, g), block_diag(pair_cols(spk, g))) * mask2
        near[:, 256 * g : 256 * (g + 1)] = dot(scores.astype(BF), value_block(pair_cols(vv, g)))


def attend_and_ffn(x, near, qf, recvs, params, w_out, w_up, w_down, waits, outs, tmp, tmp_up):
    att, rden, mixed, hat1, scale1, normed, hidden, gprime, hat2, scale2, prefix, result = outs
    rows = x.shape[0]
    total = sum_messages(recvs, False)
    prefix[...] = total
    for g in range(PAIRS):
        both = pair_cols(near, g, 256) + dot_nt(pair_cols(qf, g, 256), state_block(total, g))
        inverse = 1.0 / both[:, 128:]
        attended = both[:, :128] * inverse
        cols = slice(128 * g, 128 * (g + 1))
        att[:, cols] = attended
        rden[:, cols] = inverse
        mixed[:, cols] = attended.astype(BF)
    gain1, bias1, b_down, gain2, bias2 = (params[i : i + 1, :] for i in range(5))
    waits[0]()
    tmp[...] = x[...].astype(F32) + dot(mixed[...], w_out[...])

    def put_normed(s, value):
        normed[s, :] = value.astype(BF)
        tmp[s, :] = value

    norm_forward(tmp, gain1, bias1, hat1, scale1, put_normed)
    waits[1]()
    for c in range(FF // D):
        cols = slice(c * D, (c + 1) * D)
        tmp_up[...] = dot(normed[...], w_up[:, cols])
        b_up = params[5 + c : 6 + c, :]

        def activate(s, _, cols=cols, b_up=b_up):
            up = tmp_up[s, :] + b_up
            cdf = 0.5 + 0.5 * lax.erf(up * (1.0 / math.sqrt(2.0)))
            density = jnp.exp(-0.5 * up * up) * (1.0 / math.sqrt(2.0 * math.pi))
            hidden[s, cols] = (up * cdf).astype(BF)
            gprime[s, cols] = (cdf + up * density).astype(BF)

        each_rows(rows, activate, unroll=True)
    waits[2]()
    tmp[...] = tmp[...] + b_down + dot(hidden[...], w_down[...])

    def put_result(s, value):
        result[s, :] = value.astype(BF)

    norm_forward(tmp, gain2, bias2, hat2, scale2, put_result)


def column_sum(values):
    return jnp.sum(values, axis=0, keepdims=True)


def norm_backward(grad_fn, gain, hat_ref, scale_ref, rows, put, extras=0):
    def norm(s, sums):
        grad = grad_fn(s)
        hat = hat_ref[s, :]
        scaled = grad * gain
        first = row_mean(scaled)
        second = row_mean(scaled * hat)
        scale = scale_ref[s, :][:, :1]
        extra = put(s, (scaled - first - hat * second) * scale)
        new = (column_sum(grad * hat), column_sum(grad)) + extra
        return tuple(a + b for a, b in zip(sums, new))

    zero = jnp.zeros((1, D), F32)
    return each_rows(rows, norm, (zero,) * (2 + extras), True)


def ffn_backward(grad_fn, att, rden, qf, hat1, scale1, gprime, hat2, scale2, params, w_out, w_up, w_down, waits, outs, tmp, tmp_up):
    d_ffn, d_up, d_branch, d_pre_one, r_low, t_high, t_low, smalls, msg = outs
    rows = att.shape[0]
    gain1, gain2 = params[0:1, :], params[3:4, :]

    def put_two(s, value):
        rounded = value.astype(BF)
        tmp[s, :] = value
        d_ffn[s, :] = rounded
        return (column_sum(rounded.astype(F32)),)

    d_gain2, d_bias2, d_b_down = norm_backward(
        grad_fn, gain2, hat2, scale2, rows, put_two, 1
    )
    waits[0]()
    b_up = []
    for c in range(FF // D):
        cols = slice(c * D, (c + 1) * D)
        tmp_up[...] = dot_nt(d_ffn[...], w_down[cols, :])

        def scale_up(s, total, cols=cols):
            value = (tmp_up[s, :] * gprime[s, cols].astype(F32)).astype(BF)
            d_up[s, cols] = value
            return total + column_sum(value.astype(F32))

        b_up.append(each_rows(rows, scale_up, jnp.zeros((1, D), F32), True))
    waits[1]()
    tmp[...] = tmp[...] + dot_nt(d_up[...], w_up[...])

    def put_one(s, value):
        d_pre_one[s, :] = value
        d_branch[s, :] = value.astype(BF)
        return ()

    d_gain1, d_bias1 = norm_backward(lambda s: tmp[s, :], gain1, hat1, scale1, rows, put_one)
    waits[2]()
    tmp[...] = dot_nt(d_branch[...], w_out[...])

    def scores(s, _):
        rounded = (tmp[s, :] * rden[s, :]).astype(BF)
        product = -(rounded.astype(F32) * att[s, :])
        high = product.astype(BF)
        r_low[s, :] = rounded
        t_high[s, :] = high
        t_low[s, :] = (product - high.astype(F32)).astype(BF)

    each_rows(rows, scores, unroll=True)
    low = low_half(64, 256)
    blocks, keys = [], []
    for g in range(PAIRS):
        sides = jnp.concatenate([pair_cols(r_low, g), pair_cols(t_high, g)], axis=1)
        full = dot_tn(sides, pair_cols(qf, g, 256))
        blocks.append(jnp.where(low, full[:64], full[64:128]))
        keys.append(column_sum(jnp.where(low, full[128:192], full[192:])))
    msg[...] = pack_message(blocks, keys)
    smalls[...] = jnp.concatenate(
        [d_gain1, d_bias1, d_b_down, d_gain2, d_bias2] + b_up + [jnp.zeros((7, D), F32)], axis=0
    )


def near_backward(spq, spk, vv, r_low, t_high, t_low, mask, mask_t, outs):
    near_q, near_k, near_v = outs
    mask2 = jnp.concatenate([mask[...], mask[...]], axis=1)
    mask_t2 = jnp.concatenate([mask_t[...], mask_t[...]], axis=1)
    for g in range(PAIRS):
        spq_g, spk_g, vv_g = pair_cols(spq, g), pair_cols(spk, g), pair_cols(vv, g)
        r_g, th_g, tl_g = pair_cols(r_low, g), pair_cols(t_high, g), pair_cols(t_low, g)
        values = value_block(vv_g)
        spk_diag, spq_diag, r_diag = block_diag(spk_g), block_diag(spq_g), block_diag(r_g)
        cols = slice(128 * g, 128 * (g + 1))
        d_scores = dot_nt(jnp.concatenate([r_g, th_g], axis=1), values) + dot_nt(tl_g, values[:, 128:])
        near_q[:, cols] = dot((d_scores * mask2).astype(BF), spk_diag)
        scores_t = (dot_nt(spk_g, spq_diag) * mask_t2).astype(BF)
        near_v[:, cols] = dot(scores_t, r_diag)
        d_scores_t = dot_nt(
            jnp.concatenate([vv_g, jnp.ones_like(vv_g)], axis=1),
            jnp.concatenate([r_diag, block_diag(th_g)], axis=1),
        )
        near_k[:, cols] = dot((d_scores_t * mask_t2).astype(BF), spq_diag)


def attention_backward(
    layer, x, vv, sigq, sigk, kf, r_low, t_high, t_low, prefix, near, recvs, cosb, sinb,
    d_pre_one, mixed, d_branch, smalls, w_qkv, wait, outs, d_qkv,
):
    d_in, kept, sent = outs
    near_q, near_k, near_v = near
    total = sum_messages(recvs, True)
    low = low_half(64, 256)
    for g in range(PAIRS):
        cols = slice(128 * g, 128 * (g + 1))
        vv_g = pair_cols(vv, g)
        sides = jnp.concatenate([pair_cols(r_low, g), pair_cols(t_high, g)], axis=1)
        state = state_block(prefix[...], g)
        d_feat = dot(sides, state) + dot(pair_cols(t_low, g), state[128:, :])
        d_soft_q = near_q[:, cols] + cosb[...] * d_feat[:, :128] + sinb[...] * d_feat[:, 128:]
        block = total[64 * g : 64 * (g + 1), :]
        zero = jnp.zeros_like(block)
        later = jnp.concatenate([jnp.where(low, block, zero), jnp.where(low, zero, block)], axis=0).astype(BF)
        d_value = near_v[:, cols] + dot_nt(pair_cols(kf, g, 256), later)
        d_feat_k = dot(vv_g, later) + total[256 + g : 257 + g, :]
        d_soft_k = near_k[:, cols] + cosb[...] * d_feat_k[:, :128] + sinb[...] * d_feat_k[:, 128:]
        d_qkv[:, 128 * g : 128 * (g + 1)] = (pair_cols(sigq, g) * d_soft_q).astype(BF)
        d_qkv[:, D + 128 * g : D + 128 * (g + 1)] = (pair_cols(sigk, g) * d_soft_k).astype(BF)
        d_qkv[:, 2 * D + 128 * g : 2 * D + 128 * (g + 1)] = d_value.astype(BF)
    wait()
    d_in[...] = (d_pre_one[...] + dot_nt(d_qkv[...], w_qkv[...])).astype(BF)
    core = lax.axis_index("section")
    ids = part_ids(1)
    half_rows = D // 2
    for out, half in ((kept, core), (sent, 1 - core)):
        order = jnp.where(half == 0, ids[0], ids[1])
        start = pl.multiple_of(half * half_rows, half_rows)
        x_half = x[:, pl.ds(start, half_rows)]
        for j in range(3):
            store_chunks(out, j * half_rows, dot_tn(x_half, d_qkv[:, j * D : (j + 1) * D]).astype(BF), order, 4 * half_rows)
        value = dot_tn(mixed[:, pl.ds(start, half_rows)], d_branch[...]).astype(BF)
        store_chunks(out, 3 * half_rows, value, order, 4 * half_rows)
        put_smalls(out, 4 * half_rows, smalls[...])


def ffn_weight_grads(layer, normed, hidden, d_ffn, d_up, kept, sent):
    core = lax.axis_index("section")
    ids = part_ids(0)
    for out, half in ((kept, core), (sent, 1 - core)):
        order = jnp.where(half == 0, ids[0], ids[1])
        for j in range(2):
            start = pl.multiple_of(half * (FF // 2) + j * D, D)
            store_chunks(out, j * D, dot_tn(normed[...], d_up[:, pl.ds(start, D)]).astype(BF), order, 4 * D)
            value = dot_tn(hidden[:, pl.ds(start, D)], d_ffn[...]).astype(BF)
            store_chunks(out, (2 + j) * D, value, order, 4 * D)


def partner_bits():
    bits = [(axis, i) for axis in ("dp", "seq") for i in range(lax.axis_size(axis).bit_length() - 1)]
    last = bits.pop()
    return bits, last


def turned(bits, places):
    return bits[places:] + bits[:places]


def orders_of(part):
    bits, _ = partner_bits()
    third = max(1, len(bits) // 3)
    a, b, c = bits[:third], bits[third : 2 * third], bits[2 * third :]
    return [a + b + c, b + a + c] if part == 0 else [b + c + a, a + c + b]


def part_ids(part):
    ids = []
    for order in orders_of(part):
        number = jnp.int32(0)
        for axis, i in order:
            number = 2 * number + lax.rem(lax.div(lax.axis_index(axis), 1 << i), 2)
        ids.append(number)
    return ids


def chunk_rows(total):
    bits, _ = partner_bits()
    return total >> len(bits)


def store_chunks(out, first_row, value, number, total):
    size = chunk_rows(total)
    for i in range(value.shape[0] // size):
        chunk = first_row // size + i
        spot = pl.multiple_of(jnp.bitwise_xor(jnp.int32(chunk), number) * size, size)
        out[pl.ds(spot, size), :] = value[i * size : (i + 1) * size, :]


SMALL = 32


def put_smalls(out, start, value):
    high = value.astype(BF)
    out[start : start + 16, :] = high
    out[start + 16 : start + SMALL, :] = (value - high.astype(F32)).astype(BF)


def get_smalls(ref, start):
    return ref[start : start + 16, :].astype(F32) + ref[start + 16 : start + SMALL, :].astype(F32)


def load_weights(core, layer, pairs, sems):
    waits = []
    for own, other, held, parts in pairs:
        width = held.shape[1] // parts
        for p in range(parts):
            i = len(waits)
            cols = slice(p * width, (p + 1) * width)

            @pl.when(core == layer)
            def _(own=own, held=held, i=i, cols=cols):
                pltpu.make_async_copy(own.at[:, cols], held.at[:, cols], sems.at[i]).start()

            @pl.when(core != layer)
            def _(other=other, held=held, i=i, cols=cols):
                pltpu.make_async_copy(other.at[:, cols], held.at[:, cols], sems.at[i]).start()

            def wait(own=own, held=held, i=i, cols=cols):
                pltpu.make_async_copy(own.at[:, cols], held.at[:, cols], sems.at[i]).wait()

            waits.append(wait)
    return waits


def shape(rows, cols, kind):
    return jax.ShapeDtypeStruct((rows, cols), kind)


VMEM_SPEC = pl.BlockSpec(memory_space=pltpu.VMEM)
HBM_SPEC = pl.BlockSpec(memory_space=pltpu.HBM)
ANY_SPEC = pl.BlockSpec(memory_space=pl.ANY)


def call(kernel, args, specs, outs, scratch, name, micros, limit=16, pinned=()):
    if pinned:
        args = [pltpu.with_memory_space_constraint(a, pltpu.HBM) if i in pinned else a for i, a in enumerate(args)]
    return pl.pallas_call(
        kernel,
        out_shape=tuple(outs),
        in_specs=specs,
        out_specs=tuple(VMEM_SPEC for _ in outs),
        scratch_shapes=scratch,
        compiler_params=pltpu.CompilerParams(vmem_limit_bytes=limit * MIB),
        cost_estimate=pl.CostEstimate(flops=int(micros * FLOPS), bytes_accessed=1 << 10, transcendentals=0),
        name=name,
    )(*args)


def run_project(layer, sources, w_own, w_other, cosb, sinb):
    rows = sources[-1].shape[0]
    count = len(sources)
    outs = [shape(rows, D, BF)] * 3 + [shape(rows, D, F32)] * 2 + [shape(rows, 2 * D, BF)] * 2 + [shape(272, 256, BF)]

    if count == 2:
        outs = outs + [shape(rows, D, BF)]

    def kernel(*refs):
        own, other, cos_ref, sin_ref = refs[count : count + 4]
        out_refs = refs[count + 4 : count + 4 + len(outs)]
        held, tmp, sems = refs[count + 4 + len(outs) :]
        waits = load_weights(lax.axis_index("section"), layer, [(own, other, held, 3)], sems)
        if count == 1:
            x = refs[0][...]
        else:
            x = own_rows(refs[0], refs[1])
            out_refs[-1][...] = x
        project(x, held, waits, cos_ref, sin_ref, out_refs[:8], tmp)

    return call(
        kernel,
        (*sources, w_own, w_other, cosb, sinb),
        [VMEM_SPEC] * count + [HBM_SPEC, HBM_SPEC, VMEM_SPEC, VMEM_SPEC],
        outs,
        [pltpu.VMEM((D, 3 * D), BF), pltpu.VMEM((rows, D), F32), pltpu.SemaphoreType.DMA((3,))],
        f"project_{layer}",
        3,
        pinned=(count,) if layer == 0 else (),
    )


def run_near(layer, spq, spk, vv, mask):
    return call(
        near_attention,
        (spq, spk, vv, mask),
        [VMEM_SPEC] * 4,
        [shape(spq.shape[0], 2 * D, F32)],
        [],
        f"near_{layer}",
        3,
    )[0]


def ffn_scratch(rows):
    return [
        pltpu.VMEM((D, D), BF),
        pltpu.VMEM((D, FF), BF),
        pltpu.VMEM((FF, D), BF),
        pltpu.VMEM((16, D), F32),
        pltpu.VMEM((rows, D), F32),
        pltpu.VMEM((rows, D), F32),
        pltpu.SemaphoreType.DMA((3,)),
    ]


def run_forward(layer, x, near, qf, recvs, params, weights):
    rows = x.shape[0]
    outs = (
        [shape(rows, D, F32)] * 2
        + [shape(rows, D, BF), shape(rows, D, F32), shape(rows, 128, F32), shape(rows, D, BF)]
        + [shape(rows, FF, BF)] * 2
        + [shape(rows, D, F32), shape(rows, 128, F32), shape(272, 256, F32), shape(rows, D, BF)]
    )
    count = len(recvs)

    def kernel(*refs):
        core = lax.axis_index("section")
        x_ref, near_ref, qf_ref, own_p, other_p = refs[:5]
        recv_refs = refs[5 : 5 + count]
        w = refs[5 + count : 11 + count]
        out_refs = refs[11 + count : 23 + count]
        held_out, held_up, held_down, params_ref, tmp, tmp_up, sems = refs[23 + count :]
        waits = load_weights(
            core, layer, [(w[0], w[1], held_out, 1), (w[2], w[3], held_up, 1), (w[4], w[5], held_down, 1)], sems
        )
        params_ref[...] = jnp.where(core == layer, own_p[...], other_p[...])
        attend_and_ffn(
            x_ref, near_ref, qf_ref, recv_refs, params_ref, held_out, held_up, held_down, waits, out_refs, tmp, tmp_up
        )

    return call(
        kernel,
        (x, near, qf, *params, *recvs, *weights),
        [VMEM_SPEC] * (5 + count) + [HBM_SPEC] * 6,
        outs,
        ffn_scratch(rows),
        f"forward_{layer}",
        5,
        20,
    )


def run_ffn_backward(layer, sources, kept, params, weights):
    rows = sources[-1].shape[0]
    count = len(sources)
    outs = (
        [shape(rows, D, BF), shape(rows, FF, BF), shape(rows, D, BF), shape(rows, D, F32)]
        + [shape(rows, D, BF)] * 3
        + [shape(16, D, F32), shape(272, 256, BF)]
    )

    def kernel(*refs):
        core = lax.axis_index("section")
        att, rden, qf, hat1, scale1, gprime, hat2, scale2, own_p, other_p = refs[count : count + 10]
        w = refs[count + 10 : count + 16]
        out_refs = refs[count + 16 : count + 25]
        held_out, held_up, held_down, params_ref, tmp, tmp_up, sems = refs[count + 25 :]

        def grad_fn(s):
            if count == 1:
                return refs[0][s, :].astype(F32)
            return own_rows(refs[0], refs[1], s).astype(F32)

        waits = load_weights(
            core, layer, [(w[4], w[5], held_down, 1), (w[2], w[3], held_up, 1), (w[0], w[1], held_out, 1)], sems
        )
        params_ref[...] = jnp.where(core == layer, own_p[...], other_p[...])
        ffn_backward(
            grad_fn, att, rden, qf, hat1, scale1, gprime, hat2, scale2, params_ref,
            held_out, held_up, held_down, waits, out_refs, tmp, tmp_up,
        )

    return call(
        kernel,
        (*sources, *kept, *params, *weights),
        [VMEM_SPEC] * (10 + count) + [HBM_SPEC] * 6,
        outs,
        ffn_scratch(rows),
        f"ffn_backward_{layer}",
        5,
        20,
    )


def run_ffn_grads(layer, normed, hidden, d_ffn, d_up):
    return call(
        functools.partial(ffn_weight_grads, layer),
        (normed, hidden, d_ffn, d_up),
        [VMEM_SPEC] * 4,
        [shape(4 * D, D, BF)] * 2,
        [],
        f"ffn_grads_{layer}",
        4,
    )


def run_near_backward(layer, spq, spk, vv, r_low, t_high, t_low, mask, mask_t):
    def kernel(*refs):
        near_backward(*refs[:8], refs[8:])

    return call(
        kernel,
        (spq, spk, vv, r_low, t_high, t_low, mask, mask_t),
        [VMEM_SPEC] * 8,
        [shape(spq.shape[0], D, F32)] * 3,
        [],
        f"near_backward_{layer}",
        4,
    )


def run_attention_backward(layer, x, kept, near, recvs, fixed, rest, w_own, w_other):
    rows = x.shape[0]
    count = len(recvs)

    def kernel(*refs):
        x_ref, vv, sigq, sigk, kf, r_low, t_high, t_low, prefix = refs[:9]
        near_refs = refs[9:12]
        recv_refs = refs[12 : 12 + count]
        cosb, sinb, d_pre_one, mixed, d_branch, smalls, own, other = refs[12 + count : 20 + count]
        d_in, grads_kept, grads_sent, held, d_qkv, sems = refs[20 + count :]
        (wait,) = load_weights(lax.axis_index("section"), layer, [(own, other, held, 1)], sems)
        attention_backward(
            layer, x_ref, vv, sigq, sigk, kf, r_low, t_high, t_low, prefix, near_refs, recv_refs, cosb, sinb,
            d_pre_one, mixed, d_branch, smalls, held, wait, (d_in, grads_kept, grads_sent), d_qkv,
        )

    return call(
        kernel,
        (x, *kept, *near, *recvs, *fixed, *rest, w_own, w_other),
        [VMEM_SPEC] * (18 + count) + [HBM_SPEC] * 2,
        [shape(rows, D, BF)] + [shape(2 * D + SMALL, D, BF)] * 2,
        [pltpu.VMEM((D, 3 * D), BF), pltpu.VMEM((rows, 3 * D), BF), pltpu.SemaphoreType.DMA((1,))],
        f"attention_backward_{layer}",
        5,
        20,
    )


def combine(kept, received, tail, last, name):
    rows = kept.shape[0] - (SMALL if tail else 0)
    next_rows = rows if last else rows // 2
    count = 1 if last else 2

    def kernel(kept_ref, received_ref, *outs):
        for i, out in enumerate(outs):
            s = slice(i * next_rows, (i + 1) * next_rows)
            out[:next_rows, :] = (kept_ref[s, :].astype(F32) + received_ref[s, :].astype(F32)).astype(BF)
            if tail:
                put_smalls(out, next_rows, get_smalls(kept_ref, rows) + get_smalls(received_ref, rows))

    out_rows = next_rows + (SMALL if tail else 0)
    return call(
        kernel,
        (kept, received),
        [VMEM_SPEC] * 2,
        [shape(out_rows, kept.shape[1], BF)] * count,
        [],
        name,
        1,
    )


def join(a, b, name):
    def kernel(a_ref, b_ref, out):
        out[: a.shape[0], :] = a_ref[...]
        out[a.shape[0] :, :] = b_ref[...]

    return call(kernel, (a, b), [VMEM_SPEC] * 2, [shape(a.shape[0] + b.shape[0], D, BF)], [], name, 1)[0]


def split_sums(joined, received, ffn_rows, other_rows, name):
    def kernel(joined_ref, received_ref, ffn, other, smalls):
        for out, start, rows in ((ffn, 0, ffn_rows), (other, ffn_rows, other_rows)):
            s = slice(start, start + rows)
            out[...] = (joined_ref[s, :].astype(F32) + received_ref[s, :].astype(F32)).astype(BF)
        start = ffn_rows + other_rows
        smalls[...] = get_smalls(joined_ref, start) + get_smalls(received_ref, start)

    return call(
        kernel,
        (joined, received),
        [VMEM_SPEC] * 2,
        [shape(ffn_rows, D, BF), shape(other_rows, D, BF), shape(16, D, F32)],
        [],
        name,
        1,
    )


def by_core(zero, one, name, both=True):
    rows = [block.shape[0] for block in zero]

    def kernel(*refs):
        core = lax.axis_index("section")
        outs = refs[4:]
        for out, wanted in zip(outs, (0, 1) if both else (1,)):
            for layer in range(2):

                @pl.when(core == (layer if wanted == 0 else 1 - layer))
                def _(out=out, layer=layer):
                    out[: rows[0], :] = refs[2 * layer][...]
                    out[rows[0] :, :] = refs[2 * layer + 1][...]

    count = 2 if both else 1
    return call(kernel, (*zero, *one), [VMEM_SPEC] * 4, [shape(sum(rows), D, BF)] * count, [], name, 1)


def small_gradients(zero, one):
    def kernel(zero_ref, one_ref, *outs):
        small = jnp.where(lax.axis_index("section") == 0, zero_ref[...], one_ref[...])
        for i in range(5):
            outs[i][...] = small[i : i + 1, :]
        for c in range(FF // D):
            outs[5][:, c * D : (c + 1) * D] = small[5 + c : 6 + c, :]

    return call(
        kernel, (zero, one), [VMEM_SPEC] * 2, [shape(1, D, F32)] * 5 + [shape(1, FF, F32)], [], "small_gradients", 1
    )


def unpack(blocks, second, arrays, name):
    given = []
    for block in blocks:
        if isinstance(block, list):
            given += [part for pair in block for part in pair]
        elif block is not None:
            given.append(block)
    ffn_total, other_total = 4 * D, 2 * D
    sizes = (chunk_rows(ffn_total), chunk_rows(other_total))
    count = ffn_total // sizes[0] // 2
    out_shapes = [shape(D, FF, F32), shape(FF, D, F32), shape(D, 3 * D, F32), shape(D, D, F32)]

    def kernel(*refs):
        refs = list(refs)
        sources = [refs.pop(0) for _ in given]
        if arrays is not None:
            del refs[:4]
        up, down, qkv, out, held_ffn, held_other, sem_ffn, sem_other = refs
        core = lax.axis_index("section")
        slot = 0
        waits = []
        for block_place, block in enumerate(blocks):
            if block is None:
                continue
            pairs = [sources.pop(0) for _ in range(4)] if isinstance(block, list) else None
            source = None if pairs else sources.pop(0)
            half = core if block_place == 0 else 1 - core
            for part, size, held, sems in ((0, sizes[0], held_ffn, sem_ffn), (1, sizes[1], held_other, sem_other)):
                ids = part_ids(part)
                number = jnp.where(half == 0, ids[0], ids[1])
                base = 0 if part == 0 else ffn_total // 2
                for k in range(count):
                    index = slot * count + k
                    rows = slice(k * size, (k + 1) * size)
                    if pairs is None:
                        held[index] = source[base + k * size : base + (k + 1) * size, :].astype(F32)
                    else:
                        for layer in range(2):

                            @pl.when(core == layer)
                            def _(index=index, rows=rows, held=held, part_ref=pairs[2 * layer + part]):
                                held[index] = part_ref[rows, :].astype(F32)

                    chunk = jnp.bitwise_xor(k + (count if second else 0), number)
                    row = chunk * size
                    if part == 0:
                        piece, sub = lax.div(row, D), lax.rem(row, D)

                        @pl.when(piece < 2)
                        def _(piece=piece, sub=sub, index=index, half=half, held=held, sems=sems, size=size):
                            cols = pl.ds(pl.multiple_of((2 * half + piece) * D, D), D)
                            to = up.at[pl.ds(pl.multiple_of(sub, size), size), cols]
                            pltpu.make_async_copy(held.at[index], to, sems.at[index]).start()

                        @pl.when(piece >= 2)
                        def _(piece=piece, sub=sub, index=index, half=half, held=held, sems=sems, size=size):
                            start = pl.multiple_of((2 * half + piece - 2) * D + sub, size)
                            to = down.at[pl.ds(start, size), :]
                            pltpu.make_async_copy(held.at[index], to, sems.at[index]).start()

                        waits.append((held.at[index], down.at[pl.ds(0, size), :], sems.at[index]))
                    else:
                        piece, sub = lax.div(row, D // 2), lax.rem(row, D // 2)
                        start = pl.multiple_of(half * (D // 2) + sub, size)

                        @pl.when(piece < 3)
                        def _(piece=piece, start=start, index=index, held=held, sems=sems, size=size):
                            to = qkv.at[pl.ds(start, size), pl.ds(pl.multiple_of(piece * D, D), D)]
                            pltpu.make_async_copy(held.at[index], to, sems.at[index]).start()

                        @pl.when(piece == 3)
                        def _(start=start, index=index, held=held, sems=sems, size=size):
                            to = out.at[pl.ds(start, size), :]
                            pltpu.make_async_copy(held.at[index], to, sems.at[index]).start()

                        waits.append((held.at[index], out.at[pl.ds(0, size), :], sems.at[index]))
            slot += 1
        for wait in waits:
            pltpu.make_async_copy(*wait).wait()

    total = sum(block is not None for block in blocks) * count
    return pl.pallas_call(
        kernel,
        out_shape=tuple(out_shapes),
        in_specs=[VMEM_SPEC] * len(given) + ([ANY_SPEC] * 4 if arrays is not None else []),
        out_specs=(ANY_SPEC,) * 4,
        scratch_shapes=[
            pltpu.VMEM((total, sizes[0], D), F32),
            pltpu.VMEM((total, sizes[1], D), F32),
            pltpu.SemaphoreType.DMA((total,)),
            pltpu.SemaphoreType.DMA((total,)),
        ],
        input_output_aliases={} if arrays is None else {len(given) + k: k for k in range(4)},
        compiler_params=pltpu.CompilerParams(vmem_limit_bytes=24 * MIB),
        cost_estimate=pl.CostEstimate(flops=FLOPS, bytes_accessed=1 << 10, transcendentals=0),
        name=name,
    )(*given, *(arrays or ()))


def swap_cores(block):
    return lax.ppermute(block, "section", [(0, 1), (1, 0)])


def from_chips(message):
    length = lax.axis_size("seq") // 2
    received = []
    for distance in range(1, length):
        route = [(base + j, base + (j + distance) % length) for base in (0, length) for j in range(length)]
        received.append(lax.ppermute(message, "seq", route))
    return received


def from_cores(message, received):
    return received + [swap_cores(message)] + [swap_cores(m) for m in received]


def halves_route(cores):
    length = lax.axis_size("seq") // 2
    route = []
    for j in range(length):
        route.append((2 * (j + length) + cores[0][0], 2 * j + cores[0][1]))
        route.append((2 * j + cores[1][0], 2 * (j + length) + cores[1][1]))
    return route


def pick_rows(tokens, cotangent):
    rows = tokens.shape[1]

    def kernel(*refs):
        _, lower, _, _ = place()
        sems = refs[4]
        index = jnp.where(lower, 1, 0)
        copies = [pltpu.make_async_copy(refs[k].at[index], refs[2 + k], sems.at[k]) for k in range(2)]
        for copy in copies:
            copy.start()
        for copy in copies:
            copy.wait()

    return call(
        kernel, (tokens, cotangent), [HBM_SPEC] * 2, [shape(rows, D, BF)] * 2,
        [pltpu.SemaphoreType.DMA((2,))], "pick_rows", 1, pinned=(0, 1),
    )


def own_rows(whole_ref, far_ref, s=slice(None)):
    _, lower, _, _ = place()
    return jnp.where(stays(), whole_ref[jnp.where(lower, 0, 1), s, :], far_ref[s, :])


def stays():
    core, lower, _, _ = place()
    return (core == 0) == lower


def swap_halves(block):
    return lax.ppermute(block, ("seq", "section"), halves_route(((1, 1), (0, 0))))


def place_rows(firsts, seconds, name):
    count = len(firsts)
    rows, width = firsts[0].shape
    half = count * rows

    def stack(*refs):
        _, lower, _, _ = place()
        out, hop = refs[2 * count :]
        for k in range(2 * count):
            out[k * rows : (k + 1) * rows, :] = refs[k][...]
        for k in range(count):
            hop[k * rows : (k + 1) * rows, :] = jnp.where(lower, refs[count + k][...], refs[k][...])

    both, hop = call(
        stack, (*firsts, *seconds), [VMEM_SPEC] * 2 * count, [shape(2 * half, width, BF), shape(half, width, BF)],
        [], f"stack_{name}", 1,
    )
    far = lax.ppermute(both, ("seq", "section"), halves_route(((0, 0), (1, 0))))

    def finish(far):
        def kernel(both_ref, hop_ref, far_ref, far_second_ref, *outs):
            core, lower, _, _ = place()
            for k, out in enumerate(outs):
                s = slice(k * rows, (k + 1) * rows)
                own = jnp.where(core == 0, both_ref[s, :], both_ref[half + k * rows : half + (k + 1) * rows, :])
                local = jnp.where((core == 0) == lower, own, hop_ref[s, :])
                remote = jnp.where(core == 0, far_ref[s, :], far_second_ref[s, :])
                out[0, :, :] = jnp.where(lower, local, remote)
                out[1, :, :] = jnp.where(lower, remote, local)

        far_second = lax.ppermute(far[half:], "section", [(0, 1)])
        outs = [jax.ShapeDtypeStruct((2, rows, width), BF)] * count
        placed = call(kernel, (both, swap_cores(hop), far, far_second), [VMEM_SPEC] * 4, outs, [], f"place_{name}", 1)
        return [out[None] for out in placed]

    return far, finish


def exchange(block, layer, part, step):
    routes = []
    dp, seq = lax.axis_size("dp"), lax.axis_size("seq")
    for core, order in enumerate(orders_of(part)):
        axis, i = order[step]
        for a in range(dp):
            for b in range(seq):
                to = (a ^ (1 << i), b) if axis == "dp" else (a, b ^ (1 << i))
                routes.append(((a * seq + b) * 2 + core, (to[0] * seq + to[1]) * 2 + core))
    return lax.ppermute(block, ("dp", "seq", "section"), routes)


def exchange_last(block):
    _, (axis, i) = partner_bits()
    return lax.ppermute(block, axis, [(j, j ^ (1 << i)) for j in range(lax.axis_size(axis))])


def tie(*trees):
    return lax.optimization_barrier(trees)


class PartSum:
    def __init__(self, layer, part, kept, sent):
        self.name = f"{layer}_{part}"
        self.layer, self.part = layer, part
        self.kept, self.sent = kept, sent
        self.step = -1

    def send(self):
        self.received = swap_cores(self.sent) if self.step < 0 else exchange(self.sent, self.layer, self.part, self.step)

    def add(self):
        last = self.step == len(partner_bits()[0]) - 1
        result = combine(self.kept, self.received, self.part == 1, last, f"add_{self.name}_{self.step + 1}")
        self.kept, self.sent = result[0], result[-1]
        self.step += 1


EVENTS = (
    "B0", "F1.s0", "F0.w", "C1.s0", "C0.w", "F1.s1", "ra", "C1.s1", "C1.s2", "F1.s2", "F0.s0", "C0.s0", "Z1", "C0.s1", "F0.s1", "F1.a2",
    "C1.a2", "F0.s2", "C0.s2", "C1.a1", "F1.a1", "Z0", "C1.a0", "C0.a2", "F0.a2", "rs", "F0.a1", "F1.a0", "C0.a1", "small", "pa", "pre",
    "unpack", "C0.a0", "rd", "pd", "F0.a0",
)


def default_events(steps):
    events = ["B0", "F0.w", "C0.w"]
    for layer in (1, 0):
        events += [f"{part}{layer}.s{step}" for step in range(steps) for part in ("F", "C")] + [f"Z{layer}"]
    events += ["ra", "pa", "rs", "rd", "pd"]
    for step in reversed(range(steps)):
        events += ["small", "pre", "unpack"] if step == 0 else []
        events += [f"{part}{layer}.a{step}" for layer in (1, 0) for part in ("F", "C")]
    return events


class Sums:
    def __init__(self, parts):
        self.parts = parts
        self.steps = len(partner_bits()[0])
        self.token = None
        self.joined, self.far, self.smalls = {}, {}, {}
        self.whole, self.received = {}, {}

    def after(self, received):
        if self.token is not None:
            received, self.token = tie(received, self.token)
        return received

    def of(self, layer):
        return self.whole[f"F{layer}"], self.whole[f"C{layer}"]

    def last(self, layer):
        return self.received[f"F{layer}"], self.received[f"C{layer}"]

    def gather(self, name, step):
        if step >= 0:
            self.received[name] = exchange(self.whole[name], int(name[1]), "FC".index(name[0]), step)

    def process(self, event):
        if event[0] == "Z":
            layer = int(event[1])
            pair = self.parts[f"F{layer}"], self.parts[f"C{layer}"]
            rows = pair[0].kept.shape[0], pair[1].kept.shape[0] - SMALL
            far = self.after(self.far[layer])
            ffn, other, self.smalls[layer] = split_sums(self.joined[layer], far, *rows, f"split_{layer}")
            self.token = self.smalls[layer]
            for name, block in ((f"C{layer}", other), (f"F{layer}", ffn)):
                self.whole[name] = block
                self.gather(name, self.steps - 1)
            return
        name, kind = event.split(".")
        layer = int(name[1])
        if kind[0] == "a":
            step = int(kind[1:])
            received = self.after(self.received[name])
            self.received[name] = received
            if step == 0:
                self.token = received
                return
            self.whole[name] = join(self.whole[name], received, f"join_{name}_{step}")
            self.token = self.whole[name]
            self.gather(name, step - 1)
            return
        part = self.parts[name]
        part.received = self.after(part.received)
        part.add()
        self.token = part.kept
        if part.step < self.steps:
            part.send()
        pair = [self.parts.get(f"{p}{layer}") for p in "FC"]
        if all(p is not None and p.step == self.steps for p in pair):
            self.joined[layer] = join(pair[0].kept, pair[1].kept, f"join_{layer}")
            self.far[layer] = exchange_last(self.joined[layer])


def body(tokens, cotangent, w_qkv, w_out, first_norm_gain, ln1_bias, w_up, b_up, w_down, b_down, ln2_gain, ln2_bias):
    core, _, j, length = place()
    rows = tokens.shape[1]
    whole = rows * lax.axis_size("seq")
    step = math.pi / (2.0 * whole)
    sent, sent_cot = pick_rows(tokens, cotangent)
    far, far_cot = swap_halves(sent), swap_halves(sent_cot)
    vectors = (first_norm_gain, ln1_bias, b_down, ln2_gain, ln2_bias, b_up)
    sent, w_qkv, vectors = tie(sent, w_qkv, vectors)
    qkv_w = (w_qkv[0], swap_cores(w_qkv[0]))
    own_p = jnp.concatenate([*vectors[:5], vectors[5].reshape(4, D), jnp.zeros((7, D), F32)], axis=0)
    places = jnp.arange(rows, dtype=jnp.int32)
    angles = ((j + core * length) * rows + places).astype(F32) * step
    cosb = jnp.broadcast_to(jnp.cos(angles)[:, None], (rows, 128))
    sinb = jnp.broadcast_to(jnp.sin(angles)[:, None], (rows, 128))
    apart = places[:, None] - places[None, :]
    near = jnp.cos(apart.astype(F32) * step)
    mask = jnp.where(apart >= 0, near, 0.0)
    mask_t = jnp.where(apart <= 0, near, 0.0)

    far, own_p, mask, mask_t, cosb, sinb, qkv_w = tie(far, own_p, mask, mask_t, cosb, sinb, qkv_w)

    saved = []
    x = None
    for layer in range(2):
        projected = run_project(layer, (tokens, far) if layer == 0 else (x,), *qkv_w, cosb, sinb)
        spq, spk, vv, sigq, sigk, qf, kf, msg = projected[:8]
        if layer == 0:
            x = projected[8]
            msg, own_p, own_w = tie(msg, own_p, (w_out[0], w_up[0], w_down[0]))
            other_w = tuple(swap_cores(w) for w in own_w)
            rest_w = (own_w[0], other_w[0], own_w[1], other_w[1], own_w[2], other_w[2])
            params = (own_p, swap_cores(own_p))
        recvs = from_chips(msg)
        near_sums = run_near(layer, spq, spk, vv, mask)
        recvs, near_sums, far_cot = tie(recvs, near_sums, far_cot)
        recvs = from_cores(msg, recvs)
        forward = run_forward(layer, x, near_sums, qf, recvs, params, rest_w)
        saved.append((x, projected[:8], forward))
        x = forward[-1]
    outputs = (saved[0][2][-1], saved[1][2][-1])

    def ffn_part(layer, sources):
        x, (spq, spk, vv, sigq, sigk, qf, kf, _), forward = saved[layer]
        att, rden, mixed, hat1, scale1, normed, hidden, gprime, hat2, scale2, prefix, _ = forward
        d_ffn, d_up, d_branch, d_pre_one, r_low, t_high, t_low, small, msg = run_ffn_backward(
            layer, sources, (att, rden, qf, hat1, scale1, gprime, hat2, scale2), params, rest_w
        )
        recvs = from_chips(msg)
        sums = PartSum(layer, 0, *run_ffn_grads(layer, normed, hidden, d_ffn, d_up))
        return (r_low, t_high, t_low), (d_pre_one, mixed, d_branch, small), (msg, recvs), sums

    def near_part(layer, sides):
        _, (spq, spk, vv, _, _, _, _, _), _ = saved[layer]
        return run_near_backward(layer, spq, spk, vv, *sides, mask, mask_t)

    def attention_part(layer, sides, rest, near_grads, recvs):
        x, (_, _, vv, sigq, sigk, _, kf, _), forward = saved[layer]
        grad, kept, sent = run_attention_backward(
            layer, x, (vv, sigq, sigk, kf, *sides, forward[-2]), near_grads, recvs, (cosb, sinb), rest, *qkv_w
        )
        return grad, PartSum(layer, 1, kept, sent)

    sides, rest, (msg, recvs), ffn1 = ffn_part(1, (cotangent, far_cot))
    ffn1.send()
    near_grads = near_part(1, sides)
    near_grads, recvs, ffn1.received = tie(near_grads, recvs, ffn1.received)
    recvs = from_cores(msg, recvs)
    ffn1.add()
    recvs, ffn1.kept, ffn1.sent = tie(recvs, ffn1.kept, ffn1.sent)
    d_second, other1 = attention_part(1, sides, rest, near_grads, recvs)
    ffn1.send()
    other1.send()
    sides, rest, (msg, recvs), ffn0 = ffn_part(0, (d_second,))
    near_grads = near_part(0, sides)
    near_grads, recvs, other1.received = tie(near_grads, recvs, other1.received)
    recvs = from_cores(msg, recvs)
    other1.add()
    sums = Sums({"F1": ffn1, "C1": other1, "F0": ffn0})
    sums.token = other1.kept
    for event in EVENTS if sums.steps == 3 else default_events(sums.steps):
        if event == "B0":
            d_first, sums.parts["C0"] = attention_part(0, sides, rest, sums.after(near_grads), recvs)
            other0 = sums.parts["C0"]
            d_first, other0.sent, ffn0.sent, other1.sent, ffn1.received = tie(
                d_first, other0.sent, ffn0.sent, other1.sent, ffn1.received
            )
            sums.token = d_first
            ffn0.send()
            other1.send()
            other0.send()
            outputs_far, outputs_finish = place_rows((outputs[0],), (outputs[1],), "outputs")
        elif event == "ra":
            outputs_far = sums.after(outputs_far)
            sums.token = outputs_far
        elif event == "pa":
            (layer_outputs,) = outputs_finish(sums.after(outputs_far))
            sums.token = layer_outputs
        elif event == "rs":
            d_first = sums.after(d_first)
            inputs_far, inputs_finish = place_rows((d_first,), (d_second,), "inputs")
        elif event == "rd":
            inputs_far = sums.after(inputs_far)
            sums.token = inputs_far
        elif event == "pd":
            (input_grads,) = inputs_finish(sums.after(inputs_far))
            sums.token = input_grads
        elif event == "pre":
            mine, theirs = by_core(sums.of(0), sums.of(1), "by_core_0")
            hop = swap_cores(theirs)
        elif event == "small":
            small = small_gradients(sums.smalls[0], sums.after(sums.smalls[1]))
            sums.token = small[0]
        elif event == "unpack":
            arrays = unpack((mine, sums.after(hop)), False, None, "unpack_0")
            sums.token = arrays[3]
        else:
            sums.process(event)
    d_gain1, d_bias1, d_b_down, d_gain2, d_bias2, d_b_up = small
    zero, one = sums.last(0), sums.last(1)
    (theirs,) = by_core(zero, one, "by_core_1", False)
    arrays = unpack(([zero, one], None), True, arrays, "unpack_1")
    grad_up, grad_down, grad_qkv, grad_out = unpack((None, swap_cores(theirs)), True, arrays, "unpack_2")
    return (
        layer_outputs,
        input_grads,
        grad_qkv[None],
        grad_out[None],
        d_gain1,
        d_bias1,
        grad_up[None],
        d_b_up,
        grad_down[None],
        d_b_down,
        d_gain2,
        d_bias2,
    )


def solution(mesh):
    rows = P("dp", "seq", None)
    matrix = P("section", None, None)
    vector = P("section", None)
    out_rows = P("section", "dp", "seq", None)
    return jax.shard_map(
        body,
        mesh=mesh,
        in_specs=(rows, rows, matrix, matrix, vector, vector, matrix, vector, matrix, vector, vector, vector),
        out_specs=(
            out_rows, out_rows, matrix, matrix, vector, vector, matrix, vector, matrix, vector, vector, vector,
        ),
        check_vma=False,
    )
```

```python
import functools
import math

import jax
import jax.numpy as jnp
from jax import lax
from jax.experimental import pallas as pl
from jax.experimental.pallas import tpu as pltpu
from jax.sharding import PartitionSpec as P

D = 512
HEADS = 8
HEAD_DIM = 64
FF = 2048
PAIRS = HEADS // 2
EPS = 1e-05
BF = jnp.bfloat16
F32 = jnp.float32
MIB = 1024 * 1024
FLOPS = 1 << 20


def dot(a, b):
    return lax.dot_general(a, b, (((1,), (0,)), ((), ())), preferred_element_type=F32)


def dot_nt(a, b):
    return lax.dot_general(a, b, (((1,), (1,)), ((), ())), preferred_element_type=F32)


def dot_tn(a, b):
    return lax.dot_general(a, b, (((0,), (0,)), ((), ())), preferred_element_type=F32)


def low_half(rows, lanes):
    place = lax.broadcasted_iota(jnp.int32, (rows, lanes), 1)
    return lax.rem(place, 128) < HEAD_DIM


def block_diag(pair):
    rows, lanes = pair.shape
    low = low_half(rows, lanes)
    zero = jnp.zeros_like(pair)
    return jnp.concatenate([jnp.where(low, pair, zero), jnp.where(low, zero, pair)], axis=0)


def pair_cols(ref, g, width=128):
    return ref[:, g * width : (g + 1) * width]


def value_block(v_pair):
    ones = jnp.ones_like(v_pair)
    return jnp.concatenate([block_diag(v_pair), block_diag(ones)], axis=1)


def pack_message(blocks, keys):
    places = lax.broadcasted_iota(jnp.int32, (16, 256), 0)
    tail = jnp.zeros((16, 256), F32)
    for g in range(PAIRS):
        tail = jnp.where(places == g, jnp.broadcast_to(keys[g], (16, 256)), tail)
    return jnp.concatenate(list(blocks) + [tail], axis=0).astype(BF)


def place():
    length = lax.axis_size("seq") // 2
    z = lax.axis_index("seq")
    lower = z < length
    return lax.axis_index("section"), lower, jnp.where(lower, z, z - length), length


def sum_messages(refs, backward):
    core, _, j, length = place()
    total = jnp.zeros(refs[0].shape, F32)
    for i, ref in enumerate(refs):
        distance = i + 1
        if distance < length:
            wanted = j < distance if backward else j >= distance
        else:
            wanted = core == (0 if backward else 1)
        total = total + jnp.where(wanted, ref[...].astype(F32), 0.0)
    return total


CHUNK = 32


def each_rows(rows, fn, carry=None, unroll=False):
    if unroll:
        for r in range(0, rows, CHUNK):
            carry = fn(slice(r, r + CHUNK), carry)
        return carry

    def one(i, carry):
        return fn(pl.ds(pl.multiple_of(i * CHUNK, CHUNK), CHUNK), carry)

    return lax.fori_loop(0, rows // CHUNK, one, carry)


def row_mean(values):
    return jnp.sum(values, axis=-1, keepdims=True) * (1.0 / values.shape[-1])


def softplus_part(x, w_ref, part, cosb, sinb, sp_ref, sig_ref, f_ref, tmp):
    tmp[...] = dot(x, w_ref[:, part * D : (part + 1) * D])

    def soften(s, _):
        raw = tmp[s, :]
        tail = jnp.exp(-jnp.abs(raw))
        soft = jnp.maximum(raw, 0.0) + jnp.log1p(tail)
        sig = jnp.where(raw >= 0.0, 1.0, tail) / (1.0 + tail)
        sp_ref[s, :] = soft.astype(BF)
        sig_ref[s, :] = sig
        cos_rows = cosb[s, :]
        sin_rows = sinb[s, :]
        for g in range(PAIRS):
            pair = soft[:, 128 * g : 128 * (g + 1)]
            f_ref[s, 256 * g : 256 * g + 128] = (pair * cos_rows).astype(BF)
            f_ref[s, 256 * g + 128 : 256 * (g + 1)] = (pair * sin_rows).astype(BF)

    each_rows(x.shape[0], soften)


def project_keys(x, w_ref, waits, cosb, sinb, outs, tmp):
    spk, sigk, kf, vv, msg = outs
    waits[1]()
    softplus_part(x, w_ref, 1, cosb, sinb, spk, sigk, kf, tmp)
    waits[2]()
    vv[...] = dot(x, w_ref[:, 2 * D : 3 * D]).astype(BF)
    low = low_half(64, 256)
    blocks, keys = [], []
    for g in range(PAIRS):
        kf_g = pair_cols(kf, g, 256)
        full = dot_tn(pair_cols(vv, g), kf_g)
        blocks.append(jnp.where(low, full[:64], full[64:]))
        keys.append(jnp.sum(kf_g.astype(F32), axis=0, keepdims=True))
    msg[...] = pack_message(blocks, keys)


def state_block(total, g):
    low = low_half(64, 256)
    block = total[64 * g : 64 * (g + 1), :]
    keys = jnp.broadcast_to(total[256 + g : 257 + g, :], (64, 256))
    zero = jnp.zeros((64, 256), F32)
    return jnp.concatenate(
        [
            jnp.where(low, block, zero),
            jnp.where(low, zero, block),
            jnp.where(low, keys, zero),
            jnp.where(low, zero, keys),
        ],
        axis=0,
    ).astype(BF)


def norm_forward(tmp, gain, bias, hat_ref, scale_ref, out_fn):

    def norm(s, _):
        values = tmp[s, :]
        centered = values - row_mean(values)
        scale = lax.rsqrt(row_mean(centered * centered) + EPS)
        hat = centered * scale
        hat_ref[s, :] = hat
        scale_ref[s, :] = jnp.broadcast_to(scale, (32, 128))
        out_fn(s, hat * gain + bias)

    each_rows(tmp.shape[0], norm, unroll=True)


def near_attention(spq, spk, vv, mask, near):
    mask2 = jnp.concatenate([mask[...], mask[...]], axis=1)
    for g in range(PAIRS):
        scores = dot_nt(pair_cols(spq, g), block_diag(pair_cols(spk, g))) * mask2
        near[:, 256 * g : 256 * (g + 1)] = dot(scores.astype(BF), value_block(pair_cols(vv, g)))


def attend_and_ffn(x, near, qf, recvs, params, w_out, w_up, w_down, waits, outs, tmp, tmp_up):
    att, rden, mixed, hat1, scale1, normed, hidden, gprime, hat2, scale2, prefix, result = outs
    rows = x.shape[0]
    total = sum_messages(recvs, False)
    prefix[...] = total
    for g in range(PAIRS):
        both = pair_cols(near, g, 256) + dot_nt(pair_cols(qf, g, 256), state_block(total, g))
        inverse = 1.0 / both[:, 128:]
        attended = both[:, :128] * inverse
        cols = slice(128 * g, 128 * (g + 1))
        att[:, cols] = attended
        rden[:, cols] = inverse
        mixed[:, cols] = attended.astype(BF)
    gain1, bias1, b_down, gain2, bias2 = (params[i : i + 1, :] for i in range(5))
    waits[0]()
    tmp[...] = x[...].astype(F32) + dot(mixed[...], w_out[...])

    def put_normed(s, value):
        normed[s, :] = value.astype(BF)
        tmp[s, :] = value

    norm_forward(tmp, gain1, bias1, hat1, scale1, put_normed)
    waits[1]()
    for c in range(FF // D):
        cols = slice(c * D, (c + 1) * D)
        tmp_up[...] = dot(normed[...], w_up[:, cols])
        b_up = params[5 + c : 6 + c, :]

        def activate(s, _, cols=cols, b_up=b_up):
            up = tmp_up[s, :] + b_up
            cdf = 0.5 + 0.5 * lax.erf(up * (1.0 / math.sqrt(2.0)))
            density = jnp.exp(-0.5 * up * up) * (1.0 / math.sqrt(2.0 * math.pi))
            hidden[s, cols] = (up * cdf).astype(BF)
            gprime[s, cols] = (cdf + up * density).astype(BF)

        each_rows(rows, activate, unroll=True)
    waits[2]()
    tmp[...] = tmp[...] + b_down + dot(hidden[...], w_down[...])

    def put_result(s, value):
        result[s, :] = value.astype(BF)

    norm_forward(tmp, gain2, bias2, hat2, scale2, put_result)


def column_sum(values):
    return jnp.sum(values, axis=0, keepdims=True)


def norm_backward(grad_fn, gain, hat_ref, scale_ref, rows, put, extras=0):
    def norm(s, sums):
        grad = grad_fn(s)
        hat = hat_ref[s, :]
        scaled = grad * gain
        first = row_mean(scaled)
        second = row_mean(scaled * hat)
        scale = scale_ref[s, :][:, :1]
        extra = put(s, (scaled - first - hat * second) * scale)
        new = (column_sum(grad * hat), column_sum(grad)) + extra
        return tuple(a + b for a, b in zip(sums, new))

    zero = jnp.zeros((1, D), F32)
    return each_rows(rows, norm, (zero,) * (2 + extras), True)


def ffn_backward(grad_fn, att, rden, qf, hat1, scale1, gprime, hat2, scale2, params, w_out, w_up, w_down, waits, outs, tmp, tmp_up):
    d_ffn, d_up, d_branch, d_pre_one, r_low, t_high, t_low, smalls, msg = outs
    rows = att.shape[0]
    gain1, gain2 = params[0:1, :], params[3:4, :]

    def put_two(s, value):
        rounded = value.astype(BF)
        tmp[s, :] = value
        d_ffn[s, :] = rounded
        return (column_sum(rounded.astype(F32)),)

    d_gain2, d_bias2, d_b_down = norm_backward(
        grad_fn, gain2, hat2, scale2, rows, put_two, 1
    )
    waits[0]()
    b_up = []
    for c in range(FF // D):
        cols = slice(c * D, (c + 1) * D)
        tmp_up[...] = dot_nt(d_ffn[...], w_down[cols, :])

        def scale_up(s, total, cols=cols):
            value = (tmp_up[s, :] * gprime[s, cols].astype(F32)).astype(BF)
            d_up[s, cols] = value
            return total + column_sum(value.astype(F32))

        b_up.append(each_rows(rows, scale_up, jnp.zeros((1, D), F32), True))
    waits[1]()
    tmp[...] = tmp[...] + dot_nt(d_up[...], w_up[...])

    def put_one(s, value):
        d_pre_one[s, :] = value
        d_branch[s, :] = value.astype(BF)
        return ()

    d_gain1, d_bias1 = norm_backward(lambda s: tmp[s, :], gain1, hat1, scale1, rows, put_one)
    waits[2]()
    tmp[...] = dot_nt(d_branch[...], w_out[...])

    def scores(s, _):
        rounded = (tmp[s, :] * rden[s, :]).astype(BF)
        product = -(rounded.astype(F32) * att[s, :])
        high = product.astype(BF)
        r_low[s, :] = rounded
        t_high[s, :] = high
        t_low[s, :] = (product - high.astype(F32)).astype(BF)

    each_rows(rows, scores, unroll=True)
    low = low_half(64, 256)
    blocks, keys = [], []
    for g in range(PAIRS):
        sides = jnp.concatenate([pair_cols(r_low, g), pair_cols(t_high, g)], axis=1)
        full = dot_tn(sides, pair_cols(qf, g, 256))
        blocks.append(jnp.where(low, full[:64], full[64:128]))
        keys.append(column_sum(jnp.where(low, full[128:192], full[192:])))
    msg[...] = pack_message(blocks, keys)
    smalls[...] = jnp.concatenate(
        [d_gain1, d_bias1, d_b_down, d_gain2, d_bias2] + b_up + [jnp.zeros((7, D), F32)], axis=0
    )


def near_backward(spq, spk, vv, r_low, t_high, t_low, mask, mask_t, outs):
    near_q, near_k, near_v = outs
    mask2 = jnp.concatenate([mask[...], mask[...]], axis=1)
    mask_t2 = jnp.concatenate([mask_t[...], mask_t[...]], axis=1)
    for g in range(PAIRS):
        spq_g, spk_g, vv_g = pair_cols(spq, g), pair_cols(spk, g), pair_cols(vv, g)
        r_g, th_g, tl_g = pair_cols(r_low, g), pair_cols(t_high, g), pair_cols(t_low, g)
        values = value_block(vv_g)
        spk_diag, spq_diag, r_diag = block_diag(spk_g), block_diag(spq_g), block_diag(r_g)
        cols = slice(128 * g, 128 * (g + 1))
        d_scores = dot_nt(jnp.concatenate([r_g, th_g], axis=1), values) + dot_nt(tl_g, values[:, 128:])
        near_q[:, cols] = dot((d_scores * mask2).astype(BF), spk_diag)
        scores_t = (dot_nt(spk_g, spq_diag) * mask_t2).astype(BF)
        near_v[:, cols] = dot(scores_t, r_diag)
        d_scores_t = dot_nt(
            jnp.concatenate([vv_g, jnp.ones_like(vv_g)], axis=1),
            jnp.concatenate([r_diag, block_diag(th_g)], axis=1),
        )
        near_k[:, cols] = dot((d_scores_t * mask_t2).astype(BF), spq_diag)


def attention_backward(
    layer, x, vv, sigq, sigk, kf, r_low, t_high, t_low, prefix, near, recvs, cosb, sinb,
    d_pre_one, mixed, d_branch, smalls, w_qkv, wait, outs, d_qkv,
):
    d_in, kept, sent = outs
    near_q, near_k, near_v = near
    total = sum_messages(recvs, True)
    low = low_half(64, 256)
    for g in range(PAIRS):
        cols = slice(128 * g, 128 * (g + 1))
        vv_g = pair_cols(vv, g)
        sides = jnp.concatenate([pair_cols(r_low, g), pair_cols(t_high, g)], axis=1)
        state = state_block(prefix[...], g)
        d_feat = dot(sides, state) + dot(pair_cols(t_low, g), state[128:, :])
        d_soft_q = near_q[:, cols] + cosb[...] * d_feat[:, :128] + sinb[...] * d_feat[:, 128:]
        block = total[64 * g : 64 * (g + 1), :]
        zero = jnp.zeros_like(block)
        later = jnp.concatenate([jnp.where(low, block, zero), jnp.where(low, zero, block)], axis=0).astype(BF)
        d_value = near_v[:, cols] + dot_nt(pair_cols(kf, g, 256), later)
        d_feat_k = dot(vv_g, later) + total[256 + g : 257 + g, :]
        d_soft_k = near_k[:, cols] + cosb[...] * d_feat_k[:, :128] + sinb[...] * d_feat_k[:, 128:]
        d_qkv[:, 128 * g : 128 * (g + 1)] = (pair_cols(sigq, g) * d_soft_q).astype(BF)
        d_qkv[:, D + 128 * g : D + 128 * (g + 1)] = (pair_cols(sigk, g) * d_soft_k).astype(BF)
        d_qkv[:, 2 * D + 128 * g : 2 * D + 128 * (g + 1)] = d_value.astype(BF)
    wait()
    d_in[...] = (d_pre_one[...] + dot_nt(d_qkv[...], w_qkv[...])).astype(BF)
    core = lax.axis_index("section")
    ids = part_ids(1)
    half_rows = D // 2
    for out, half in ((kept, core), (sent, 1 - core)):
        order = jnp.where(half == 0, ids[0], ids[1])
        start = pl.multiple_of(half * half_rows, half_rows)
        x_half = x[:, pl.ds(start, half_rows)]
        for j in range(3):
            store_chunks(out, j * half_rows, dot_tn(x_half, d_qkv[:, j * D : (j + 1) * D]).astype(BF), order, 4 * half_rows)
        value = dot_tn(mixed[:, pl.ds(start, half_rows)], d_branch[...]).astype(BF)
        store_chunks(out, 3 * half_rows, value, order, 4 * half_rows)
        put_smalls(out, 4 * half_rows, smalls[...])


def ffn_weight_grads(layer, normed, hidden, d_ffn, d_up, kept, sent):
    core = lax.axis_index("section")
    ids = part_ids(0)
    for out, half in ((kept, core), (sent, 1 - core)):
        order = jnp.where(half == 0, ids[0], ids[1])
        for j in range(2):
            start = pl.multiple_of(half * (FF // 2) + j * D, D)
            store_chunks(out, j * D, dot_tn(normed[...], d_up[:, pl.ds(start, D)]).astype(BF), order, 4 * D)
            value = dot_tn(hidden[:, pl.ds(start, D)], d_ffn[...]).astype(BF)
            store_chunks(out, (2 + j) * D, value, order, 4 * D)


def partner_bits():
    bits = [(axis, i) for axis in ("dp", "seq") for i in range(lax.axis_size(axis).bit_length() - 1)]
    last = bits.pop()
    return bits, last


def turned(bits, places):
    return bits[places:] + bits[:places]


def orders_of(part):
    bits, _ = partner_bits()
    third = max(1, len(bits) // 3)
    a, b, c = bits[:third], bits[third : 2 * third], bits[2 * third :]
    return [a + b + c, b + a + c] if part == 0 else [b + c + a, a + c + b]


def part_ids(part):
    ids = []
    for order in orders_of(part):
        number = jnp.int32(0)
        for axis, i in order:
            number = 2 * number + lax.rem(lax.div(lax.axis_index(axis), 1 << i), 2)
        ids.append(number)
    return ids


def chunk_rows(total):
    bits, _ = partner_bits()
    return total >> len(bits)


def store_chunks(out, first_row, value, number, total):
    size = chunk_rows(total)
    for i in range(value.shape[0] // size):
        chunk = first_row // size + i
        spot = pl.multiple_of(jnp.bitwise_xor(jnp.int32(chunk), number) * size, size)
        out[pl.ds(spot, size), :] = value[i * size : (i + 1) * size, :]


SMALL = 32


def put_smalls(out, start, value):
    high = value.astype(BF)
    out[start : start + 16, :] = high
    out[start + 16 : start + SMALL, :] = (value - high.astype(F32)).astype(BF)


def get_smalls(ref, start):
    return ref[start : start + 16, :].astype(F32) + ref[start + 16 : start + SMALL, :].astype(F32)


def load_weights(core, layer, pairs, sems):
    waits = []
    for own, other, held, parts in pairs:
        width = held.shape[1] // parts
        for p in range(parts):
            i = len(waits)
            cols = slice(p * width, (p + 1) * width)

            @pl.when(core == layer)
            def _(own=own, held=held, i=i, cols=cols):
                pltpu.make_async_copy(own.at[:, cols], held.at[:, cols], sems.at[i]).start()

            @pl.when(core != layer)
            def _(other=other, held=held, i=i, cols=cols):
                pltpu.make_async_copy(other.at[:, cols], held.at[:, cols], sems.at[i]).start()

            def wait(own=own, held=held, i=i, cols=cols):
                pltpu.make_async_copy(own.at[:, cols], held.at[:, cols], sems.at[i]).wait()

            waits.append(wait)
    return waits


def shape(rows, cols, kind):
    return jax.ShapeDtypeStruct((rows, cols), kind)


VMEM_SPEC = pl.BlockSpec(memory_space=pltpu.VMEM)
HBM_SPEC = pl.BlockSpec(memory_space=pltpu.HBM)
ANY_SPEC = pl.BlockSpec(memory_space=pl.ANY)


def call(kernel, args, specs, outs, scratch, name, micros, limit=16, pinned=()):
    if pinned:
        args = [pltpu.with_memory_space_constraint(a, pltpu.HBM) if i in pinned else a for i, a in enumerate(args)]
    return pl.pallas_call(
        kernel,
        out_shape=tuple(outs),
        in_specs=specs,
        out_specs=tuple(VMEM_SPEC for _ in outs),
        scratch_shapes=scratch,
        compiler_params=pltpu.CompilerParams(vmem_limit_bytes=limit * MIB),
        cost_estimate=pl.CostEstimate(flops=int(micros * FLOPS), bytes_accessed=1 << 10, transcendentals=0),
        name=name,
    )(*args)


def run_project(layer, sources, w_own, w_other, cosb, sinb):
    rows = sources[-1].shape[0]
    count = len(sources)
    outs = [shape(rows, D, BF), shape(rows, D, F32), shape(rows, 2 * D, BF), shape(rows, D, BF), shape(272, 256, BF)]
    outs += [shape(rows, D, BF), shape(D, D, BF)]

    def kernel(*refs):
        own, other, cos_ref, sin_ref = refs[count : count + 4]
        out_refs = refs[count + 4 : count + 4 + len(outs)]
        held, tmp, sems = refs[count + 4 + len(outs) :]
        waits = load_weights(lax.axis_index("section"), layer, [(own, other, held, 3)], sems)
        x = refs[0][...] if count == 1 else own_rows(refs[0], refs[1])
        out_refs[5][...] = x
        project_keys(x, held, waits, cos_ref, sin_ref, out_refs[:5], tmp)
        waits[0]()
        out_refs[6][...] = held[:, :D]

    return call(
        kernel,
        (*sources, w_own, w_other, cosb, sinb),
        [VMEM_SPEC] * count + [HBM_SPEC, HBM_SPEC, VMEM_SPEC, VMEM_SPEC],
        outs,
        [pltpu.VMEM((D, 3 * D), BF), pltpu.VMEM((rows, D), F32), pltpu.SemaphoreType.DMA((3,))],
        f"project_{layer}",
        3,
        pinned=(count,) if layer == 0 else (),
    )


def run_near(layer, x, w_q, spk, vv, mask, cosb, sinb):
    rows = x.shape[0]

    def kernel(x_ref, w_ref, spk_ref, vv_ref, mask_ref, cos_ref, sin_ref, spq, sigq, qf, near, tmp):
        softplus_part(x_ref[...], w_ref, 0, cos_ref, sin_ref, spq, sigq, qf, tmp)
        near_attention(spq, spk_ref, vv_ref, mask_ref, near)

    return call(
        kernel,
        (x, w_q, spk, vv, mask, cosb, sinb),
        [VMEM_SPEC] * 7,
        [shape(rows, D, BF), shape(rows, D, F32), shape(rows, 2 * D, BF), shape(rows, 2 * D, F32)],
        [pltpu.VMEM((rows, D), F32)],
        f"near_{layer}",
        3,
    )


def ffn_scratch(rows):
    return [
        pltpu.VMEM((D, D), BF),
        pltpu.VMEM((D, FF), BF),
        pltpu.VMEM((FF, D), BF),
        pltpu.VMEM((16, D), F32),
        pltpu.VMEM((rows, D), F32),
        pltpu.VMEM((rows, D), F32),
        pltpu.SemaphoreType.DMA((3,)),
    ]


def run_forward(layer, x, near, qf, recvs, params, weights):
    rows = x.shape[0]
    outs = (
        [shape(rows, D, F32)] * 2
        + [shape(rows, D, BF), shape(rows, D, F32), shape(rows, 128, F32), shape(rows, D, BF)]
        + [shape(rows, FF, BF)] * 2
        + [shape(rows, D, F32), shape(rows, 128, F32), shape(272, 256, F32), shape(rows, D, BF)]
    )
    count = len(recvs)

    def kernel(*refs):
        core = lax.axis_index("section")
        x_ref, near_ref, qf_ref, own_p, other_p = refs[:5]
        recv_refs = refs[5 : 5 + count]
        w = refs[5 + count : 11 + count]
        out_refs = refs[11 + count : 23 + count]
        held_out, held_up, held_down, params_ref, tmp, tmp_up, sems = refs[23 + count :]
        waits = load_weights(
            core, layer, [(w[0], w[1], held_out, 1), (w[2], w[3], held_up, 1), (w[4], w[5], held_down, 1)], sems
        )
        params_ref[...] = jnp.where(core == layer, own_p[...], other_p[...])
        attend_and_ffn(
            x_ref, near_ref, qf_ref, recv_refs, params_ref, held_out, held_up, held_down, waits, out_refs, tmp, tmp_up
        )

    return call(
        kernel,
        (x, near, qf, *params, *recvs, *weights),
        [VMEM_SPEC] * (5 + count) + [HBM_SPEC] * 6,
        outs,
        ffn_scratch(rows),
        f"forward_{layer}",
        5,
        20,
    )


def run_ffn_backward(layer, sources, kept, params, weights):
    rows = sources[-1].shape[0]
    count = len(sources)
    outs = (
        [shape(rows, D, BF), shape(rows, FF, BF), shape(rows, D, BF), shape(rows, D, F32)]
        + [shape(rows, D, BF)] * 3
        + [shape(16, D, F32), shape(272, 256, BF)]
    )

    def kernel(*refs):
        core = lax.axis_index("section")
        att, rden, qf, hat1, scale1, gprime, hat2, scale2, own_p, other_p = refs[count : count + 10]
        w = refs[count + 10 : count + 16]
        out_refs = refs[count + 16 : count + 25]
        held_out, held_up, held_down, params_ref, tmp, tmp_up, sems = refs[count + 25 :]

        def grad_fn(s):
            if count == 1:
                return refs[0][s, :].astype(F32)
            return own_rows(refs[0], refs[1], s).astype(F32)

        waits = load_weights(
            core, layer, [(w[4], w[5], held_down, 1), (w[2], w[3], held_up, 1), (w[0], w[1], held_out, 1)], sems
        )
        params_ref[...] = jnp.where(core == layer, own_p[...], other_p[...])
        ffn_backward(
            grad_fn, att, rden, qf, hat1, scale1, gprime, hat2, scale2, params_ref,
            held_out, held_up, held_down, waits, out_refs, tmp, tmp_up,
        )

    return call(
        kernel,
        (*sources, *kept, *params, *weights),
        [VMEM_SPEC] * (10 + count) + [HBM_SPEC] * 6,
        outs,
        ffn_scratch(rows),
        f"ffn_backward_{layer}",
        5,
        20,
    )


def run_ffn_grads(layer, normed, hidden, d_ffn, d_up):
    return call(
        functools.partial(ffn_weight_grads, layer),
        (normed, hidden, d_ffn, d_up),
        [VMEM_SPEC] * 4,
        [shape(4 * D, D, BF)] * 2,
        [],
        f"ffn_grads_{layer}",
        4,
    )


def run_near_backward(layer, spq, spk, vv, r_low, t_high, t_low, mask, mask_t):
    def kernel(*refs):
        near_backward(*refs[:8], refs[8:])

    return call(
        kernel,
        (spq, spk, vv, r_low, t_high, t_low, mask, mask_t),
        [VMEM_SPEC] * 8,
        [shape(spq.shape[0], D, F32)] * 3,
        [],
        f"near_backward_{layer}",
        4,
    )


def run_attention_backward(layer, x, kept, near, recvs, fixed, rest, w_own, w_other):
    rows = x.shape[0]
    count = len(recvs)

    def kernel(*refs):
        x_ref, vv, sigq, sigk, kf, r_low, t_high, t_low, prefix = refs[:9]
        near_refs = refs[9:12]
        recv_refs = refs[12 : 12 + count]
        cosb, sinb, d_pre_one, mixed, d_branch, smalls, own, other = refs[12 + count : 20 + count]
        d_in, grads_kept, grads_sent, held, d_qkv, sems = refs[20 + count :]
        (wait,) = load_weights(lax.axis_index("section"), layer, [(own, other, held, 1)], sems)
        attention_backward(
            layer, x_ref, vv, sigq, sigk, kf, r_low, t_high, t_low, prefix, near_refs, recv_refs, cosb, sinb,
            d_pre_one, mixed, d_branch, smalls, held, wait, (d_in, grads_kept, grads_sent), d_qkv,
        )

    return call(
        kernel,
        (x, *kept, *near, *recvs, *fixed, *rest, w_own, w_other),
        [VMEM_SPEC] * (18 + count) + [HBM_SPEC] * 2,
        [shape(rows, D, BF)] + [shape(2 * D + SMALL, D, BF)] * 2,
        [pltpu.VMEM((D, 3 * D), BF), pltpu.VMEM((rows, 3 * D), BF), pltpu.SemaphoreType.DMA((1,))],
        f"attention_backward_{layer}",
        5,
        20,
    )


def combine(kept, received, tail, last, name):
    rows = kept.shape[0] - (SMALL if tail else 0)
    next_rows = rows if last else rows // 2
    count = 1 if last else 2

    def kernel(kept_ref, received_ref, *outs):
        for i, out in enumerate(outs):
            s = slice(i * next_rows, (i + 1) * next_rows)
            out[:next_rows, :] = (kept_ref[s, :].astype(F32) + received_ref[s, :].astype(F32)).astype(BF)
            if tail:
                put_smalls(out, next_rows, get_smalls(kept_ref, rows) + get_smalls(received_ref, rows))

    out_rows = next_rows + (SMALL if tail else 0)
    return call(
        kernel,
        (kept, received),
        [VMEM_SPEC] * 2,
        [shape(out_rows, kept.shape[1], BF)] * count,
        [],
        name,
        1,
    )


def join(a, b, name):
    def kernel(a_ref, b_ref, out):
        out[: a.shape[0], :] = a_ref[...]
        out[a.shape[0] :, :] = b_ref[...]

    return call(kernel, (a, b), [VMEM_SPEC] * 2, [shape(a.shape[0] + b.shape[0], D, BF)], [], name, 1)[0]


def split_sums(joined, received, ffn_rows, other_rows, name):
    def kernel(joined_ref, received_ref, ffn, other, smalls):
        for out, start, rows in ((ffn, 0, ffn_rows), (other, ffn_rows, other_rows)):
            s = slice(start, start + rows)
            out[...] = (joined_ref[s, :].astype(F32) + received_ref[s, :].astype(F32)).astype(BF)
        start = ffn_rows + other_rows
        smalls[...] = get_smalls(joined_ref, start) + get_smalls(received_ref, start)

    return call(
        kernel,
        (joined, received),
        [VMEM_SPEC] * 2,
        [shape(ffn_rows, D, BF), shape(other_rows, D, BF), shape(16, D, F32)],
        [],
        name,
        1,
    )


def by_core(zero, one, name, both=True):
    rows = [block.shape[0] for block in zero]

    def kernel(*refs):
        core = lax.axis_index("section")
        outs = refs[4:]
        for out, wanted in zip(outs, (0, 1) if both else (1,)):
            for layer in range(2):

                @pl.when(core == (layer if wanted == 0 else 1 - layer))
                def _(out=out, layer=layer):
                    out[: rows[0], :] = refs[2 * layer][...]
                    out[rows[0] :, :] = refs[2 * layer + 1][...]

    count = 2 if both else 1
    return call(kernel, (*zero, *one), [VMEM_SPEC] * 4, [shape(sum(rows), D, BF)] * count, [], name, 1)


def small_gradients(zero, one):
    def kernel(zero_ref, one_ref, *outs):
        small = jnp.where(lax.axis_index("section") == 0, zero_ref[...], one_ref[...])
        for i in range(5):
            outs[i][...] = small[i : i + 1, :]
        for c in range(FF // D):
            outs[5][:, c * D : (c + 1) * D] = small[5 + c : 6 + c, :]

    return call(
        kernel, (zero, one), [VMEM_SPEC] * 2, [shape(1, D, F32)] * 5 + [shape(1, FF, F32)], [], "small_gradients", 1
    )


def unpack(blocks, second, arrays, name):
    given = []
    for block in blocks:
        if isinstance(block, list):
            given += [part for pair in block for part in pair]
        elif block is not None:
            given.append(block)
    ffn_total, other_total = 4 * D, 2 * D
    sizes = (chunk_rows(ffn_total), chunk_rows(other_total))
    count = ffn_total // sizes[0] // 2
    out_shapes = [shape(D, FF, F32), shape(FF, D, F32), shape(D, 3 * D, F32), shape(D, D, F32)]

    def kernel(*refs):
        refs = list(refs)
        sources = [refs.pop(0) for _ in given]
        if arrays is not None:
            del refs[:4]
        up, down, qkv, out, held_ffn, held_other, sem_ffn, sem_other = refs
        core = lax.axis_index("section")
        slot = 0
        waits = []
        for block_place, block in enumerate(blocks):
            if block is None:
                continue
            pairs = [sources.pop(0) for _ in range(4)] if isinstance(block, list) else None
            source = None if pairs else sources.pop(0)
            half = core if block_place == 0 else 1 - core
            for part, size, held, sems in ((0, sizes[0], held_ffn, sem_ffn), (1, sizes[1], held_other, sem_other)):
                ids = part_ids(part)
                number = jnp.where(half == 0, ids[0], ids[1])
                base = 0 if part == 0 else ffn_total // 2
                for k in range(count):
                    index = slot * count + k
                    rows = slice(k * size, (k + 1) * size)
                    if pairs is None:
                        held[index] = source[base + k * size : base + (k + 1) * size, :].astype(F32)
                    else:
                        for layer in range(2):

                            @pl.when(core == layer)
                            def _(index=index, rows=rows, held=held, part_ref=pairs[2 * layer + part]):
                                held[index] = part_ref[rows, :].astype(F32)

                    chunk = jnp.bitwise_xor(k + (count if second else 0), number)
                    row = chunk * size
                    if part == 0:
                        piece, sub = lax.div(row, D), lax.rem(row, D)

                        @pl.when(piece < 2)
                        def _(piece=piece, sub=sub, index=index, half=half, held=held, sems=sems, size=size):
                            cols = pl.ds(pl.multiple_of((2 * half + piece) * D, D), D)
                            to = up.at[pl.ds(pl.multiple_of(sub, size), size), cols]
                            pltpu.make_async_copy(held.at[index], to, sems.at[index]).start()

                        @pl.when(piece >= 2)
                        def _(piece=piece, sub=sub, index=index, half=half, held=held, sems=sems, size=size):
                            start = pl.multiple_of((2 * half + piece - 2) * D + sub, size)
                            to = down.at[pl.ds(start, size), :]
                            pltpu.make_async_copy(held.at[index], to, sems.at[index]).start()

                        waits.append((held.at[index], down.at[pl.ds(0, size), :], sems.at[index]))
                    else:
                        piece, sub = lax.div(row, D // 2), lax.rem(row, D // 2)
                        start = pl.multiple_of(half * (D // 2) + sub, size)

                        @pl.when(piece < 3)
                        def _(piece=piece, start=start, index=index, held=held, sems=sems, size=size):
                            to = qkv.at[pl.ds(start, size), pl.ds(pl.multiple_of(piece * D, D), D)]
                            pltpu.make_async_copy(held.at[index], to, sems.at[index]).start()

                        @pl.when(piece == 3)
                        def _(start=start, index=index, held=held, sems=sems, size=size):
                            to = out.at[pl.ds(start, size), :]
                            pltpu.make_async_copy(held.at[index], to, sems.at[index]).start()

                        waits.append((held.at[index], out.at[pl.ds(0, size), :], sems.at[index]))
            slot += 1
        for wait in waits:
            pltpu.make_async_copy(*wait).wait()

    total = sum(block is not None for block in blocks) * count
    return pl.pallas_call(
        kernel,
        out_shape=tuple(out_shapes),
        in_specs=[VMEM_SPEC] * len(given) + ([ANY_SPEC] * 4 if arrays is not None else []),
        out_specs=(ANY_SPEC,) * 4,
        scratch_shapes=[
            pltpu.VMEM((total, sizes[0], D), F32),
            pltpu.VMEM((total, sizes[1], D), F32),
            pltpu.SemaphoreType.DMA((total,)),
            pltpu.SemaphoreType.DMA((total,)),
        ],
        input_output_aliases={} if arrays is None else {len(given) + k: k for k in range(4)},
        compiler_params=pltpu.CompilerParams(vmem_limit_bytes=24 * MIB),
        cost_estimate=pl.CostEstimate(flops=FLOPS, bytes_accessed=1 << 10, transcendentals=0),
        name=name,
    )(*given, *(arrays or ()))


def swap_cores(block):
    return lax.ppermute(block, "section", [(0, 1), (1, 0)])


def from_chips(message):
    length = lax.axis_size("seq") // 2
    received = []
    for distance in range(1, length):
        route = [(base + j, base + (j + distance) % length) for base in (0, length) for j in range(length)]
        received.append(lax.ppermute(message, "seq", route))
    return received


def from_cores(message, received):
    return received + [swap_cores(message)] + [swap_cores(m) for m in received]


def halves_route(cores):
    length = lax.axis_size("seq") // 2
    route = []
    for j in range(length):
        route.append((2 * (j + length) + cores[0][0], 2 * j + cores[0][1]))
        route.append((2 * j + cores[1][0], 2 * (j + length) + cores[1][1]))
    return route


def pick_rows(tokens, cotangent):
    rows = tokens.shape[1]

    def kernel(*refs):
        _, lower, _, _ = place()
        sems = refs[4]
        index = jnp.where(lower, 1, 0)
        copies = [pltpu.make_async_copy(refs[k].at[index], refs[2 + k], sems.at[k]) for k in range(2)]
        for copy in copies:
            copy.start()
        for copy in copies:
            copy.wait()

    return call(
        kernel, (tokens, cotangent), [HBM_SPEC] * 2, [shape(rows, D, BF)] * 2,
        [pltpu.SemaphoreType.DMA((2,))], "pick_rows", 1, pinned=(0, 1),
    )


def own_rows(whole_ref, far_ref, s=slice(None)):
    _, lower, _, _ = place()
    return jnp.where(stays(), whole_ref[jnp.where(lower, 0, 1), s, :], far_ref[s, :])


def stays():
    core, lower, _, _ = place()
    return (core == 0) == lower


def swap_halves(block):
    return lax.ppermute(block, ("seq", "section"), halves_route(((1, 1), (0, 0))))


def place_rows(firsts, seconds, name):
    count = len(firsts)
    rows, width = firsts[0].shape
    half = count * rows

    def stack(*refs):
        _, lower, _, _ = place()
        out, hop = refs[2 * count :]
        for k in range(2 * count):
            out[k * rows : (k + 1) * rows, :] = refs[k][...]
        for k in range(count):
            hop[k * rows : (k + 1) * rows, :] = jnp.where(lower, refs[count + k][...], refs[k][...])

    both, hop = call(
        stack, (*firsts, *seconds), [VMEM_SPEC] * 2 * count, [shape(2 * half, width, BF), shape(half, width, BF)],
        [], f"stack_{name}", 1,
    )
    far = lax.ppermute(both, ("seq", "section"), halves_route(((0, 0), (1, 0))))

    def finish(far):
        def kernel(both_ref, hop_ref, far_ref, far_second_ref, *outs):
            core, lower, _, _ = place()
            for k, out in enumerate(outs):
                s = slice(k * rows, (k + 1) * rows)
                own = jnp.where(core == 0, both_ref[s, :], both_ref[half + k * rows : half + (k + 1) * rows, :])
                local = jnp.where((core == 0) == lower, own, hop_ref[s, :])
                remote = jnp.where(core == 0, far_ref[s, :], far_second_ref[s, :])
                out[0, :, :] = jnp.where(lower, local, remote)
                out[1, :, :] = jnp.where(lower, remote, local)

        far_second = lax.ppermute(far[half:], "section", [(0, 1)])
        outs = [jax.ShapeDtypeStruct((2, rows, width), BF)] * count
        placed = call(kernel, (both, swap_cores(hop), far, far_second), [VMEM_SPEC] * 4, outs, [], f"place_{name}", 1)
        return [out[None] for out in placed]

    return far, finish


def exchange(block, layer, part, step):
    routes = []
    dp, seq = lax.axis_size("dp"), lax.axis_size("seq")
    for core, order in enumerate(orders_of(part)):
        axis, i = order[step]
        for a in range(dp):
            for b in range(seq):
                to = (a ^ (1 << i), b) if axis == "dp" else (a, b ^ (1 << i))
                routes.append(((a * seq + b) * 2 + core, (to[0] * seq + to[1]) * 2 + core))
    return lax.ppermute(block, ("dp", "seq", "section"), routes)


def exchange_last(block):
    _, (axis, i) = partner_bits()
    return lax.ppermute(block, axis, [(j, j ^ (1 << i)) for j in range(lax.axis_size(axis))])


def tie(*trees):
    return lax.optimization_barrier(trees)


class PartSum:
    def __init__(self, layer, part, kept, sent):
        self.name = f"{layer}_{part}"
        self.layer, self.part = layer, part
        self.kept, self.sent = kept, sent
        self.step = -1

    def send(self):
        self.received = swap_cores(self.sent) if self.step < 0 else exchange(self.sent, self.layer, self.part, self.step)

    def add(self):
        last = self.step == len(partner_bits()[0]) - 1
        result = combine(self.kept, self.received, self.part == 1, last, f"add_{self.name}_{self.step + 1}")
        self.kept, self.sent = result[0], result[-1]
        self.step += 1


EVENTS = (
    "B0", "F1.s0", "F0.w", "C1.s0", "C0.w", "F1.s1", "ra", "C1.s1", "C1.s2", "F1.s2", "F0.s0", "C0.s0", "Z1", "C0.s1", "F0.s1", "C1.a2",
    "F1.a2", "F0.s2", "C0.s2", "C1.a1", "F1.a1", "Z0", "C1.a0", "C0.a2", "F0.a2", "F0.a1", "rs", "F1.a0", "C0.a1", "small", "pa", "pre",
    "unpack", "C0.a0", "rd", "F0.a0", "pd",
)


def default_events(steps):
    events = ["B0", "F0.w", "C0.w"]
    for layer in (1, 0):
        events += [f"{part}{layer}.s{step}" for step in range(steps) for part in ("F", "C")] + [f"Z{layer}"]
    events += ["ra", "pa", "rs", "rd", "pd"]
    for step in reversed(range(steps)):
        events += ["small", "pre", "unpack"] if step == 0 else []
        events += [f"{part}{layer}.a{step}" for layer in (1, 0) for part in ("F", "C")]
    return events


class Sums:
    def __init__(self, parts):
        self.parts = parts
        self.steps = len(partner_bits()[0])
        self.token = None
        self.joined, self.far, self.smalls = {}, {}, {}
        self.whole, self.received = {}, {}

    def after(self, received):
        if self.token is not None:
            received, self.token = tie(received, self.token)
        return received

    def of(self, layer):
        return self.whole[f"F{layer}"], self.whole[f"C{layer}"]

    def last(self, layer):
        return self.received[f"F{layer}"], self.received[f"C{layer}"]

    def gather(self, name, step):
        if step >= 0:
            self.received[name] = exchange(self.whole[name], int(name[1]), "FC".index(name[0]), step)

    def process(self, event):
        if event[0] == "Z":
            layer = int(event[1])
            pair = self.parts[f"F{layer}"], self.parts[f"C{layer}"]
            rows = pair[0].kept.shape[0], pair[1].kept.shape[0] - SMALL
            far = self.after(self.far[layer])
            ffn, other, self.smalls[layer] = split_sums(self.joined[layer], far, *rows, f"split_{layer}")
            self.token = self.smalls[layer]
            for name, block in ((f"C{layer}", other), (f"F{layer}", ffn)):
                self.whole[name] = block
                self.gather(name, self.steps - 1)
            return
        name, kind = event.split(".")
        layer = int(name[1])
        if kind[0] == "a":
            step = int(kind[1:])
            received = self.after(self.received[name])
            self.received[name] = received
            if step == 0:
                self.token = received
                return
            self.whole[name] = join(self.whole[name], received, f"join_{name}_{step}")
            self.token = self.whole[name]
            self.gather(name, step - 1)
            return
        part = self.parts[name]
        part.received = self.after(part.received)
        part.add()
        self.token = part.kept
        if part.step < self.steps:
            part.send()
        pair = [self.parts.get(f"{p}{layer}") for p in "FC"]
        if all(p is not None and p.step == self.steps for p in pair):
            self.joined[layer] = join(pair[0].kept, pair[1].kept, f"join_{layer}")
            self.far[layer] = exchange_last(self.joined[layer])


def body(tokens, cotangent, w_qkv, w_out, first_norm_gain, ln1_bias, w_up, b_up, w_down, b_down, ln2_gain, ln2_bias):
    core, _, j, length = place()
    rows = tokens.shape[1]
    whole = rows * lax.axis_size("seq")
    step = math.pi / (2.0 * whole)
    sent, sent_cot = pick_rows(tokens, cotangent)
    far, far_cot = swap_halves(sent), swap_halves(sent_cot)
    vectors = (first_norm_gain, ln1_bias, b_down, ln2_gain, ln2_bias, b_up)
    sent, w_qkv, vectors = tie(sent, w_qkv, vectors)
    qkv_w = (w_qkv[0], swap_cores(w_qkv[0]))
    own_p = jnp.concatenate([*vectors[:5], vectors[5].reshape(4, D), jnp.zeros((7, D), F32)], axis=0)
    places = jnp.arange(rows, dtype=jnp.int32)
    angles = ((j + core * length) * rows + places).astype(F32) * step
    cosb = jnp.broadcast_to(jnp.cos(angles)[:, None], (rows, 128))
    sinb = jnp.broadcast_to(jnp.sin(angles)[:, None], (rows, 128))
    apart = places[:, None] - places[None, :]
    near = jnp.cos(apart.astype(F32) * step)
    mask = jnp.where(apart >= 0, near, 0.0)
    mask_t = jnp.where(apart <= 0, near, 0.0)

    far, own_p, mask, mask_t, cosb, sinb, qkv_w = tie(far, own_p, mask, mask_t, cosb, sinb, qkv_w)

    saved = []
    x = None
    for layer in range(2):
        projected = run_project(layer, (tokens, far) if layer == 0 else (x,), *qkv_w, cosb, sinb)
        spk, sigk, kf, vv, msg, x, w_q = projected
        if layer == 0:
            msg, own_p, own_w = tie(msg, own_p, (w_out[0], w_up[0], w_down[0]))
            other_w = tuple(swap_cores(w) for w in own_w)
            rest_w = (own_w[0], other_w[0], own_w[1], other_w[1], own_w[2], other_w[2])
            params = (own_p, swap_cores(own_p))
        recvs = from_chips(msg)
        spq, sigq, qf, near_sums = run_near(layer, x, w_q, spk, vv, mask, cosb, sinb)
        recvs, near_sums, far_cot = tie(recvs, near_sums, far_cot)
        recvs = from_cores(msg, recvs)
        forward = run_forward(layer, x, near_sums, qf, recvs, params, rest_w)
        saved.append((x, (spq, spk, vv, sigq, sigk, qf, kf, None), forward))
        x = forward[-1]
    outputs = (saved[0][2][-1], saved[1][2][-1])

    def ffn_part(layer, sources):
        x, (spq, spk, vv, sigq, sigk, qf, kf, _), forward = saved[layer]
        att, rden, mixed, hat1, scale1, normed, hidden, gprime, hat2, scale2, prefix, _ = forward
        d_ffn, d_up, d_branch, d_pre_one, r_low, t_high, t_low, small, msg = run_ffn_backward(
            layer, sources, (att, rden, qf, hat1, scale1, gprime, hat2, scale2), params, rest_w
        )
        recvs = from_chips(msg)
        sums = PartSum(layer, 0, *run_ffn_grads(layer, normed, hidden, d_ffn, d_up))
        return (r_low, t_high, t_low), (d_pre_one, mixed, d_branch, small), (msg, recvs), sums

    def near_part(layer, sides):
        _, (spq, spk, vv, _, _, _, _, _), _ = saved[layer]
        return run_near_backward(layer, spq, spk, vv, *sides, mask, mask_t)

    def attention_part(layer, sides, rest, near_grads, recvs):
        x, (_, _, vv, sigq, sigk, _, kf, _), forward = saved[layer]
        grad, kept, sent = run_attention_backward(
            layer, x, (vv, sigq, sigk, kf, *sides, forward[-2]), near_grads, recvs, (cosb, sinb), rest, *qkv_w
        )
        return grad, PartSum(layer, 1, kept, sent)

    sides, rest, (msg, recvs), ffn1 = ffn_part(1, (cotangent, far_cot))
    ffn1.send()
    near_grads = near_part(1, sides)
    near_grads, recvs, ffn1.received = tie(near_grads, recvs, ffn1.received)
    recvs = from_cores(msg, recvs)
    ffn1.add()
    recvs, ffn1.kept, ffn1.sent = tie(recvs, ffn1.kept, ffn1.sent)
    d_second, other1 = attention_part(1, sides, rest, near_grads, recvs)
    ffn1.send()
    other1.send()
    sides, rest, (msg, recvs), ffn0 = ffn_part(0, (d_second,))
    near_grads = near_part(0, sides)
    near_grads, recvs, other1.received = tie(near_grads, recvs, other1.received)
    recvs = from_cores(msg, recvs)
    other1.add()
    sums = Sums({"F1": ffn1, "C1": other1, "F0": ffn0})
    sums.token = other1.kept
    for event in EVENTS if sums.steps == 3 else default_events(sums.steps):
        if event == "B0":
            d_first, sums.parts["C0"] = attention_part(0, sides, rest, sums.after(near_grads), recvs)
            other0 = sums.parts["C0"]
            d_first, other0.sent, ffn0.sent, other1.sent, ffn1.received = tie(
                d_first, other0.sent, ffn0.sent, other1.sent, ffn1.received
            )
            sums.token = d_first
            ffn0.send()
            other1.send()
            other0.send()
            outputs_far, outputs_finish = place_rows((outputs[0],), (outputs[1],), "outputs")
        elif event == "ra":
            outputs_far = sums.after(outputs_far)
            sums.token = outputs_far
        elif event == "pa":
            (layer_outputs,) = outputs_finish(sums.after(outputs_far))
            sums.token = layer_outputs
        elif event == "rs":
            d_first = sums.after(d_first)
            inputs_far, inputs_finish = place_rows((d_first,), (d_second,), "inputs")
        elif event == "rd":
            inputs_far = sums.after(inputs_far)
            sums.token = inputs_far
        elif event == "pd":
            (input_grads,) = inputs_finish(sums.after(inputs_far))
            sums.token = input_grads
        elif event == "pre":
            mine, theirs = by_core(sums.of(0), sums.of(1), "by_core_0")
            hop = swap_cores(theirs)
        elif event == "small":
            small = small_gradients(sums.smalls[0], sums.after(sums.smalls[1]))
            sums.token = small[0]
        elif event == "unpack":
            arrays = unpack((mine, sums.after(hop)), False, None, "unpack_0")
            sums.token = arrays[3]
        else:
            sums.process(event)
    d_gain1, d_bias1, d_b_down, d_gain2, d_bias2, d_b_up = small
    zero, one = sums.last(0), sums.last(1)
    (theirs,) = by_core(zero, one, "by_core_1", False)
    arrays = unpack(([zero, one], None), True, arrays, "unpack_1")
    grad_up, grad_down, grad_qkv, grad_out = unpack((None, swap_cores(theirs)), True, arrays, "unpack_2")
    return (
        layer_outputs,
        input_grads,
        grad_qkv[None],
        grad_out[None],
        d_gain1,
        d_bias1,
        grad_up[None],
        d_b_up,
        grad_down[None],
        d_b_down,
        d_gain2,
        d_bias2,
    )


def solution(mesh):
    rows = P("dp", "seq", None)
    matrix = P("section", None, None)
    vector = P("section", None)
    out_rows = P("section", "dp", "seq", None)
    return jax.shard_map(
        body,
        mesh=mesh,
        in_specs=(rows, rows, matrix, matrix, vector, vector, matrix, vector, matrix, vector, vector, vector),
        out_specs=(
            out_rows, out_rows, matrix, matrix, vector, vector, matrix, vector, matrix, vector, vector, vector,
        ),
        check_vma=False,
    )
```

```python
import functools
import math

import jax
import jax.numpy as jnp
from jax import lax
from jax.experimental import pallas as pl
from jax.experimental.pallas import tpu as pltpu
from jax.sharding import PartitionSpec as P

D = 512
HEADS = 8
HEAD_DIM = 64
FF = 2048
PAIRS = HEADS // 2
EPS = 1e-05
BF = jnp.bfloat16
F32 = jnp.float32
MIB = 1024 * 1024
FLOPS = 1 << 20


def dot(a, b):
    return lax.dot_general(a, b, (((1,), (0,)), ((), ())), preferred_element_type=F32)


def dot_nt(a, b):
    return lax.dot_general(a, b, (((1,), (1,)), ((), ())), preferred_element_type=F32)


def dot_tn(a, b):
    return lax.dot_general(a, b, (((0,), (0,)), ((), ())), preferred_element_type=F32)


def low_half(rows, lanes):
    place = lax.broadcasted_iota(jnp.int32, (rows, lanes), 1)
    return lax.rem(place, 128) < HEAD_DIM


def block_diag(pair):
    rows, lanes = pair.shape
    low = low_half(rows, lanes)
    zero = jnp.zeros_like(pair)
    return jnp.concatenate([jnp.where(low, pair, zero), jnp.where(low, zero, pair)], axis=0)


def pair_cols(ref, g, width=128):
    return ref[:, g * width : (g + 1) * width]


def value_block(v_pair):
    ones = jnp.ones_like(v_pair)
    return jnp.concatenate([block_diag(v_pair), block_diag(ones)], axis=1)


def pack_message(blocks, keys):
    places = lax.broadcasted_iota(jnp.int32, (16, 256), 0)
    tail = jnp.zeros((16, 256), F32)
    for g in range(PAIRS):
        tail = jnp.where(places == g, jnp.broadcast_to(keys[g], (16, 256)), tail)
    return jnp.concatenate(list(blocks) + [tail], axis=0).astype(BF)


def place():
    length = lax.axis_size("seq") // 2
    z = lax.axis_index("seq")
    lower = z < length
    return lax.axis_index("section"), lower, jnp.where(lower, z, z - length), length


def sum_messages(refs, backward):
    core, _, j, length = place()
    total = jnp.zeros(refs[0].shape, F32)
    for i, ref in enumerate(refs):
        distance = i + 1
        if distance < length:
            wanted = j < distance if backward else j >= distance
        else:
            wanted = core == (0 if backward else 1)
        total = total + jnp.where(wanted, ref[...].astype(F32), 0.0)
    return total


CHUNK = 32


def each_rows(rows, fn, carry=None, unroll=False):
    if unroll:
        for r in range(0, rows, CHUNK):
            carry = fn(slice(r, r + CHUNK), carry)
        return carry

    def one(i, carry):
        return fn(pl.ds(pl.multiple_of(i * CHUNK, CHUNK), CHUNK), carry)

    return lax.fori_loop(0, rows // CHUNK, one, carry)


def row_mean(values):
    return jnp.sum(values, axis=-1, keepdims=True) * (1.0 / values.shape[-1])


def softplus_part(x, w_ref, part, cosb, sinb, sp_ref, sig_ref, f_ref, tmp):
    tmp[...] = dot(x, w_ref[:, part * D : (part + 1) * D])

    def soften(s, _):
        raw = tmp[s, :]
        tail = jnp.exp(-jnp.abs(raw))
        soft = jnp.maximum(raw, 0.0) + jnp.log1p(tail)
        sig = jnp.where(raw >= 0.0, 1.0, tail) / (1.0 + tail)
        sp_ref[s, :] = soft.astype(BF)
        sig_ref[s, :] = sig
        cos_rows = cosb[s, :]
        sin_rows = sinb[s, :]
        for g in range(PAIRS):
            pair = soft[:, 128 * g : 128 * (g + 1)]
            f_ref[s, 256 * g : 256 * g + 128] = (pair * cos_rows).astype(BF)
            f_ref[s, 256 * g + 128 : 256 * (g + 1)] = (pair * sin_rows).astype(BF)

    each_rows(x.shape[0], soften)


def project_keys(x, w_ref, waits, cosb, sinb, outs, tmp):
    spk, sigk, kf, vv, msg = outs
    waits[1]()
    softplus_part(x, w_ref, 1, cosb, sinb, spk, sigk, kf, tmp)
    waits[2]()
    vv[...] = dot(x, w_ref[:, 2 * D : 3 * D]).astype(BF)
    low = low_half(64, 256)
    blocks, keys = [], []
    for g in range(PAIRS):
        kf_g = pair_cols(kf, g, 256)
        full = dot_tn(pair_cols(vv, g), kf_g)
        blocks.append(jnp.where(low, full[:64], full[64:]))
        keys.append(jnp.sum(kf_g.astype(F32), axis=0, keepdims=True))
    msg[...] = pack_message(blocks, keys)


def state_block(total, g):
    low = low_half(64, 256)
    block = total[64 * g : 64 * (g + 1), :]
    keys = jnp.broadcast_to(total[256 + g : 257 + g, :], (64, 256))
    zero = jnp.zeros((64, 256), F32)
    return jnp.concatenate(
        [
            jnp.where(low, block, zero),
            jnp.where(low, zero, block),
            jnp.where(low, keys, zero),
            jnp.where(low, zero, keys),
        ],
        axis=0,
    ).astype(BF)


def norm_forward(tmp, gain, bias, hat_ref, scale_ref, out_fn):

    def norm(s, _):
        values = tmp[s, :]
        centered = values - row_mean(values)
        scale = lax.rsqrt(row_mean(centered * centered) + EPS)
        hat = centered * scale
        hat_ref[s, :] = hat
        scale_ref[s, :] = jnp.broadcast_to(scale, (32, 128))
        out_fn(s, hat * gain + bias)

    each_rows(tmp.shape[0], norm, unroll=True)


def near_attention(spq, spk, vv, mask, near):
    mask2 = jnp.concatenate([mask[...], mask[...]], axis=1)
    for g in range(PAIRS):
        scores = dot_nt(pair_cols(spq, g), block_diag(pair_cols(spk, g))) * mask2
        near[:, 256 * g : 256 * (g + 1)] = dot(scores.astype(BF), value_block(pair_cols(vv, g)))


def attend_and_ffn(x, near, qf, recvs, params, w_out, w_up, w_down, waits, outs, tmp, tmp_up):
    att, rden, mixed, hat1, scale1, normed, hidden, gprime, hat2, scale2, prefix, result = outs
    rows = x.shape[0]
    total = sum_messages(recvs, False)
    prefix[...] = total
    for g in range(PAIRS):
        both = pair_cols(near, g, 256) + dot_nt(pair_cols(qf, g, 256), state_block(total, g))
        inverse = 1.0 / both[:, 128:]
        attended = both[:, :128] * inverse
        cols = slice(128 * g, 128 * (g + 1))
        att[:, cols] = attended
        rden[:, cols] = inverse
        mixed[:, cols] = attended.astype(BF)
    gain1, bias1, b_down, gain2, bias2 = (params[i : i + 1, :] for i in range(5))
    waits[0]()
    tmp[...] = x[...].astype(F32) + dot(mixed[...], w_out[...])

    def put_normed(s, value):
        normed[s, :] = value.astype(BF)
        tmp[s, :] = value

    norm_forward(tmp, gain1, bias1, hat1, scale1, put_normed)
    waits[1]()
    for c in range(FF // D):
        cols = slice(c * D, (c + 1) * D)
        tmp_up[...] = dot(normed[...], w_up[:, cols])
        b_up = params[5 + c : 6 + c, :]

        def activate(s, _, cols=cols, b_up=b_up):
            up = tmp_up[s, :] + b_up
            cdf = 0.5 + 0.5 * lax.erf(up * (1.0 / math.sqrt(2.0)))
            density = jnp.exp(-0.5 * up * up) * (1.0 / math.sqrt(2.0 * math.pi))
            hidden[s, cols] = (up * cdf).astype(BF)
            gprime[s, cols] = (cdf + up * density).astype(BF)

        each_rows(rows, activate, unroll=True)
    waits[2]()
    tmp[...] = tmp[...] + b_down + dot(hidden[...], w_down[...])

    def put_result(s, value):
        result[s, :] = value.astype(BF)

    norm_forward(tmp, gain2, bias2, hat2, scale2, put_result)


def column_sum(values):
    return jnp.sum(values, axis=0, keepdims=True)


def norm_backward(grad_fn, gain, hat_ref, scale_ref, rows, put, extras=0):
    def norm(s, sums):
        grad = grad_fn(s)
        hat = hat_ref[s, :]
        scaled = grad * gain
        first = row_mean(scaled)
        second = row_mean(scaled * hat)
        scale = scale_ref[s, :][:, :1]
        extra = put(s, (scaled - first - hat * second) * scale)
        new = (column_sum(grad * hat), column_sum(grad)) + extra
        return tuple(a + b for a, b in zip(sums, new))

    zero = jnp.zeros((1, D), F32)
    return each_rows(rows, norm, (zero,) * (2 + extras), True)


def ffn_backward(grad_fn, att, rden, qf, hat1, scale1, gprime, hat2, scale2, params, w_out, w_up, w_down, waits, outs, tmp, tmp_up):
    d_ffn, d_up, d_branch, d_pre_one, r_low, t_high, t_low, smalls, msg = outs
    rows = att.shape[0]
    gain1, gain2 = params[0:1, :], params[3:4, :]

    def put_two(s, value):
        rounded = value.astype(BF)
        tmp[s, :] = value
        d_ffn[s, :] = rounded
        return (column_sum(rounded.astype(F32)),)

    d_gain2, d_bias2, d_b_down = norm_backward(
        grad_fn, gain2, hat2, scale2, rows, put_two, 1
    )
    waits[0]()
    b_up = []
    for c in range(FF // D):
        cols = slice(c * D, (c + 1) * D)
        tmp_up[...] = dot_nt(d_ffn[...], w_down[cols, :])

        def scale_up(s, total, cols=cols):
            value = (tmp_up[s, :] * gprime[s, cols].astype(F32)).astype(BF)
            d_up[s, cols] = value
            return total + column_sum(value.astype(F32))

        b_up.append(each_rows(rows, scale_up, jnp.zeros((1, D), F32), True))
    waits[1]()
    tmp[...] = tmp[...] + dot_nt(d_up[...], w_up[...])

    def put_one(s, value):
        d_pre_one[s, :] = value
        d_branch[s, :] = value.astype(BF)
        return ()

    d_gain1, d_bias1 = norm_backward(lambda s: tmp[s, :], gain1, hat1, scale1, rows, put_one)
    waits[2]()
    tmp[...] = dot_nt(d_branch[...], w_out[...])

    def scores(s, _):
        rounded = (tmp[s, :] * rden[s, :]).astype(BF)
        product = -(rounded.astype(F32) * att[s, :])
        high = product.astype(BF)
        r_low[s, :] = rounded
        t_high[s, :] = high
        t_low[s, :] = (product - high.astype(F32)).astype(BF)

    each_rows(rows, scores, unroll=True)
    low = low_half(64, 256)
    blocks, keys = [], []
    for g in range(PAIRS):
        sides = jnp.concatenate([pair_cols(r_low, g), pair_cols(t_high, g)], axis=1)
        full = dot_tn(sides, pair_cols(qf, g, 256))
        blocks.append(jnp.where(low, full[:64], full[64:128]))
        keys.append(column_sum(jnp.where(low, full[128:192], full[192:])))
    msg[...] = pack_message(blocks, keys)
    smalls[...] = jnp.concatenate(
        [d_gain1, d_bias1, d_b_down, d_gain2, d_bias2] + b_up + [jnp.zeros((7, D), F32)], axis=0
    )


def near_backward(spq, spk, vv, r_low, t_high, t_low, mask, mask_t, outs):
    near_q, near_k, near_v = outs
    mask2 = jnp.concatenate([mask[...], mask[...]], axis=1)
    mask_t2 = jnp.concatenate([mask_t[...], mask_t[...]], axis=1)
    for g in range(PAIRS):
        spq_g, spk_g, vv_g = pair_cols(spq, g), pair_cols(spk, g), pair_cols(vv, g)
        r_g, th_g, tl_g = pair_cols(r_low, g), pair_cols(t_high, g), pair_cols(t_low, g)
        values = value_block(vv_g)
        spk_diag, spq_diag, r_diag = block_diag(spk_g), block_diag(spq_g), block_diag(r_g)
        cols = slice(128 * g, 128 * (g + 1))
        d_scores = dot_nt(jnp.concatenate([r_g, th_g], axis=1), values) + dot_nt(tl_g, values[:, 128:])
        near_q[:, cols] = dot((d_scores * mask2).astype(BF), spk_diag)
        scores_t = (dot_nt(spk_g, spq_diag) * mask_t2).astype(BF)
        near_v[:, cols] = dot(scores_t, r_diag)
        d_scores_t = dot_nt(
            jnp.concatenate([vv_g, jnp.ones_like(vv_g)], axis=1),
            jnp.concatenate([r_diag, block_diag(th_g)], axis=1),
        )
        near_k[:, cols] = dot((d_scores_t * mask_t2).astype(BF), spq_diag)


def attention_backward(
    layer, x, vv, sigq, sigk, kf, r_low, t_high, t_low, prefix, near, recvs, cosb, sinb,
    d_pre_one, mixed, d_branch, smalls, w_qkv, wait, outs, d_qkv,
):
    d_in, kept, sent = outs
    near_q, near_k, near_v = near
    total = sum_messages(recvs, True)
    low = low_half(64, 256)
    for g in range(PAIRS):
        cols = slice(128 * g, 128 * (g + 1))
        vv_g = pair_cols(vv, g)
        sides = jnp.concatenate([pair_cols(r_low, g), pair_cols(t_high, g)], axis=1)
        state = state_block(prefix[...], g)
        d_feat = dot(sides, state) + dot(pair_cols(t_low, g), state[128:, :])
        d_soft_q = near_q[:, cols] + cosb[...] * d_feat[:, :128] + sinb[...] * d_feat[:, 128:]
        block = total[64 * g : 64 * (g + 1), :]
        zero = jnp.zeros_like(block)
        later = jnp.concatenate([jnp.where(low, block, zero), jnp.where(low, zero, block)], axis=0).astype(BF)
        d_value = near_v[:, cols] + dot_nt(pair_cols(kf, g, 256), later)
        d_feat_k = dot(vv_g, later) + total[256 + g : 257 + g, :]
        d_soft_k = near_k[:, cols] + cosb[...] * d_feat_k[:, :128] + sinb[...] * d_feat_k[:, 128:]
        d_qkv[:, 128 * g : 128 * (g + 1)] = (pair_cols(sigq, g) * d_soft_q).astype(BF)
        d_qkv[:, D + 128 * g : D + 128 * (g + 1)] = (pair_cols(sigk, g) * d_soft_k).astype(BF)
        d_qkv[:, 2 * D + 128 * g : 2 * D + 128 * (g + 1)] = d_value.astype(BF)
    wait()
    d_in[...] = (d_pre_one[...] + dot_nt(d_qkv[...], w_qkv[...])).astype(BF)
    core = lax.axis_index("section")
    ids = part_ids(1)
    half_rows = D // 2
    for out, half in ((kept, core), (sent, 1 - core)):
        order = jnp.where(half == 0, ids[0], ids[1])
        start = pl.multiple_of(half * half_rows, half_rows)
        x_half = x[:, pl.ds(start, half_rows)]
        for j in range(3):
            store_chunks(out, j * half_rows, dot_tn(x_half, d_qkv[:, j * D : (j + 1) * D]).astype(BF), order, 4 * half_rows)
        value = dot_tn(mixed[:, pl.ds(start, half_rows)], d_branch[...]).astype(BF)
        store_chunks(out, 3 * half_rows, value, order, 4 * half_rows)
        put_smalls(out, 4 * half_rows, smalls[...])


def ffn_weight_grads(layer, normed, hidden, d_ffn, d_up, kept, sent):
    core = lax.axis_index("section")
    ids = part_ids(0)
    for out, half in ((kept, core), (sent, 1 - core)):
        order = jnp.where(half == 0, ids[0], ids[1])
        for j in range(2):
            start = pl.multiple_of(half * (FF // 2) + j * D, D)
            store_chunks(out, j * D, dot_tn(normed[...], d_up[:, pl.ds(start, D)]).astype(BF), order, 4 * D)
            value = dot_tn(hidden[:, pl.ds(start, D)], d_ffn[...]).astype(BF)
            store_chunks(out, (2 + j) * D, value, order, 4 * D)


def partner_bits():
    bits = [(axis, i) for axis in ("dp", "seq") for i in range(lax.axis_size(axis).bit_length() - 1)]
    last = bits.pop()
    return bits, last


def turned(bits, places):
    return bits[places:] + bits[:places]


def orders_of(part):
    bits, _ = partner_bits()
    third = max(1, len(bits) // 3)
    a, b, c = bits[:third], bits[third : 2 * third], bits[2 * third :]
    return [a + b + c, b + a + c] if part == 0 else [b + c + a, a + c + b]


def part_ids(part):
    ids = []
    for order in orders_of(part):
        number = jnp.int32(0)
        for axis, i in order:
            number = 2 * number + lax.rem(lax.div(lax.axis_index(axis), 1 << i), 2)
        ids.append(number)
    return ids


def chunk_rows(total):
    bits, _ = partner_bits()
    return total >> len(bits)


def store_chunks(out, first_row, value, number, total):
    size = chunk_rows(total)
    for i in range(value.shape[0] // size):
        chunk = first_row // size + i
        spot = pl.multiple_of(jnp.bitwise_xor(jnp.int32(chunk), number) * size, size)
        out[pl.ds(spot, size), :] = value[i * size : (i + 1) * size, :]


SMALL = 16
SMALL_ROWS = 5 + FF // D


def put_smalls(out, start, value):
    high = value.astype(BF).astype(F32)
    rest = (value - high)[: SMALL - SMALL_ROWS]
    out[start : start + SMALL, :] = jnp.concatenate([high[:SMALL_ROWS], rest], axis=0).astype(BF)


def get_smalls(ref, start):
    rows = ref[start : start + SMALL, :].astype(F32)
    left = SMALL - SMALL_ROWS
    zero = jnp.zeros((left, D), F32)
    rest = jnp.concatenate([rows[SMALL_ROWS:], jnp.zeros((SMALL_ROWS, D), F32)], axis=0)
    return jnp.concatenate([rows[:SMALL_ROWS], zero], axis=0) + rest


def load_weights(core, layer, pairs, sems):
    waits = []
    for own, other, held, parts in pairs:
        width = held.shape[1] // parts
        for p in range(parts):
            i = len(waits)
            cols = slice(p * width, (p + 1) * width)

            @pl.when(core == layer)
            def _(own=own, held=held, i=i, cols=cols):
                pltpu.make_async_copy(own.at[:, cols], held.at[:, cols], sems.at[i]).start()

            @pl.when(core != layer)
            def _(other=other, held=held, i=i, cols=cols):
                pltpu.make_async_copy(other.at[:, cols], held.at[:, cols], sems.at[i]).start()

            def wait(own=own, held=held, i=i, cols=cols):
                pltpu.make_async_copy(own.at[:, cols], held.at[:, cols], sems.at[i]).wait()

            waits.append(wait)
    return waits


def shape(rows, cols, kind):
    return jax.ShapeDtypeStruct((rows, cols), kind)


VMEM_SPEC = pl.BlockSpec(memory_space=pltpu.VMEM)
HBM_SPEC = pl.BlockSpec(memory_space=pltpu.HBM)
ANY_SPEC = pl.BlockSpec(memory_space=pl.ANY)


def call(kernel, args, specs, outs, scratch, name, micros, limit=16, pinned=()):
    if pinned:
        args = [pltpu.with_memory_space_constraint(a, pltpu.HBM) if i in pinned else a for i, a in enumerate(args)]
    return pl.pallas_call(
        kernel,
        out_shape=tuple(outs),
        in_specs=specs,
        out_specs=tuple(VMEM_SPEC for _ in outs),
        scratch_shapes=scratch,
        compiler_params=pltpu.CompilerParams(vmem_limit_bytes=limit * MIB),
        cost_estimate=pl.CostEstimate(flops=int(micros * FLOPS), bytes_accessed=1 << 10, transcendentals=0),
        name=name,
    )(*args)


def run_project(layer, sources, w_own, w_other, cosb, sinb):
    rows = sources[-1].shape[0]
    count = len(sources)
    outs = [shape(rows, D, BF), shape(rows, D, F32), shape(rows, 2 * D, BF), shape(rows, D, BF), shape(272, 256, BF)]
    outs += [shape(rows, D, BF), shape(D, D, BF)]

    def kernel(*refs):
        own, other, cos_ref, sin_ref = refs[count : count + 4]
        out_refs = refs[count + 4 : count + 4 + len(outs)]
        held, tmp, sems = refs[count + 4 + len(outs) :]
        waits = load_weights(lax.axis_index("section"), layer, [(own, other, held, 3)], sems)
        x = refs[0][...] if count == 1 else own_rows(refs[0], refs[1])
        out_refs[5][...] = x
        project_keys(x, held, waits, cos_ref, sin_ref, out_refs[:5], tmp)
        waits[0]()
        out_refs[6][...] = held[:, :D]

    return call(
        kernel,
        (*sources, w_own, w_other, cosb, sinb),
        [VMEM_SPEC] * count + [HBM_SPEC, HBM_SPEC, VMEM_SPEC, VMEM_SPEC],
        outs,
        [pltpu.VMEM((D, 3 * D), BF), pltpu.VMEM((rows, D), F32), pltpu.SemaphoreType.DMA((3,))],
        f"project_{layer}",
        3,
        pinned=(count,) if layer == 0 else (),
    )


def run_near(layer, x, w_q, spk, vv, mask, cosb, sinb):
    rows = x.shape[0]

    def kernel(x_ref, w_ref, spk_ref, vv_ref, mask_ref, cos_ref, sin_ref, spq, sigq, qf, near, tmp):
        softplus_part(x_ref[...], w_ref, 0, cos_ref, sin_ref, spq, sigq, qf, tmp)
        near_attention(spq, spk_ref, vv_ref, mask_ref, near)

    return call(
        kernel,
        (x, w_q, spk, vv, mask, cosb, sinb),
        [VMEM_SPEC] * 7,
        [shape(rows, D, BF), shape(rows, D, F32), shape(rows, 2 * D, BF), shape(rows, 2 * D, F32)],
        [pltpu.VMEM((rows, D), F32)],
        f"near_{layer}",
        3,
    )


def ffn_scratch(rows):
    return [
        pltpu.VMEM((D, D), BF),
        pltpu.VMEM((D, FF), BF),
        pltpu.VMEM((FF, D), BF),
        pltpu.VMEM((16, D), F32),
        pltpu.VMEM((rows, D), F32),
        pltpu.VMEM((rows, D), F32),
        pltpu.SemaphoreType.DMA((3,)),
    ]


def run_forward(layer, x, near, qf, recvs, params, weights):
    rows = x.shape[0]
    outs = (
        [shape(rows, D, F32)] * 2
        + [shape(rows, D, BF), shape(rows, D, F32), shape(rows, 128, F32), shape(rows, D, BF)]
        + [shape(rows, FF, BF)] * 2
        + [shape(rows, D, F32), shape(rows, 128, F32), shape(272, 256, F32), shape(rows, D, BF)]
    )
    count = len(recvs)

    def kernel(*refs):
        core = lax.axis_index("section")
        x_ref, near_ref, qf_ref, own_p, other_p = refs[:5]
        recv_refs = refs[5 : 5 + count]
        w = refs[5 + count : 11 + count]
        out_refs = refs[11 + count : 23 + count]
        held_out, held_up, held_down, params_ref, tmp, tmp_up, sems = refs[23 + count :]
        waits = load_weights(
            core, layer, [(w[0], w[1], held_out, 1), (w[2], w[3], held_up, 1), (w[4], w[5], held_down, 1)], sems
        )
        params_ref[...] = jnp.where(core == layer, own_p[...], other_p[...])
        attend_and_ffn(
            x_ref, near_ref, qf_ref, recv_refs, params_ref, held_out, held_up, held_down, waits, out_refs, tmp, tmp_up
        )

    return call(
        kernel,
        (x, near, qf, *params, *recvs, *weights),
        [VMEM_SPEC] * (5 + count) + [HBM_SPEC] * 6,
        outs,
        ffn_scratch(rows),
        f"forward_{layer}",
        5,
        20,
    )


def run_ffn_backward(layer, sources, kept, params, weights):
    rows = sources[-1].shape[0]
    count = len(sources)
    outs = (
        [shape(rows, D, BF), shape(rows, FF, BF), shape(rows, D, BF), shape(rows, D, F32)]
        + [shape(rows, D, BF)] * 3
        + [shape(16, D, F32), shape(272, 256, BF)]
    )

    def kernel(*refs):
        core = lax.axis_index("section")
        att, rden, qf, hat1, scale1, gprime, hat2, scale2, own_p, other_p = refs[count : count + 10]
        w = refs[count + 10 : count + 16]
        out_refs = refs[count + 16 : count + 25]
        held_out, held_up, held_down, params_ref, tmp, tmp_up, sems = refs[count + 25 :]

        def grad_fn(s):
            if count == 1:
                return refs[0][s, :].astype(F32)
            return own_rows(refs[0], refs[1], s).astype(F32)

        waits = load_weights(
            core, layer, [(w[4], w[5], held_down, 1), (w[2], w[3], held_up, 1), (w[0], w[1], held_out, 1)], sems
        )
        params_ref[...] = jnp.where(core == layer, own_p[...], other_p[...])
        ffn_backward(
            grad_fn, att, rden, qf, hat1, scale1, gprime, hat2, scale2, params_ref,
            held_out, held_up, held_down, waits, out_refs, tmp, tmp_up,
        )

    return call(
        kernel,
        (*sources, *kept, *params, *weights),
        [VMEM_SPEC] * (10 + count) + [HBM_SPEC] * 6,
        outs,
        ffn_scratch(rows),
        f"ffn_backward_{layer}",
        5,
        20,
    )


def run_ffn_grads(layer, normed, hidden, d_ffn, d_up):
    return call(
        functools.partial(ffn_weight_grads, layer),
        (normed, hidden, d_ffn, d_up),
        [VMEM_SPEC] * 4,
        [shape(4 * D, D, BF)] * 2,
        [],
        f"ffn_grads_{layer}",
        4,
    )


def run_near_backward(layer, spq, spk, vv, r_low, t_high, t_low, mask, mask_t):
    def kernel(*refs):
        near_backward(*refs[:8], refs[8:])

    return call(
        kernel,
        (spq, spk, vv, r_low, t_high, t_low, mask, mask_t),
        [VMEM_SPEC] * 8,
        [shape(spq.shape[0], D, F32)] * 3,
        [],
        f"near_backward_{layer}",
        4,
    )


def run_attention_backward(layer, x, kept, near, recvs, fixed, rest, w_own, w_other):
    rows = x.shape[0]
    count = len(recvs)

    def kernel(*refs):
        x_ref, vv, sigq, sigk, kf, r_low, t_high, t_low, prefix = refs[:9]
        near_refs = refs[9:12]
        recv_refs = refs[12 : 12 + count]
        cosb, sinb, d_pre_one, mixed, d_branch, smalls, own, other = refs[12 + count : 20 + count]
        d_in, grads_kept, grads_sent, held, d_qkv, sems = refs[20 + count :]
        (wait,) = load_weights(lax.axis_index("section"), layer, [(own, other, held, 1)], sems)
        attention_backward(
            layer, x_ref, vv, sigq, sigk, kf, r_low, t_high, t_low, prefix, near_refs, recv_refs, cosb, sinb,
            d_pre_one, mixed, d_branch, smalls, held, wait, (d_in, grads_kept, grads_sent), d_qkv,
        )

    return call(
        kernel,
        (x, *kept, *near, *recvs, *fixed, *rest, w_own, w_other),
        [VMEM_SPEC] * (18 + count) + [HBM_SPEC] * 2,
        [shape(rows, D, BF)] + [shape(2 * D + SMALL, D, BF)] * 2,
        [pltpu.VMEM((D, 3 * D), BF), pltpu.VMEM((rows, 3 * D), BF), pltpu.SemaphoreType.DMA((1,))],
        f"attention_backward_{layer}",
        5,
        20,
    )


def combine(kept, received, tail, last, name):
    rows = kept.shape[0] - (SMALL if tail else 0)
    next_rows = rows if last else rows // 2
    count = 1 if last else 2

    def kernel(kept_ref, received_ref, *outs):
        for i, out in enumerate(outs):
            s = slice(i * next_rows, (i + 1) * next_rows)
            out[:next_rows, :] = (kept_ref[s, :].astype(F32) + received_ref[s, :].astype(F32)).astype(BF)
            if tail:
                put_smalls(out, next_rows, get_smalls(kept_ref, rows) + get_smalls(received_ref, rows))

    out_rows = next_rows + (SMALL if tail else 0)
    return call(
        kernel,
        (kept, received),
        [VMEM_SPEC] * 2,
        [shape(out_rows, kept.shape[1], BF)] * count,
        [],
        name,
        1,
    )


def join(a, b, name):
    def kernel(a_ref, b_ref, out):
        out[: a.shape[0], :] = a_ref[...]
        out[a.shape[0] :, :] = b_ref[...]

    return call(kernel, (a, b), [VMEM_SPEC] * 2, [shape(a.shape[0] + b.shape[0], D, BF)], [], name, 1)[0]


def split_sums(joined, received, ffn_rows, other_rows, name):
    def kernel(joined_ref, received_ref, ffn, other, smalls):
        for out, start, rows in ((ffn, 0, ffn_rows), (other, ffn_rows, other_rows)):
            s = slice(start, start + rows)
            out[...] = (joined_ref[s, :].astype(F32) + received_ref[s, :].astype(F32)).astype(BF)
        start = ffn_rows + other_rows
        smalls[...] = get_smalls(joined_ref, start) + get_smalls(received_ref, start)

    return call(
        kernel,
        (joined, received),
        [VMEM_SPEC] * 2,
        [shape(ffn_rows, D, BF), shape(other_rows, D, BF), shape(16, D, F32)],
        [],
        name,
        1,
    )


def by_core(zero, one, name, both=True):
    rows = [block.shape[0] for block in zero]

    def kernel(*refs):
        core = lax.axis_index("section")
        outs = refs[4:]
        for out, wanted in zip(outs, (0, 1) if both else (1,)):
            for layer in range(2):

                @pl.when(core == (layer if wanted == 0 else 1 - layer))
                def _(out=out, layer=layer):
                    out[: rows[0], :] = refs[2 * layer][...]
                    out[rows[0] :, :] = refs[2 * layer + 1][...]

    count = 2 if both else 1
    return call(kernel, (*zero, *one), [VMEM_SPEC] * 4, [shape(sum(rows), D, BF)] * count, [], name, 1)


def small_gradients(zero, one):
    def kernel(zero_ref, one_ref, *outs):
        small = jnp.where(lax.axis_index("section") == 0, zero_ref[...], one_ref[...])
        for i in range(5):
            outs[i][...] = small[i : i + 1, :]
        for c in range(FF // D):
            outs[5][:, c * D : (c + 1) * D] = small[5 + c : 6 + c, :]

    return call(
        kernel, (zero, one), [VMEM_SPEC] * 2, [shape(1, D, F32)] * 5 + [shape(1, FF, F32)], [], "small_gradients", 1
    )


def unpack(blocks, second, arrays, name):
    given = []
    for block in blocks:
        if isinstance(block, list):
            given += [part for pair in block for part in pair]
        elif block is not None:
            given.append(block)
    ffn_total, other_total = 4 * D, 2 * D
    sizes = (chunk_rows(ffn_total), chunk_rows(other_total))
    count = ffn_total // sizes[0] // 2
    out_shapes = [shape(D, FF, F32), shape(FF, D, F32), shape(D, 3 * D, F32), shape(D, D, F32)]

    def kernel(*refs):
        refs = list(refs)
        sources = [refs.pop(0) for _ in given]
        if arrays is not None:
            del refs[:4]
        up, down, qkv, out, held_ffn, held_other, sem_ffn, sem_other = refs
        core = lax.axis_index("section")
        slot = 0
        waits = []
        for block_place, block in enumerate(blocks):
            if block is None:
                continue
            pairs = [sources.pop(0) for _ in range(4)] if isinstance(block, list) else None
            source = None if pairs else sources.pop(0)
            half = core if block_place == 0 else 1 - core
            for part, size, held, sems in ((0, sizes[0], held_ffn, sem_ffn), (1, sizes[1], held_other, sem_other)):
                ids = part_ids(part)
                number = jnp.where(half == 0, ids[0], ids[1])
                base = 0 if part == 0 else ffn_total // 2
                for k in range(count):
                    index = slot * count + k
                    rows = slice(k * size, (k + 1) * size)
                    if pairs is None:
                        held[index] = source[base + k * size : base + (k + 1) * size, :].astype(F32)
                    else:
                        for layer in range(2):

                            @pl.when(core == layer)
                            def _(index=index, rows=rows, held=held, part_ref=pairs[2 * layer + part]):
                                held[index] = part_ref[rows, :].astype(F32)

                    chunk = jnp.bitwise_xor(k + (count if second else 0), number)
                    row = chunk * size
                    if part == 0:
                        piece, sub = lax.div(row, D), lax.rem(row, D)

                        @pl.when(piece < 2)
                        def _(piece=piece, sub=sub, index=index, half=half, held=held, sems=sems, size=size):
                            cols = pl.ds(pl.multiple_of((2 * half + piece) * D, D), D)
                            to = up.at[pl.ds(pl.multiple_of(sub, size), size), cols]
                            pltpu.make_async_copy(held.at[index], to, sems.at[index]).start()

                        @pl.when(piece >= 2)
                        def _(piece=piece, sub=sub, index=index, half=half, held=held, sems=sems, size=size):
                            start = pl.multiple_of((2 * half + piece - 2) * D + sub, size)
                            to = down.at[pl.ds(start, size), :]
                            pltpu.make_async_copy(held.at[index], to, sems.at[index]).start()

                        waits.append((held.at[index], down.at[pl.ds(0, size), :], sems.at[index]))
                    else:
                        piece, sub = lax.div(row, D // 2), lax.rem(row, D // 2)
                        start = pl.multiple_of(half * (D // 2) + sub, size)

                        @pl.when(piece < 3)
                        def _(piece=piece, start=start, index=index, held=held, sems=sems, size=size):
                            to = qkv.at[pl.ds(start, size), pl.ds(pl.multiple_of(piece * D, D), D)]
                            pltpu.make_async_copy(held.at[index], to, sems.at[index]).start()

                        @pl.when(piece == 3)
                        def _(start=start, index=index, held=held, sems=sems, size=size):
                            to = out.at[pl.ds(start, size), :]
                            pltpu.make_async_copy(held.at[index], to, sems.at[index]).start()

                        waits.append((held.at[index], out.at[pl.ds(0, size), :], sems.at[index]))
            slot += 1
        for wait in waits:
            pltpu.make_async_copy(*wait).wait()

    total = sum(block is not None for block in blocks) * count
    return pl.pallas_call(
        kernel,
        out_shape=tuple(out_shapes),
        in_specs=[VMEM_SPEC] * len(given) + ([ANY_SPEC] * 4 if arrays is not None else []),
        out_specs=(ANY_SPEC,) * 4,
        scratch_shapes=[
            pltpu.VMEM((total, sizes[0], D), F32),
            pltpu.VMEM((total, sizes[1], D), F32),
            pltpu.SemaphoreType.DMA((total,)),
            pltpu.SemaphoreType.DMA((total,)),
        ],
        input_output_aliases={} if arrays is None else {len(given) + k: k for k in range(4)},
        compiler_params=pltpu.CompilerParams(vmem_limit_bytes=24 * MIB),
        cost_estimate=pl.CostEstimate(flops=FLOPS, bytes_accessed=1 << 10, transcendentals=0),
        name=name,
    )(*given, *(arrays or ()))


def swap_cores(block):
    return lax.ppermute(block, "section", [(0, 1), (1, 0)])


def from_chips(message):
    length = lax.axis_size("seq") // 2
    received = []
    for distance in range(1, length):
        route = [(base + j, base + (j + distance) % length) for base in (0, length) for j in range(length)]
        received.append(lax.ppermute(message, "seq", route))
    return received


def from_cores(message, received):
    return received + [swap_cores(message)] + [swap_cores(m) for m in received]


def halves_route(cores):
    length = lax.axis_size("seq") // 2
    route = []
    for j in range(length):
        route.append((2 * (j + length) + cores[0][0], 2 * j + cores[0][1]))
        route.append((2 * j + cores[1][0], 2 * (j + length) + cores[1][1]))
    return route


def pick_rows(tokens, cotangent):
    rows = tokens.shape[1]

    def kernel(*refs):
        _, lower, _, _ = place()
        sems = refs[4]
        index = jnp.where(lower, 1, 0)
        copies = [pltpu.make_async_copy(refs[k].at[index], refs[2 + k], sems.at[k]) for k in range(2)]
        for copy in copies:
            copy.start()
        for copy in copies:
            copy.wait()

    return call(
        kernel, (tokens, cotangent), [HBM_SPEC] * 2, [shape(rows, D, BF)] * 2,
        [pltpu.SemaphoreType.DMA((2,))], "pick_rows", 1, pinned=(0, 1),
    )


def own_rows(whole_ref, far_ref, s=slice(None)):
    _, lower, _, _ = place()
    return jnp.where(stays(), whole_ref[jnp.where(lower, 0, 1), s, :], far_ref[s, :])


def stays():
    core, lower, _, _ = place()
    return (core == 0) == lower


def swap_halves(block):
    return lax.ppermute(block, ("seq", "section"), halves_route(((1, 1), (0, 0))))


def place_rows(firsts, seconds, name):
    count = len(firsts)
    rows, width = firsts[0].shape
    half = count * rows

    def stack(*refs):
        _, lower, _, _ = place()
        out, hop = refs[2 * count :]
        for k in range(2 * count):
            out[k * rows : (k + 1) * rows, :] = refs[k][...]
        for k in range(count):
            hop[k * rows : (k + 1) * rows, :] = jnp.where(lower, refs[count + k][...], refs[k][...])

    both, hop = call(
        stack, (*firsts, *seconds), [VMEM_SPEC] * 2 * count, [shape(2 * half, width, BF), shape(half, width, BF)],
        [], f"stack_{name}", 1,
    )
    far = lax.ppermute(both, ("seq", "section"), halves_route(((0, 0), (1, 0))))

    def finish(far):
        def kernel(both_ref, hop_ref, far_ref, far_second_ref, *outs):
            core, lower, _, _ = place()
            for k, out in enumerate(outs):
                s = slice(k * rows, (k + 1) * rows)
                own = jnp.where(core == 0, both_ref[s, :], both_ref[half + k * rows : half + (k + 1) * rows, :])
                local = jnp.where((core == 0) == lower, own, hop_ref[s, :])
                remote = jnp.where(core == 0, far_ref[s, :], far_second_ref[s, :])
                out[0, :, :] = jnp.where(lower, local, remote)
                out[1, :, :] = jnp.where(lower, remote, local)

        far_second = lax.ppermute(far[half:], "section", [(0, 1)])
        outs = [jax.ShapeDtypeStruct((2, rows, width), BF)] * count
        placed = call(kernel, (both, swap_cores(hop), far, far_second), [VMEM_SPEC] * 4, outs, [], f"place_{name}", 1)
        return [out[None] for out in placed]

    return far, finish


def exchange(block, layer, part, step):
    routes = []
    dp, seq = lax.axis_size("dp"), lax.axis_size("seq")
    for core, order in enumerate(orders_of(part)):
        axis, i = order[step]
        for a in range(dp):
            for b in range(seq):
                to = (a ^ (1 << i), b) if axis == "dp" else (a, b ^ (1 << i))
                routes.append(((a * seq + b) * 2 + core, (to[0] * seq + to[1]) * 2 + core))
    return lax.ppermute(block, ("dp", "seq", "section"), routes)


def exchange_last(block):
    _, (axis, i) = partner_bits()
    return lax.ppermute(block, axis, [(j, j ^ (1 << i)) for j in range(lax.axis_size(axis))])


def tie(*trees):
    return lax.optimization_barrier(trees)


class PartSum:
    def __init__(self, layer, part, kept, sent):
        self.name = f"{layer}_{part}"
        self.layer, self.part = layer, part
        self.kept, self.sent = kept, sent
        self.step = -1

    def send(self):
        self.received = swap_cores(self.sent) if self.step < 0 else exchange(self.sent, self.layer, self.part, self.step)

    def add(self):
        last = self.step == len(partner_bits()[0]) - 1
        result = combine(self.kept, self.received, self.part == 1, last, f"add_{self.name}_{self.step + 1}")
        self.kept, self.sent = result[0], result[-1]
        self.step += 1


EVENTS = (
    "B0", "F1.s0", "F0.w", "C1.s0", "C0.w", "F1.s1", "ra", "C1.s1", "C1.s2", "F1.s2", "F0.s0", "C0.s0", "Z1", "C0.s1", "F0.s1", "C1.a2",
    "F1.a2", "F0.s2", "C0.s2", "C1.a1", "F1.a1", "Z0", "C1.a0", "C0.a2", "F0.a2", "F0.a1", "rs", "F1.a0", "C0.a1", "small", "pa", "pre",
    "unpack", "C0.a0", "rd", "F0.a0", "pd",
)


def default_events(steps):
    events = ["B0", "F0.w", "C0.w"]
    for layer in (1, 0):
        events += [f"{part}{layer}.s{step}" for step in range(steps) for part in ("F", "C")] + [f"Z{layer}"]
    events += ["ra", "pa", "rs", "rd", "pd"]
    for step in reversed(range(steps)):
        events += ["small", "pre", "unpack"] if step == 0 else []
        events += [f"{part}{layer}.a{step}" for layer in (1, 0) for part in ("F", "C")]
    return events


class Sums:
    def __init__(self, parts):
        self.parts = parts
        self.steps = len(partner_bits()[0])
        self.token = None
        self.joined, self.far, self.smalls = {}, {}, {}
        self.whole, self.received = {}, {}

    def after(self, received):
        if self.token is not None:
            received, self.token = tie(received, self.token)
        return received

    def of(self, layer):
        return self.whole[f"F{layer}"], self.whole[f"C{layer}"]

    def last(self, layer):
        return self.received[f"F{layer}"], self.received[f"C{layer}"]

    def gather(self, name, step):
        if step >= 0:
            self.received[name] = exchange(self.whole[name], int(name[1]), "FC".index(name[0]), step)

    def process(self, event):
        if event[0] == "Z":
            layer = int(event[1])
            pair = self.parts[f"F{layer}"], self.parts[f"C{layer}"]
            rows = pair[0].kept.shape[0], pair[1].kept.shape[0] - SMALL
            far = self.after(self.far[layer])
            ffn, other, self.smalls[layer] = split_sums(self.joined[layer], far, *rows, f"split_{layer}")
            self.token = self.smalls[layer]
            for name, block in ((f"C{layer}", other), (f"F{layer}", ffn)):
                self.whole[name] = block
                self.gather(name, self.steps - 1)
            return
        name, kind = event.split(".")
        layer = int(name[1])
        if kind[0] == "a":
            step = int(kind[1:])
            received = self.after(self.received[name])
            self.received[name] = received
            if step == 0:
                self.token = received
                return
            self.whole[name] = join(self.whole[name], received, f"join_{name}_{step}")
            self.token = self.whole[name]
            self.gather(name, step - 1)
            return
        part = self.parts[name]
        part.received = self.after(part.received)
        part.add()
        self.token = part.kept
        if part.step < self.steps:
            part.send()
        pair = [self.parts.get(f"{p}{layer}") for p in "FC"]
        if all(p is not None and p.step == self.steps for p in pair):
            self.joined[layer] = join(pair[0].kept, pair[1].kept, f"join_{layer}")
            self.far[layer] = exchange_last(self.joined[layer])


def body(tokens, cotangent, w_qkv, w_out, first_norm_gain, ln1_bias, w_up, b_up, w_down, b_down, ln2_gain, ln2_bias):
    core, _, j, length = place()
    rows = tokens.shape[1]
    whole = rows * lax.axis_size("seq")
    step = math.pi / (2.0 * whole)
    sent, sent_cot = pick_rows(tokens, cotangent)
    far, far_cot = swap_halves(sent), swap_halves(sent_cot)
    vectors = (first_norm_gain, ln1_bias, b_down, ln2_gain, ln2_bias, b_up)
    sent, w_qkv, vectors = tie(sent, w_qkv, vectors)
    qkv_w = (w_qkv[0], swap_cores(w_qkv[0]))
    own_p = jnp.concatenate([*vectors[:5], vectors[5].reshape(4, D), jnp.zeros((7, D), F32)], axis=0)
    places = jnp.arange(rows, dtype=jnp.int32)
    angles = ((j + core * length) * rows + places).astype(F32) * step
    cosb = jnp.broadcast_to(jnp.cos(angles)[:, None], (rows, 128))
    sinb = jnp.broadcast_to(jnp.sin(angles)[:, None], (rows, 128))
    apart = places[:, None] - places[None, :]
    near = jnp.cos(apart.astype(F32) * step)
    mask = jnp.where(apart >= 0, near, 0.0)
    mask_t = jnp.where(apart <= 0, near, 0.0)

    far, own_p, mask, mask_t, cosb, sinb, qkv_w = tie(far, own_p, mask, mask_t, cosb, sinb, qkv_w)

    saved = []
    x = None
    for layer in range(2):
        projected = run_project(layer, (tokens, far) if layer == 0 else (x,), *qkv_w, cosb, sinb)
        spk, sigk, kf, vv, msg, x, w_q = projected
        if layer == 0:
            msg, own_p, own_w = tie(msg, own_p, (w_out[0], w_up[0], w_down[0]))
            other_w = tuple(swap_cores(w) for w in own_w)
            rest_w = (own_w[0], other_w[0], own_w[1], other_w[1], own_w[2], other_w[2])
            params = (own_p, swap_cores(own_p))
        recvs = from_chips(msg)
        spq, sigq, qf, near_sums = run_near(layer, x, w_q, spk, vv, mask, cosb, sinb)
        recvs, near_sums, far_cot = tie(recvs, near_sums, far_cot)
        recvs = from_cores(msg, recvs)
        forward = run_forward(layer, x, near_sums, qf, recvs, params, rest_w)
        saved.append((x, (spq, spk, vv, sigq, sigk, qf, kf, None), forward))
        x = forward[-1]
    outputs = (saved[0][2][-1], saved[1][2][-1])

    def ffn_part(layer, sources):
        x, (spq, spk, vv, sigq, sigk, qf, kf, _), forward = saved[layer]
        att, rden, mixed, hat1, scale1, normed, hidden, gprime, hat2, scale2, prefix, _ = forward
        d_ffn, d_up, d_branch, d_pre_one, r_low, t_high, t_low, small, msg = run_ffn_backward(
            layer, sources, (att, rden, qf, hat1, scale1, gprime, hat2, scale2), params, rest_w
        )
        recvs = from_chips(msg)
        sums = PartSum(layer, 0, *run_ffn_grads(layer, normed, hidden, d_ffn, d_up))
        return (r_low, t_high, t_low), (d_pre_one, mixed, d_branch, small), (msg, recvs), sums

    def near_part(layer, sides):
        _, (spq, spk, vv, _, _, _, _, _), _ = saved[layer]
        return run_near_backward(layer, spq, spk, vv, *sides, mask, mask_t)

    def attention_part(layer, sides, rest, near_grads, recvs):
        x, (_, _, vv, sigq, sigk, _, kf, _), forward = saved[layer]
        grad, kept, sent = run_attention_backward(
            layer, x, (vv, sigq, sigk, kf, *sides, forward[-2]), near_grads, recvs, (cosb, sinb), rest, *qkv_w
        )
        return grad, PartSum(layer, 1, kept, sent)

    sides, rest, (msg, recvs), ffn1 = ffn_part(1, (cotangent, far_cot))
    ffn1.send()
    near_grads = near_part(1, sides)
    near_grads, recvs, ffn1.received = tie(near_grads, recvs, ffn1.received)
    recvs = from_cores(msg, recvs)
    ffn1.add()
    recvs, ffn1.kept, ffn1.sent = tie(recvs, ffn1.kept, ffn1.sent)
    d_second, other1 = attention_part(1, sides, rest, near_grads, recvs)
    ffn1.send()
    other1.send()
    sides, rest, (msg, recvs), ffn0 = ffn_part(0, (d_second,))
    near_grads = near_part(0, sides)
    near_grads, recvs, other1.received = tie(near_grads, recvs, other1.received)
    recvs = from_cores(msg, recvs)
    other1.add()
    sums = Sums({"F1": ffn1, "C1": other1, "F0": ffn0})
    sums.token = other1.kept
    for event in EVENTS if sums.steps == 3 else default_events(sums.steps):
        if event == "B0":
            d_first, sums.parts["C0"] = attention_part(0, sides, rest, sums.after(near_grads), recvs)
            other0 = sums.parts["C0"]
            d_first, other0.sent, ffn0.sent, other1.sent, ffn1.received = tie(
                d_first, other0.sent, ffn0.sent, other1.sent, ffn1.received
            )
            sums.token = d_first
            ffn0.send()
            other1.send()
            other0.send()
            outputs_far, outputs_finish = place_rows((outputs[0],), (outputs[1],), "outputs")
        elif event == "ra":
            outputs_far = sums.after(outputs_far)
            sums.token = outputs_far
        elif event == "pa":
            (layer_outputs,) = outputs_finish(sums.after(outputs_far))
            sums.token = layer_outputs
        elif event == "rs":
            d_first = sums.after(d_first)
            inputs_far, inputs_finish = place_rows((d_first,), (d_second,), "inputs")
        elif event == "rd":
            inputs_far = sums.after(inputs_far)
            sums.token = inputs_far
        elif event == "pd":
            (input_grads,) = inputs_finish(sums.after(inputs_far))
            sums.token = input_grads
        elif event == "pre":
            mine, theirs = by_core(sums.of(0), sums.of(1), "by_core_0")
            hop = swap_cores(theirs)
        elif event == "small":
            small = small_gradients(sums.smalls[0], sums.after(sums.smalls[1]))
            sums.token = small[0]
        elif event == "unpack":
            arrays = unpack((mine, sums.after(hop)), False, None, "unpack_0")
            sums.token = arrays[3]
        else:
            sums.process(event)
    d_gain1, d_bias1, d_b_down, d_gain2, d_bias2, d_b_up = small
    zero, one = sums.last(0), sums.last(1)
    (theirs,) = by_core(zero, one, "by_core_1", False)
    arrays = unpack(([zero, one], None), True, arrays, "unpack_1")
    grad_up, grad_down, grad_qkv, grad_out = unpack((None, swap_cores(theirs)), True, arrays, "unpack_2")
    return (
        layer_outputs,
        input_grads,
        grad_qkv[None],
        grad_out[None],
        d_gain1,
        d_bias1,
        grad_up[None],
        d_b_up,
        grad_down[None],
        d_b_down,
        d_gain2,
        d_bias2,
    )


def solution(mesh):
    rows = P("dp", "seq", None)
    matrix = P("section", None, None)
    vector = P("section", None)
    out_rows = P("section", "dp", "seq", None)
    return jax.shard_map(
        body,
        mesh=mesh,
        in_specs=(rows, rows, matrix, matrix, vector, vector, matrix, vector, matrix, vector, vector, vector),
        out_specs=(
            out_rows, out_rows, matrix, matrix, vector, vector, matrix, vector, matrix, vector, vector, vector,
        ),
        check_vma=False,
    )
```

```python
import functools
import math

import jax
import jax.numpy as jnp
from jax import lax
from jax.experimental import pallas as pl
from jax.experimental.pallas import tpu as pltpu
from jax.sharding import PartitionSpec as P

D = 512
HEADS = 8
HEAD_DIM = 64
FF = 2048
PAIRS = HEADS // 2
EPS = 1e-05
BF = jnp.bfloat16
F32 = jnp.float32
MIB = 1024 * 1024
FLOPS = 1 << 20


def dot(a, b):
    return lax.dot_general(a, b, (((1,), (0,)), ((), ())), preferred_element_type=F32)


def dot_nt(a, b):
    return lax.dot_general(a, b, (((1,), (1,)), ((), ())), preferred_element_type=F32)


def dot_tn(a, b):
    return lax.dot_general(a, b, (((0,), (0,)), ((), ())), preferred_element_type=F32)


def low_half(rows, lanes):
    place = lax.broadcasted_iota(jnp.int32, (rows, lanes), 1)
    return lax.rem(place, 128) < HEAD_DIM


def block_diag(pair):
    rows, lanes = pair.shape
    low = low_half(rows, lanes)
    zero = jnp.zeros_like(pair)
    return jnp.concatenate([jnp.where(low, pair, zero), jnp.where(low, zero, pair)], axis=0)


def pair_cols(ref, g, width=128):
    return ref[:, g * width : (g + 1) * width]


def value_block(v_pair):
    ones = jnp.ones_like(v_pair)
    return jnp.concatenate([block_diag(v_pair), block_diag(ones)], axis=1)


def pack_message(blocks, keys):
    places = lax.broadcasted_iota(jnp.int32, (16, 256), 0)
    tail = jnp.zeros((16, 256), F32)
    for g in range(PAIRS):
        tail = jnp.where(places == g, jnp.broadcast_to(keys[g], (16, 256)), tail)
    return jnp.concatenate(list(blocks) + [tail], axis=0).astype(BF)


def place():
    length = lax.axis_size("seq") // 2
    z = lax.axis_index("seq")
    lower = z < length
    return lax.axis_index("section"), lower, jnp.where(lower, z, z - length), length


def sum_messages(refs, backward):
    core, _, j, length = place()
    total = jnp.zeros(refs[0].shape, F32)
    for i, ref in enumerate(refs):
        distance = i + 1
        if distance < length:
            wanted = j < distance if backward else j >= distance
        else:
            wanted = core == (0 if backward else 1)
        total = total + jnp.where(wanted, ref[...].astype(F32), 0.0)
    return total


CHUNK = 32


def each_rows(rows, fn, carry=None, unroll=False):
    if unroll:
        for r in range(0, rows, CHUNK):
            carry = fn(slice(r, r + CHUNK), carry)
        return carry

    def one(i, carry):
        return fn(pl.ds(pl.multiple_of(i * CHUNK, CHUNK), CHUNK), carry)

    return lax.fori_loop(0, rows // CHUNK, one, carry)


def row_mean(values):
    return jnp.sum(values, axis=-1, keepdims=True) * (1.0 / values.shape[-1])


def softplus_part(x, w_ref, part, cosb, sinb, sp_ref, sig_ref, f_ref, tmp, unroll=False):
    tmp[...] = dot(x, w_ref[:, part * D : (part + 1) * D])

    def soften(s, _):
        raw = tmp[s, :]
        tail = jnp.exp(-jnp.abs(raw))
        soft = jnp.maximum(raw, 0.0) + jnp.log1p(tail)
        sig = jnp.where(raw >= 0.0, 1.0, tail) / (1.0 + tail)
        sp_ref[s, :] = soft.astype(BF)
        sig_ref[s, :] = sig
        cos_rows = cosb[s, :]
        sin_rows = sinb[s, :]
        for g in range(PAIRS):
            pair = soft[:, 128 * g : 128 * (g + 1)]
            f_ref[s, 256 * g : 256 * g + 128] = (pair * cos_rows).astype(BF)
            f_ref[s, 256 * g + 128 : 256 * (g + 1)] = (pair * sin_rows).astype(BF)

    each_rows(x.shape[0], soften, unroll=unroll)


def project_keys(x, w_ref, waits, cosb, sinb, outs, tmp):
    spk, sigk, kf, vv, msg = outs
    waits[1]()
    softplus_part(x, w_ref, 1, cosb, sinb, spk, sigk, kf, tmp, True)
    waits[2]()
    vv[...] = dot(x, w_ref[:, 2 * D : 3 * D]).astype(BF)
    low = low_half(64, 256)
    blocks, keys = [], []
    for g in range(PAIRS):
        kf_g = pair_cols(kf, g, 256)
        full = dot_tn(pair_cols(vv, g), kf_g)
        blocks.append(jnp.where(low, full[:64], full[64:]))
        keys.append(jnp.sum(kf_g.astype(F32), axis=0, keepdims=True))
    msg[...] = pack_message(blocks, keys)


def state_block(total, g):
    low = low_half(64, 256)
    block = total[64 * g : 64 * (g + 1), :]
    keys = jnp.broadcast_to(total[256 + g : 257 + g, :], (64, 256))
    zero = jnp.zeros((64, 256), F32)
    return jnp.concatenate(
        [
            jnp.where(low, block, zero),
            jnp.where(low, zero, block),
            jnp.where(low, keys, zero),
            jnp.where(low, zero, keys),
        ],
        axis=0,
    ).astype(BF)


def norm_forward(tmp, gain, bias, hat_ref, scale_ref, out_fn):

    def norm(s, _):
        values = tmp[s, :]
        centered = values - row_mean(values)
        scale = lax.rsqrt(row_mean(centered * centered) + EPS)
        hat = centered * scale
        hat_ref[s, :] = hat
        scale_ref[s, :] = jnp.broadcast_to(scale, (32, 128))
        out_fn(s, hat * gain + bias)

    each_rows(tmp.shape[0], norm, unroll=True)


def near_attention(spq, spk, vv, mask, near):
    mask2 = jnp.concatenate([mask[...], mask[...]], axis=1)
    for g in range(PAIRS):
        scores = dot_nt(pair_cols(spq, g), block_diag(pair_cols(spk, g))) * mask2
        near[:, 256 * g : 256 * (g + 1)] = dot(scores.astype(BF), value_block(pair_cols(vv, g)))


def attend_and_ffn(x, near, qf, recvs, params, w_out, w_up, w_down, waits, outs, tmp, tmp_up):
    att, rden, mixed, hat1, scale1, normed, hidden, gprime, hat2, scale2, prefix, result = outs
    rows = x.shape[0]
    total = sum_messages(recvs, False)
    prefix[...] = total
    for g in range(PAIRS):
        both = pair_cols(near, g, 256) + dot_nt(pair_cols(qf, g, 256), state_block(total, g))
        inverse = 1.0 / both[:, 128:]
        attended = both[:, :128] * inverse
        cols = slice(128 * g, 128 * (g + 1))
        att[:, cols] = attended
        rden[:, cols] = inverse
        mixed[:, cols] = attended.astype(BF)
    gain1, bias1, b_down, gain2, bias2 = (params[i : i + 1, :] for i in range(5))
    waits[0]()
    tmp[...] = x[...].astype(F32) + dot(mixed[...], w_out[...])

    def put_normed(s, value):
        normed[s, :] = value.astype(BF)
        tmp[s, :] = value

    norm_forward(tmp, gain1, bias1, hat1, scale1, put_normed)
    waits[1]()
    for c in range(FF // D):
        cols = slice(c * D, (c + 1) * D)
        tmp_up[...] = dot(normed[...], w_up[:, cols])
        b_up = params[5 + c : 6 + c, :]

        def activate(s, _, cols=cols, b_up=b_up):
            up = tmp_up[s, :] + b_up
            cdf = 0.5 + 0.5 * lax.erf(up * (1.0 / math.sqrt(2.0)))
            density = jnp.exp(-0.5 * up * up) * (1.0 / math.sqrt(2.0 * math.pi))
            hidden[s, cols] = (up * cdf).astype(BF)
            gprime[s, cols] = (cdf + up * density).astype(BF)

        each_rows(rows, activate, unroll=True)
    waits[2]()
    tmp[...] = tmp[...] + b_down + dot(hidden[...], w_down[...])

    def put_result(s, value):
        result[s, :] = value.astype(BF)

    norm_forward(tmp, gain2, bias2, hat2, scale2, put_result)


def column_sum(values):
    return jnp.sum(values, axis=0, keepdims=True)


def norm_backward(grad_fn, gain, hat_ref, scale_ref, rows, put, extras=0):
    def norm(s, sums):
        grad = grad_fn(s)
        hat = hat_ref[s, :]
        scaled = grad * gain
        first = row_mean(scaled)
        second = row_mean(scaled * hat)
        scale = scale_ref[s, :][:, :1]
        extra = put(s, (scaled - first - hat * second) * scale)
        new = (column_sum(grad * hat), column_sum(grad)) + extra
        return tuple(a + b for a, b in zip(sums, new))

    zero = jnp.zeros((1, D), F32)
    return each_rows(rows, norm, (zero,) * (2 + extras), True)


def ffn_backward(grad_fn, att, rden, qf, hat1, scale1, gprime, hat2, scale2, params, w_out, w_up, w_down, waits, outs, tmp, tmp_up):
    d_ffn, d_up, d_branch, d_pre_one, r_low, t_high, t_low, smalls, msg = outs
    rows = att.shape[0]
    gain1, gain2 = params[0:1, :], params[3:4, :]

    def put_two(s, value):
        rounded = value.astype(BF)
        tmp[s, :] = value
        d_ffn[s, :] = rounded
        return (column_sum(rounded.astype(F32)),)

    d_gain2, d_bias2, d_b_down = norm_backward(
        grad_fn, gain2, hat2, scale2, rows, put_two, 1
    )
    waits[0]()
    b_up = []
    for c in range(FF // D):
        cols = slice(c * D, (c + 1) * D)
        tmp_up[...] = dot_nt(d_ffn[...], w_down[cols, :])

        def scale_up(s, total, cols=cols):
            value = (tmp_up[s, :] * gprime[s, cols].astype(F32)).astype(BF)
            d_up[s, cols] = value
            return total + column_sum(value.astype(F32))

        b_up.append(each_rows(rows, scale_up, jnp.zeros((1, D), F32), True))
    waits[1]()
    tmp[...] = tmp[...] + dot_nt(d_up[...], w_up[...])

    def put_one(s, value):
        d_pre_one[s, :] = value
        d_branch[s, :] = value.astype(BF)
        return ()

    d_gain1, d_bias1 = norm_backward(lambda s: tmp[s, :], gain1, hat1, scale1, rows, put_one)
    waits[2]()
    tmp[...] = dot_nt(d_branch[...], w_out[...])

    def scores(s, _):
        rounded = (tmp[s, :] * rden[s, :]).astype(BF)
        product = -(rounded.astype(F32) * att[s, :])
        high = product.astype(BF)
        r_low[s, :] = rounded
        t_high[s, :] = high
        t_low[s, :] = (product - high.astype(F32)).astype(BF)

    each_rows(rows, scores, unroll=True)
    low = low_half(64, 256)
    blocks, keys = [], []
    for g in range(PAIRS):
        sides = jnp.concatenate([pair_cols(r_low, g), pair_cols(t_high, g)], axis=1)
        full = dot_tn(sides, pair_cols(qf, g, 256))
        blocks.append(jnp.where(low, full[:64], full[64:128]))
        keys.append(column_sum(jnp.where(low, full[128:192], full[192:])))
    msg[...] = pack_message(blocks, keys)
    smalls[...] = jnp.concatenate(
        [d_gain1, d_bias1, d_b_down, d_gain2, d_bias2] + b_up + [jnp.zeros((7, D), F32)], axis=0
    )


def near_backward(spq, spk, vv, r_low, t_high, t_low, mask, mask_t, outs):
    near_q, near_k, near_v = outs
    mask2 = jnp.concatenate([mask[...], mask[...]], axis=1)
    mask_t2 = jnp.concatenate([mask_t[...], mask_t[...]], axis=1)
    for g in range(PAIRS):
        spq_g, spk_g, vv_g = pair_cols(spq, g), pair_cols(spk, g), pair_cols(vv, g)
        r_g, th_g, tl_g = pair_cols(r_low, g), pair_cols(t_high, g), pair_cols(t_low, g)
        values = value_block(vv_g)
        spk_diag, spq_diag, r_diag = block_diag(spk_g), block_diag(spq_g), block_diag(r_g)
        cols = slice(128 * g, 128 * (g + 1))
        d_scores = dot_nt(jnp.concatenate([r_g, th_g], axis=1), values) + dot_nt(tl_g, values[:, 128:])
        near_q[:, cols] = dot((d_scores * mask2).astype(BF), spk_diag)
        scores_t = (dot_nt(spk_g, spq_diag) * mask_t2).astype(BF)
        near_v[:, cols] = dot(scores_t, r_diag)
        d_scores_t = dot_nt(
            jnp.concatenate([vv_g, jnp.ones_like(vv_g)], axis=1),
            jnp.concatenate([r_diag, block_diag(th_g)], axis=1),
        )
        near_k[:, cols] = dot((d_scores_t * mask_t2).astype(BF), spq_diag)


def attention_backward(
    layer, x, vv, sigq, sigk, kf, r_low, t_high, t_low, prefix, near, recvs, cosb, sinb,
    d_pre_one, mixed, d_branch, smalls, w_qkv, wait, outs, d_qkv,
):
    d_in, kept, sent = outs
    near_q, near_k, near_v = near
    total = sum_messages(recvs, True)
    low = low_half(64, 256)
    for g in range(PAIRS):
        cols = slice(128 * g, 128 * (g + 1))
        vv_g = pair_cols(vv, g)
        sides = jnp.concatenate([pair_cols(r_low, g), pair_cols(t_high, g)], axis=1)
        state = state_block(prefix[...], g)
        d_feat = dot(sides, state) + dot(pair_cols(t_low, g), state[128:, :])
        d_soft_q = near_q[:, cols] + cosb[...] * d_feat[:, :128] + sinb[...] * d_feat[:, 128:]
        block = total[64 * g : 64 * (g + 1), :]
        zero = jnp.zeros_like(block)
        later = jnp.concatenate([jnp.where(low, block, zero), jnp.where(low, zero, block)], axis=0).astype(BF)
        d_value = near_v[:, cols] + dot_nt(pair_cols(kf, g, 256), later)
        d_feat_k = dot(vv_g, later) + total[256 + g : 257 + g, :]
        d_soft_k = near_k[:, cols] + cosb[...] * d_feat_k[:, :128] + sinb[...] * d_feat_k[:, 128:]
        d_qkv[:, 128 * g : 128 * (g + 1)] = (pair_cols(sigq, g) * d_soft_q).astype(BF)
        d_qkv[:, D + 128 * g : D + 128 * (g + 1)] = (pair_cols(sigk, g) * d_soft_k).astype(BF)
        d_qkv[:, 2 * D + 128 * g : 2 * D + 128 * (g + 1)] = d_value.astype(BF)
    wait()
    d_in[...] = (d_pre_one[...] + dot_nt(d_qkv[...], w_qkv[...])).astype(BF)
    core = lax.axis_index("section")
    ids = part_ids(1)
    half_rows = D // 2
    for out, half in ((kept, core), (sent, 1 - core)):
        order = jnp.where(half == 0, ids[0], ids[1])
        start = pl.multiple_of(half * half_rows, half_rows)
        x_half = x[:, pl.ds(start, half_rows)]
        for j in range(3):
            store_chunks(out, j * half_rows, dot_tn(x_half, d_qkv[:, j * D : (j + 1) * D]).astype(BF), order, 4 * half_rows)
        value = dot_tn(mixed[:, pl.ds(start, half_rows)], d_branch[...]).astype(BF)
        store_chunks(out, 3 * half_rows, value, order, 4 * half_rows)
        put_smalls(out, 4 * half_rows, smalls[...])


def ffn_weight_grads(layer, normed, hidden, d_ffn, d_up, kept, sent):
    core = lax.axis_index("section")
    ids = part_ids(0)
    for out, half in ((kept, core), (sent, 1 - core)):
        order = jnp.where(half == 0, ids[0], ids[1])
        for j in range(2):
            start = pl.multiple_of(half * (FF // 2) + j * D, D)
            store_chunks(out, j * D, dot_tn(normed[...], d_up[:, pl.ds(start, D)]).astype(BF), order, 4 * D)
            value = dot_tn(hidden[:, pl.ds(start, D)], d_ffn[...]).astype(BF)
            store_chunks(out, (2 + j) * D, value, order, 4 * D)


def partner_bits():
    bits = [(axis, i) for axis in ("dp", "seq") for i in range(lax.axis_size(axis).bit_length() - 1)]
    last = bits.pop()
    return bits, last


def turned(bits, places):
    return bits[places:] + bits[:places]


def orders_of(part):
    bits, _ = partner_bits()
    third = max(1, len(bits) // 3)
    a, b, c = bits[:third], bits[third : 2 * third], bits[2 * third :]
    return [a + b + c, b + a + c] if part == 0 else [b + c + a, a + c + b]


def part_ids(part):
    ids = []
    for order in orders_of(part):
        number = jnp.int32(0)
        for axis, i in order:
            number = 2 * number + lax.rem(lax.div(lax.axis_index(axis), 1 << i), 2)
        ids.append(number)
    return ids


def chunk_rows(total):
    bits, _ = partner_bits()
    return total >> len(bits)


def store_chunks(out, first_row, value, number, total):
    size = chunk_rows(total)
    for i in range(value.shape[0] // size):
        chunk = first_row // size + i
        spot = pl.multiple_of(jnp.bitwise_xor(jnp.int32(chunk), number) * size, size)
        out[pl.ds(spot, size), :] = value[i * size : (i + 1) * size, :]


SMALL = 16
SMALL_ROWS = 5 + FF // D


def put_smalls(out, start, value):
    high = value.astype(BF).astype(F32)
    rest = (value - high)[: SMALL - SMALL_ROWS]
    out[start : start + SMALL, :] = jnp.concatenate([high[:SMALL_ROWS], rest], axis=0).astype(BF)


def get_smalls(ref, start):
    rows = ref[start : start + SMALL, :].astype(F32)
    left = SMALL - SMALL_ROWS
    zero = jnp.zeros((left, D), F32)
    rest = jnp.concatenate([rows[SMALL_ROWS:], jnp.zeros((SMALL_ROWS, D), F32)], axis=0)
    return jnp.concatenate([rows[:SMALL_ROWS], zero], axis=0) + rest


def load_weights(core, layer, pairs, sems):
    waits = []
    for own, other, held, parts in pairs:
        width = held.shape[1] // parts
        for p in range(parts):
            i = len(waits)
            cols = slice(p * width, (p + 1) * width)

            @pl.when(core == layer)
            def _(own=own, held=held, i=i, cols=cols):
                pltpu.make_async_copy(own.at[:, cols], held.at[:, cols], sems.at[i]).start()

            @pl.when(core != layer)
            def _(other=other, held=held, i=i, cols=cols):
                pltpu.make_async_copy(other.at[:, cols], held.at[:, cols], sems.at[i]).start()

            def wait(own=own, held=held, i=i, cols=cols):
                pltpu.make_async_copy(own.at[:, cols], held.at[:, cols], sems.at[i]).wait()

            waits.append(wait)
    return waits


def shape(rows, cols, kind):
    return jax.ShapeDtypeStruct((rows, cols), kind)


VMEM_SPEC = pl.BlockSpec(memory_space=pltpu.VMEM)
HBM_SPEC = pl.BlockSpec(memory_space=pltpu.HBM)
ANY_SPEC = pl.BlockSpec(memory_space=pl.ANY)


def call(kernel, args, specs, outs, scratch, name, micros, limit=16, pinned=()):
    if pinned:
        args = [pltpu.with_memory_space_constraint(a, pltpu.HBM) if i in pinned else a for i, a in enumerate(args)]
    return pl.pallas_call(
        kernel,
        out_shape=tuple(outs),
        in_specs=specs,
        out_specs=tuple(VMEM_SPEC for _ in outs),
        scratch_shapes=scratch,
        compiler_params=pltpu.CompilerParams(vmem_limit_bytes=limit * MIB),
        cost_estimate=pl.CostEstimate(flops=int(micros * FLOPS), bytes_accessed=1 << 10, transcendentals=0),
        name=name,
    )(*args)


def run_project(layer, sources, w_own, w_other, cosb, sinb):
    rows = sources[-1].shape[0]
    count = len(sources)
    outs = [shape(rows, D, BF), shape(rows, D, F32), shape(rows, 2 * D, BF), shape(rows, D, BF), shape(272, 256, BF)]
    outs += [shape(rows, D, BF), shape(D, D, BF)]

    def kernel(*refs):
        own, other, cos_ref, sin_ref = refs[count : count + 4]
        out_refs = refs[count + 4 : count + 4 + len(outs)]
        held, tmp, sems = refs[count + 4 + len(outs) :]
        waits = load_weights(lax.axis_index("section"), layer, [(own, other, held, 3)], sems)
        x = refs[0][...] if count == 1 else own_rows(refs[0], refs[1])
        out_refs[5][...] = x
        project_keys(x, held, waits, cos_ref, sin_ref, out_refs[:5], tmp)
        waits[0]()
        out_refs[6][...] = held[:, :D]

    return call(
        kernel,
        (*sources, w_own, w_other, cosb, sinb),
        [VMEM_SPEC] * count + [HBM_SPEC, HBM_SPEC, VMEM_SPEC, VMEM_SPEC],
        outs,
        [pltpu.VMEM((D, 3 * D), BF), pltpu.VMEM((rows, D), F32), pltpu.SemaphoreType.DMA((3,))],
        f"project_{layer}",
        3,
        pinned=(count,) if layer == 0 else (),
    )


def run_near(layer, x, w_q, spk, vv, mask, cosb, sinb):
    rows = x.shape[0]

    def kernel(x_ref, w_ref, spk_ref, vv_ref, mask_ref, cos_ref, sin_ref, spq, sigq, qf, near, tmp):
        softplus_part(x_ref[...], w_ref, 0, cos_ref, sin_ref, spq, sigq, qf, tmp)
        near_attention(spq, spk_ref, vv_ref, mask_ref, near)

    return call(
        kernel,
        (x, w_q, spk, vv, mask, cosb, sinb),
        [VMEM_SPEC] * 7,
        [shape(rows, D, BF), shape(rows, D, F32), shape(rows, 2 * D, BF), shape(rows, 2 * D, F32)],
        [pltpu.VMEM((rows, D), F32)],
        f"near_{layer}",
        3,
    )


def ffn_scratch(rows):
    return [
        pltpu.VMEM((D, D), BF),
        pltpu.VMEM((D, FF), BF),
        pltpu.VMEM((FF, D), BF),
        pltpu.VMEM((16, D), F32),
        pltpu.VMEM((rows, D), F32),
        pltpu.VMEM((rows, D), F32),
        pltpu.SemaphoreType.DMA((3,)),
    ]


def run_forward(layer, x, near, qf, recvs, params, weights):
    rows = x.shape[0]
    outs = (
        [shape(rows, D, F32)] * 2
        + [shape(rows, D, BF), shape(rows, D, F32), shape(rows, 128, F32), shape(rows, D, BF)]
        + [shape(rows, FF, BF)] * 2
        + [shape(rows, D, F32), shape(rows, 128, F32), shape(272, 256, F32), shape(rows, D, BF)]
    )
    count = len(recvs)

    def kernel(*refs):
        core = lax.axis_index("section")
        x_ref, near_ref, qf_ref, own_p, other_p = refs[:5]
        recv_refs = refs[5 : 5 + count]
        w = refs[5 + count : 11 + count]
        out_refs = refs[11 + count : 23 + count]
        held_out, held_up, held_down, params_ref, tmp, tmp_up, sems = refs[23 + count :]
        waits = load_weights(
            core, layer, [(w[0], w[1], held_out, 1), (w[2], w[3], held_up, 1), (w[4], w[5], held_down, 1)], sems
        )
        params_ref[...] = jnp.where(core == layer, own_p[...], other_p[...])
        attend_and_ffn(
            x_ref, near_ref, qf_ref, recv_refs, params_ref, held_out, held_up, held_down, waits, out_refs, tmp, tmp_up
        )

    return call(
        kernel,
        (x, near, qf, *params, *recvs, *weights),
        [VMEM_SPEC] * (5 + count) + [HBM_SPEC] * 6,
        outs,
        ffn_scratch(rows),
        f"forward_{layer}",
        5,
        20,
    )


def run_ffn_backward(layer, sources, kept, params, weights):
    rows = sources[-1].shape[0]
    count = len(sources)
    outs = (
        [shape(rows, D, BF), shape(rows, FF, BF), shape(rows, D, BF), shape(rows, D, F32)]
        + [shape(rows, D, BF)] * 3
        + [shape(16, D, F32), shape(272, 256, BF)]
    )

    def kernel(*refs):
        core = lax.axis_index("section")
        att, rden, qf, hat1, scale1, gprime, hat2, scale2, own_p, other_p = refs[count : count + 10]
        w = refs[count + 10 : count + 16]
        out_refs = refs[count + 16 : count + 25]
        held_out, held_up, held_down, params_ref, tmp, tmp_up, sems = refs[count + 25 :]

        def grad_fn(s):
            if count == 1:
                return refs[0][s, :].astype(F32)
            return own_rows(refs[0], refs[1], s).astype(F32)

        waits = load_weights(
            core, layer, [(w[4], w[5], held_down, 1), (w[2], w[3], held_up, 1), (w[0], w[1], held_out, 1)], sems
        )
        params_ref[...] = jnp.where(core == layer, own_p[...], other_p[...])
        ffn_backward(
            grad_fn, att, rden, qf, hat1, scale1, gprime, hat2, scale2, params_ref,
            held_out, held_up, held_down, waits, out_refs, tmp, tmp_up,
        )

    return call(
        kernel,
        (*sources, *kept, *params, *weights),
        [VMEM_SPEC] * (10 + count) + [HBM_SPEC] * 6,
        outs,
        ffn_scratch(rows),
        f"ffn_backward_{layer}",
        5,
        20,
    )


def run_ffn_grads(layer, normed, hidden, d_ffn, d_up):
    return call(
        functools.partial(ffn_weight_grads, layer),
        (normed, hidden, d_ffn, d_up),
        [VMEM_SPEC] * 4,
        [shape(4 * D, D, BF)] * 2,
        [],
        f"ffn_grads_{layer}",
        4,
    )


def run_near_backward(layer, spq, spk, vv, r_low, t_high, t_low, mask, mask_t):
    def kernel(*refs):
        near_backward(*refs[:8], refs[8:])

    return call(
        kernel,
        (spq, spk, vv, r_low, t_high, t_low, mask, mask_t),
        [VMEM_SPEC] * 8,
        [shape(spq.shape[0], D, F32)] * 3,
        [],
        f"near_backward_{layer}",
        4,
    )


def run_attention_backward(layer, x, kept, near, recvs, fixed, rest, w_own, w_other):
    rows = x.shape[0]
    count = len(recvs)

    def kernel(*refs):
        x_ref, vv, sigq, sigk, kf, r_low, t_high, t_low, prefix = refs[:9]
        near_refs = refs[9:12]
        recv_refs = refs[12 : 12 + count]
        cosb, sinb, d_pre_one, mixed, d_branch, smalls, own, other = refs[12 + count : 20 + count]
        d_in, grads_kept, grads_sent, held, d_qkv, sems = refs[20 + count :]
        (wait,) = load_weights(lax.axis_index("section"), layer, [(own, other, held, 1)], sems)
        attention_backward(
            layer, x_ref, vv, sigq, sigk, kf, r_low, t_high, t_low, prefix, near_refs, recv_refs, cosb, sinb,
            d_pre_one, mixed, d_branch, smalls, held, wait, (d_in, grads_kept, grads_sent), d_qkv,
        )

    return call(
        kernel,
        (x, *kept, *near, *recvs, *fixed, *rest, w_own, w_other),
        [VMEM_SPEC] * (18 + count) + [HBM_SPEC] * 2,
        [shape(rows, D, BF)] + [shape(2 * D + SMALL, D, BF)] * 2,
        [pltpu.VMEM((D, 3 * D), BF), pltpu.VMEM((rows, 3 * D), BF), pltpu.SemaphoreType.DMA((1,))],
        f"attention_backward_{layer}",
        5,
        20,
    )


def combine(kept, received, tail, last, name):
    rows = kept.shape[0] - (SMALL if tail else 0)
    next_rows = rows if last else rows // 2
    count = 1 if last else 2

    def kernel(kept_ref, received_ref, *outs):
        for i, out in enumerate(outs):
            s = slice(i * next_rows, (i + 1) * next_rows)
            out[:next_rows, :] = (kept_ref[s, :].astype(F32) + received_ref[s, :].astype(F32)).astype(BF)
            if tail:
                put_smalls(out, next_rows, get_smalls(kept_ref, rows) + get_smalls(received_ref, rows))

    out_rows = next_rows + (SMALL if tail else 0)
    return call(
        kernel,
        (kept, received),
        [VMEM_SPEC] * 2,
        [shape(out_rows, kept.shape[1], BF)] * count,
        [],
        name,
        1,
    )


def join(a, b, name):
    def kernel(a_ref, b_ref, out):
        out[: a.shape[0], :] = a_ref[...]
        out[a.shape[0] :, :] = b_ref[...]

    return call(kernel, (a, b), [VMEM_SPEC] * 2, [shape(a.shape[0] + b.shape[0], D, BF)], [], name, 1)[0]


def split_sums(joined, received, ffn_rows, other_rows, name):
    def kernel(joined_ref, received_ref, ffn, other, smalls):
        for out, start, rows in ((ffn, 0, ffn_rows), (other, ffn_rows, other_rows)):
            s = slice(start, start + rows)
            out[...] = (joined_ref[s, :].astype(F32) + received_ref[s, :].astype(F32)).astype(BF)
        start = ffn_rows + other_rows
        smalls[...] = get_smalls(joined_ref, start) + get_smalls(received_ref, start)

    return call(
        kernel,
        (joined, received),
        [VMEM_SPEC] * 2,
        [shape(ffn_rows, D, BF), shape(other_rows, D, BF), shape(16, D, F32)],
        [],
        name,
        1,
    )


def by_core(zero, one, name, both=True):
    rows = [block.shape[0] for block in zero]

    def kernel(*refs):
        core = lax.axis_index("section")
        outs = refs[4:]
        for out, wanted in zip(outs, (0, 1) if both else (1,)):
            for layer in range(2):

                @pl.when(core == (layer if wanted == 0 else 1 - layer))
                def _(out=out, layer=layer):
                    out[: rows[0], :] = refs[2 * layer][...]
                    out[rows[0] :, :] = refs[2 * layer + 1][...]

    count = 2 if both else 1
    return call(kernel, (*zero, *one), [VMEM_SPEC] * 4, [shape(sum(rows), D, BF)] * count, [], name, 1)


def small_gradients(zero, one):
    def kernel(zero_ref, one_ref, *outs):
        small = jnp.where(lax.axis_index("section") == 0, zero_ref[...], one_ref[...])
        for i in range(5):
            outs[i][...] = small[i : i + 1, :]
        for c in range(FF // D):
            outs[5][:, c * D : (c + 1) * D] = small[5 + c : 6 + c, :]

    return call(
        kernel, (zero, one), [VMEM_SPEC] * 2, [shape(1, D, F32)] * 5 + [shape(1, FF, F32)], [], "small_gradients", 1
    )


def unpack(blocks, second, arrays, name):
    given = []
    for block in blocks:
        if isinstance(block, list):
            given += [part for pair in block for part in pair]
        elif block is not None:
            given.append(block)
    ffn_total, other_total = 4 * D, 2 * D
    sizes = (chunk_rows(ffn_total), chunk_rows(other_total))
    count = ffn_total // sizes[0] // 2
    out_shapes = [shape(D, FF, F32), shape(FF, D, F32), shape(D, 3 * D, F32), shape(D, D, F32)]

    def kernel(*refs):
        refs = list(refs)
        sources = [refs.pop(0) for _ in given]
        if arrays is not None:
            del refs[:4]
        up, down, qkv, out, held_ffn, held_other, sem_ffn, sem_other = refs
        core = lax.axis_index("section")
        slot = 0
        waits = []
        for block_place, block in enumerate(blocks):
            if block is None:
                continue
            pairs = [sources.pop(0) for _ in range(4)] if isinstance(block, list) else None
            source = None if pairs else sources.pop(0)
            half = core if block_place == 0 else 1 - core
            for part, size, held, sems in ((0, sizes[0], held_ffn, sem_ffn), (1, sizes[1], held_other, sem_other)):
                ids = part_ids(part)
                number = jnp.where(half == 0, ids[0], ids[1])
                base = 0 if part == 0 else ffn_total // 2
                for k in range(count):
                    index = slot * count + k
                    rows = slice(k * size, (k + 1) * size)
                    if pairs is None:
                        held[index] = source[base + k * size : base + (k + 1) * size, :].astype(F32)
                    else:
                        for layer in range(2):

                            @pl.when(core == layer)
                            def _(index=index, rows=rows, held=held, part_ref=pairs[2 * layer + part]):
                                held[index] = part_ref[rows, :].astype(F32)

                    chunk = jnp.bitwise_xor(k + (count if second else 0), number)
                    row = chunk * size
                    if part == 0:
                        piece, sub = lax.div(row, D), lax.rem(row, D)

                        @pl.when(piece < 2)
                        def _(piece=piece, sub=sub, index=index, half=half, held=held, sems=sems, size=size):
                            cols = pl.ds(pl.multiple_of((2 * half + piece) * D, D), D)
                            to = up.at[pl.ds(pl.multiple_of(sub, size), size), cols]
                            pltpu.make_async_copy(held.at[index], to, sems.at[index]).start()

                        @pl.when(piece >= 2)
                        def _(piece=piece, sub=sub, index=index, half=half, held=held, sems=sems, size=size):
                            start = pl.multiple_of((2 * half + piece - 2) * D + sub, size)
                            to = down.at[pl.ds(start, size), :]
                            pltpu.make_async_copy(held.at[index], to, sems.at[index]).start()

                        waits.append((held.at[index], down.at[pl.ds(0, size), :], sems.at[index]))
                    else:
                        piece, sub = lax.div(row, D // 2), lax.rem(row, D // 2)
                        start = pl.multiple_of(half * (D // 2) + sub, size)

                        @pl.when(piece < 3)
                        def _(piece=piece, start=start, index=index, held=held, sems=sems, size=size):
                            to = qkv.at[pl.ds(start, size), pl.ds(pl.multiple_of(piece * D, D), D)]
                            pltpu.make_async_copy(held.at[index], to, sems.at[index]).start()

                        @pl.when(piece == 3)
                        def _(start=start, index=index, held=held, sems=sems, size=size):
                            to = out.at[pl.ds(start, size), :]
                            pltpu.make_async_copy(held.at[index], to, sems.at[index]).start()

                        waits.append((held.at[index], out.at[pl.ds(0, size), :], sems.at[index]))
            slot += 1
        for wait in waits:
            pltpu.make_async_copy(*wait).wait()

    total = sum(block is not None for block in blocks) * count
    return pl.pallas_call(
        kernel,
        out_shape=tuple(out_shapes),
        in_specs=[VMEM_SPEC] * len(given) + ([ANY_SPEC] * 4 if arrays is not None else []),
        out_specs=(ANY_SPEC,) * 4,
        scratch_shapes=[
            pltpu.VMEM((total, sizes[0], D), F32),
            pltpu.VMEM((total, sizes[1], D), F32),
            pltpu.SemaphoreType.DMA((total,)),
            pltpu.SemaphoreType.DMA((total,)),
        ],
        input_output_aliases={} if arrays is None else {len(given) + k: k for k in range(4)},
        compiler_params=pltpu.CompilerParams(vmem_limit_bytes=24 * MIB),
        cost_estimate=pl.CostEstimate(flops=FLOPS, bytes_accessed=1 << 10, transcendentals=0),
        name=name,
    )(*given, *(arrays or ()))


def swap_cores(block):
    return lax.ppermute(block, "section", [(0, 1), (1, 0)])


def from_chips(message):
    length = lax.axis_size("seq") // 2
    received = []
    for distance in range(1, length):
        route = [(base + j, base + (j + distance) % length) for base in (0, length) for j in range(length)]
        received.append(lax.ppermute(message, "seq", route))
    return received


def from_cores(message, received):
    return received + [swap_cores(message)] + [swap_cores(m) for m in received]


def halves_route(cores):
    length = lax.axis_size("seq") // 2
    route = []
    for j in range(length):
        route.append((2 * (j + length) + cores[0][0], 2 * j + cores[0][1]))
        route.append((2 * j + cores[1][0], 2 * (j + length) + cores[1][1]))
    return route


def pick_rows(tokens, cotangent):
    rows = tokens.shape[1]

    def kernel(*refs):
        _, lower, _, _ = place()
        sems = refs[4]
        index = jnp.where(lower, 1, 0)
        copies = [pltpu.make_async_copy(refs[k].at[index], refs[2 + k], sems.at[k]) for k in range(2)]
        for copy in copies:
            copy.start()
        for copy in copies:
            copy.wait()

    return call(
        kernel, (tokens, cotangent), [HBM_SPEC] * 2, [shape(rows, D, BF)] * 2,
        [pltpu.SemaphoreType.DMA((2,))], "pick_rows", 1, pinned=(0, 1),
    )


def own_rows(whole_ref, far_ref, s=slice(None)):
    _, lower, _, _ = place()
    return jnp.where(stays(), whole_ref[jnp.where(lower, 0, 1), s, :], far_ref[s, :])


def stays():
    core, lower, _, _ = place()
    return (core == 0) == lower


def swap_halves(block):
    return lax.ppermute(block, ("seq", "section"), halves_route(((1, 1), (0, 0))))


def place_rows(firsts, seconds, name):
    count = len(firsts)
    rows, width = firsts[0].shape
    half = count * rows

    def stack(*refs):
        _, lower, _, _ = place()
        out, hop = refs[2 * count :]
        for k in range(2 * count):
            out[k * rows : (k + 1) * rows, :] = refs[k][...]
        for k in range(count):
            hop[k * rows : (k + 1) * rows, :] = jnp.where(lower, refs[count + k][...], refs[k][...])

    both, hop = call(
        stack, (*firsts, *seconds), [VMEM_SPEC] * 2 * count, [shape(2 * half, width, BF), shape(half, width, BF)],
        [], f"stack_{name}", 1,
    )
    far = lax.ppermute(both, ("seq", "section"), halves_route(((0, 0), (1, 0))))

    def finish(far):
        def kernel(both_ref, hop_ref, far_ref, far_second_ref, *outs):
            core, lower, _, _ = place()
            for k, out in enumerate(outs):
                s = slice(k * rows, (k + 1) * rows)
                own = jnp.where(core == 0, both_ref[s, :], both_ref[half + k * rows : half + (k + 1) * rows, :])
                local = jnp.where((core == 0) == lower, own, hop_ref[s, :])
                remote = jnp.where(core == 0, far_ref[s, :], far_second_ref[s, :])
                out[0, :, :] = jnp.where(lower, local, remote)
                out[1, :, :] = jnp.where(lower, remote, local)

        far_second = lax.ppermute(far[half:], "section", [(0, 1)])
        outs = [jax.ShapeDtypeStruct((2, rows, width), BF)] * count
        placed = call(kernel, (both, swap_cores(hop), far, far_second), [VMEM_SPEC] * 4, outs, [], f"place_{name}", 1)
        return [out[None] for out in placed]

    return far, finish


def exchange(block, layer, part, step):
    routes = []
    dp, seq = lax.axis_size("dp"), lax.axis_size("seq")
    for core, order in enumerate(orders_of(part)):
        axis, i = order[step]
        for a in range(dp):
            for b in range(seq):
                to = (a ^ (1 << i), b) if axis == "dp" else (a, b ^ (1 << i))
                routes.append(((a * seq + b) * 2 + core, (to[0] * seq + to[1]) * 2 + core))
    return lax.ppermute(block, ("dp", "seq", "section"), routes)


def exchange_last(block):
    _, (axis, i) = partner_bits()
    return lax.ppermute(block, axis, [(j, j ^ (1 << i)) for j in range(lax.axis_size(axis))])


def tie(*trees):
    return lax.optimization_barrier(trees)


class PartSum:
    def __init__(self, layer, part, kept, sent):
        self.name = f"{layer}_{part}"
        self.layer, self.part = layer, part
        self.kept, self.sent = kept, sent
        self.step = -1

    def send(self):
        self.received = swap_cores(self.sent) if self.step < 0 else exchange(self.sent, self.layer, self.part, self.step)

    def add(self):
        last = self.step == len(partner_bits()[0]) - 1
        result = combine(self.kept, self.received, self.part == 1, last, f"add_{self.name}_{self.step + 1}")
        self.kept, self.sent = result[0], result[-1]
        self.step += 1


EVENTS = (
    "B0", "F1.s0", "F0.w", "C1.s0", "C0.w", "F1.s1", "ra", "C1.s1", "C1.s2", "F1.s2", "F0.s0", "C0.s0", "Z1", "C0.s1", "F0.s1", "C1.a2",
    "F1.a2", "F0.s2", "C0.s2", "C1.a1", "F1.a1", "Z0", "C1.a0", "C0.a2", "F0.a2", "F0.a1", "rs", "F1.a0", "C0.a1", "small", "pa", "pre",
    "unpack", "C0.a0", "rd", "F0.a0", "pd",
)


def default_events(steps):
    events = ["B0", "F0.w", "C0.w"]
    for layer in (1, 0):
        events += [f"{part}{layer}.s{step}" for step in range(steps) for part in ("F", "C")] + [f"Z{layer}"]
    events += ["ra", "pa", "rs", "rd", "pd"]
    for step in reversed(range(steps)):
        events += ["small", "pre", "unpack"] if step == 0 else []
        events += [f"{part}{layer}.a{step}" for layer in (1, 0) for part in ("F", "C")]
    return events


class Sums:
    def __init__(self, parts):
        self.parts = parts
        self.steps = len(partner_bits()[0])
        self.token = None
        self.joined, self.far, self.smalls = {}, {}, {}
        self.whole, self.received = {}, {}

    def after(self, received):
        if self.token is not None:
            received, self.token = tie(received, self.token)
        return received

    def of(self, layer):
        return self.whole[f"F{layer}"], self.whole[f"C{layer}"]

    def last(self, layer):
        return self.received[f"F{layer}"], self.received[f"C{layer}"]

    def gather(self, name, step):
        if step >= 0:
            self.received[name] = exchange(self.whole[name], int(name[1]), "FC".index(name[0]), step)

    def process(self, event):
        if event[0] == "Z":
            layer = int(event[1])
            pair = self.parts[f"F{layer}"], self.parts[f"C{layer}"]
            rows = pair[0].kept.shape[0], pair[1].kept.shape[0] - SMALL
            far = self.after(self.far[layer])
            ffn, other, self.smalls[layer] = split_sums(self.joined[layer], far, *rows, f"split_{layer}")
            self.token = self.smalls[layer]
            for name, block in ((f"C{layer}", other), (f"F{layer}", ffn)):
                self.whole[name] = block
                self.gather(name, self.steps - 1)
            return
        name, kind = event.split(".")
        layer = int(name[1])
        if kind[0] == "a":
            step = int(kind[1:])
            received = self.after(self.received[name])
            self.received[name] = received
            if step == 0:
                self.token = received
                return
            self.whole[name] = join(self.whole[name], received, f"join_{name}_{step}")
            self.token = self.whole[name]
            self.gather(name, step - 1)
            return
        part = self.parts[name]
        part.received = self.after(part.received)
        part.add()
        self.token = part.kept
        if part.step < self.steps:
            part.send()
        pair = [self.parts.get(f"{p}{layer}") for p in "FC"]
        if all(p is not None and p.step == self.steps for p in pair):
            self.joined[layer] = join(pair[0].kept, pair[1].kept, f"join_{layer}")
            self.far[layer] = exchange_last(self.joined[layer])


def body(tokens, cotangent, w_qkv, w_out, first_norm_gain, ln1_bias, w_up, b_up, w_down, b_down, ln2_gain, ln2_bias):
    core, _, j, length = place()
    rows = tokens.shape[1]
    whole = rows * lax.axis_size("seq")
    step = math.pi / (2.0 * whole)
    sent, sent_cot = pick_rows(tokens, cotangent)
    far, far_cot = swap_halves(sent), swap_halves(sent_cot)
    vectors = (first_norm_gain, ln1_bias, b_down, ln2_gain, ln2_bias, b_up)
    sent, w_qkv, vectors = tie(sent, w_qkv, vectors)
    qkv_w = (w_qkv[0], swap_cores(w_qkv[0]))
    own_p = jnp.concatenate([*vectors[:5], vectors[5].reshape(4, D), jnp.zeros((7, D), F32)], axis=0)
    places = jnp.arange(rows, dtype=jnp.int32)
    angles = ((j + core * length) * rows + places).astype(F32) * step
    cosb = jnp.broadcast_to(jnp.cos(angles)[:, None], (rows, 128))
    sinb = jnp.broadcast_to(jnp.sin(angles)[:, None], (rows, 128))
    apart = places[:, None] - places[None, :]
    near = jnp.cos(apart.astype(F32) * step)
    mask = jnp.where(apart >= 0, near, 0.0)
    mask_t = jnp.where(apart <= 0, near, 0.0)

    far, own_p, mask, mask_t, cosb, sinb, qkv_w = tie(far, own_p, mask, mask_t, cosb, sinb, qkv_w)

    saved = []
    x = None
    for layer in range(2):
        projected = run_project(layer, (tokens, far) if layer == 0 else (x,), *qkv_w, cosb, sinb)
        spk, sigk, kf, vv, msg, x, w_q = projected
        if layer == 0:
            msg, own_p, own_w = tie(msg, own_p, (w_out[0], w_up[0], w_down[0]))
            other_w = tuple(swap_cores(w) for w in own_w)
            rest_w = (own_w[0], other_w[0], own_w[1], other_w[1], own_w[2], other_w[2])
            params = (own_p, swap_cores(own_p))
        recvs = from_chips(msg)
        spq, sigq, qf, near_sums = run_near(layer, x, w_q, spk, vv, mask, cosb, sinb)
        recvs, near_sums, far_cot = tie(recvs, near_sums, far_cot)
        recvs = from_cores(msg, recvs)
        forward = run_forward(layer, x, near_sums, qf, recvs, params, rest_w)
        saved.append((x, (spq, spk, vv, sigq, sigk, qf, kf, None), forward))
        x = forward[-1]
    outputs = (saved[0][2][-1], saved[1][2][-1])

    def ffn_part(layer, sources):
        x, (spq, spk, vv, sigq, sigk, qf, kf, _), forward = saved[layer]
        att, rden, mixed, hat1, scale1, normed, hidden, gprime, hat2, scale2, prefix, _ = forward
        d_ffn, d_up, d_branch, d_pre_one, r_low, t_high, t_low, small, msg = run_ffn_backward(
            layer, sources, (att, rden, qf, hat1, scale1, gprime, hat2, scale2), params, rest_w
        )
        recvs = from_chips(msg)
        sums = PartSum(layer, 0, *run_ffn_grads(layer, normed, hidden, d_ffn, d_up))
        return (r_low, t_high, t_low), (d_pre_one, mixed, d_branch, small), (msg, recvs), sums

    def near_part(layer, sides):
        _, (spq, spk, vv, _, _, _, _, _), _ = saved[layer]
        return run_near_backward(layer, spq, spk, vv, *sides, mask, mask_t)

    def attention_part(layer, sides, rest, near_grads, recvs):
        x, (_, _, vv, sigq, sigk, _, kf, _), forward = saved[layer]
        grad, kept, sent = run_attention_backward(
            layer, x, (vv, sigq, sigk, kf, *sides, forward[-2]), near_grads, recvs, (cosb, sinb), rest, *qkv_w
        )
        return grad, PartSum(layer, 1, kept, sent)

    sides, rest, (msg, recvs), ffn1 = ffn_part(1, (cotangent, far_cot))
    ffn1.send()
    near_grads = near_part(1, sides)
    near_grads, recvs, ffn1.received = tie(near_grads, recvs, ffn1.received)
    recvs = from_cores(msg, recvs)
    ffn1.add()
    recvs, ffn1.kept, ffn1.sent = tie(recvs, ffn1.kept, ffn1.sent)
    d_second, other1 = attention_part(1, sides, rest, near_grads, recvs)
    ffn1.send()
    other1.send()
    sides, rest, (msg, recvs), ffn0 = ffn_part(0, (d_second,))
    near_grads = near_part(0, sides)
    near_grads, recvs, other1.received = tie(near_grads, recvs, other1.received)
    recvs = from_cores(msg, recvs)
    other1.add()
    sums = Sums({"F1": ffn1, "C1": other1, "F0": ffn0})
    sums.token = other1.kept
    for event in EVENTS if sums.steps == 3 else default_events(sums.steps):
        if event == "B0":
            d_first, sums.parts["C0"] = attention_part(0, sides, rest, sums.after(near_grads), recvs)
            other0 = sums.parts["C0"]
            d_first, other0.sent, ffn0.sent, other1.sent, ffn1.received = tie(
                d_first, other0.sent, ffn0.sent, other1.sent, ffn1.received
            )
            sums.token = d_first
            ffn0.send()
            other1.send()
            other0.send()
            outputs_far, outputs_finish = place_rows((outputs[0],), (outputs[1],), "outputs")
        elif event == "ra":
            outputs_far = sums.after(outputs_far)
            sums.token = outputs_far
        elif event == "pa":
            (layer_outputs,) = outputs_finish(sums.after(outputs_far))
            sums.token = layer_outputs
        elif event == "rs":
            d_first = sums.after(d_first)
            inputs_far, inputs_finish = place_rows((d_first,), (d_second,), "inputs")
        elif event == "rd":
            inputs_far = sums.after(inputs_far)
            sums.token = inputs_far
        elif event == "pd":
            (input_grads,) = inputs_finish(sums.after(inputs_far))
            sums.token = input_grads
        elif event == "pre":
            mine, theirs = by_core(sums.of(0), sums.of(1), "by_core_0")
            hop = swap_cores(theirs)
        elif event == "small":
            small = small_gradients(sums.smalls[0], sums.after(sums.smalls[1]))
            sums.token = small[0]
        elif event == "unpack":
            arrays = unpack((mine, sums.after(hop)), False, None, "unpack_0")
            sums.token = arrays[3]
        else:
            sums.process(event)
    d_gain1, d_bias1, d_b_down, d_gain2, d_bias2, d_b_up = small
    zero, one = sums.last(0), sums.last(1)
    (theirs,) = by_core(zero, one, "by_core_1", False)
    arrays = unpack(([zero, one], None), True, arrays, "unpack_1")
    grad_up, grad_down, grad_qkv, grad_out = unpack((None, swap_cores(theirs)), True, arrays, "unpack_2")
    return (
        layer_outputs,
        input_grads,
        grad_qkv[None],
        grad_out[None],
        d_gain1,
        d_bias1,
        grad_up[None],
        d_b_up,
        grad_down[None],
        d_b_down,
        d_gain2,
        d_bias2,
    )


def solution(mesh):
    rows = P("dp", "seq", None)
    matrix = P("section", None, None)
    vector = P("section", None)
    out_rows = P("section", "dp", "seq", None)
    return jax.shard_map(
        body,
        mesh=mesh,
        in_specs=(rows, rows, matrix, matrix, vector, vector, matrix, vector, matrix, vector, vector, vector),
        out_specs=(
            out_rows, out_rows, matrix, matrix, vector, vector, matrix, vector, matrix, vector, vector, vector,
        ),
        check_vma=False,
    )
```
